32 devices in a mesh: dp: 4 (over y, core), heads: 8 (over z, x).
Axes of the slice: x: 2, y: 2, z: 4, core: 2. Of those that a mesh axis runs over, the one named last changes fastest.
Arguments:
- block_input: float32 [4096, 2048], P(('dp', 'heads')), may hold values from -6 to 6
- output_grad: float32 [4096, 2048], P(('dp', 'heads'))
- lengths: int32 [4, 6], P('dp'), may hold values from 1 to 896, 1024 in all within a row
- norm_gains: float32 [5120], replicated, may hold values from 0.48 to 2.25
- norm_gains_first: float32 [5120], replicated
- norm_gains_second: float32 [5120], replicated, may hold values from 4096 to 16384
- query_down: float32 [2048, 1024], P('dp')
- query_down_first: float32 [2048, 1024], P('dp')
- query_down_second: float32 [2048, 1024], P('dp'), may hold values from 2621.44 to 10485.76
- key_value: float32 [2048, 512], P('dp')
- key_value_first: float32 [2048, 512], P('dp')
- key_value_second: float32 [2048, 512], P('dp'), may hold values from 16384 to 65536
- query_up: float32 [1024, 4096], P('dp', 'heads')
- query_up_first: float32 [1024, 4096], P('dp', 'heads')
- query_up_second: float32 [1024, 4096], P('dp', 'heads'), may hold values from 1024 to 4096
- head_merge: float32 [4096, 2048], P('heads', 'dp')
- head_merge_first: float32 [4096, 2048], P('heads', 'dp')
- head_merge_second: float32 [4096, 2048], P('heads', 'dp'), may hold values from 368.64 to 1474.56
- gate_weight: float32 [2048, 5632], P('dp', 'heads')
- gate_weight_first: float32 [2048, 5632], P('dp', 'heads')
- gate_weight_second: float32 [2048, 5632], P('dp', 'heads'), may hold values from 2621.44 to 10485.76
- up_weight: float32 [2048, 5632], P('dp', 'heads')
- up_weight_first: float32 [2048, 5632], P('dp', 'heads')
- up_weight_second: float32 [2048, 5632], P('dp', 'heads'), may hold values from 2621.44 to 10485.76
- down_weight: float32 [5632, 2048], P('heads', 'dp')
- down_weight_first: float32 [5632, 2048], P('heads', 'dp')
- down_weight_second: float32 [5632, 2048], P('heads', 'dp'), may hold values from 4096 to 16384
Outputs:
- block_output: float32 [4096, 2048], P(('dp', 'heads'))
- input_grad: float32 [4096, 2048], P(('dp', 'heads'))
- norm_gains_first_new: float32 [5120], replicated
- norm_gains_second_new: float32 [5120], replicated
- norm_gains_new: float32 [5120], replicated
- query_down_first_new: float32 [2048, 1024], P('dp')
- query_down_second_new: float32 [2048, 1024], P('dp')
- query_down_new: float32 [2048, 1024], P('dp')
- key_value_first_new: float32 [2048, 512], P('dp')
- key_value_second_new: float32 [2048, 512], P('dp')
- key_value_new: float32 [2048, 512], P('dp')
- query_up_first_new: float32 [1024, 4096], P('dp', 'heads')
- query_up_second_new: float32 [1024, 4096], P('dp', 'heads')
- query_up_new: float32 [1024, 4096], P('dp', 'heads')
- head_merge_first_new: float32 [4096, 2048], P('heads', 'dp')
- head_merge_second_new: float32 [4096, 2048], P('heads', 'dp')
- head_merge_new: float32 [4096, 2048], P('heads', 'dp')
- gate_weight_first_new: float32 [2048, 5632], P('dp', 'heads')
- gate_weight_second_new: float32 [2048, 5632], P('dp', 'heads')
- gate_weight_new: float32 [2048, 5632], P('dp', 'heads')
- up_weight_first_new: float32 [2048, 5632], P('dp', 'heads')
- up_weight_second_new: float32 [2048, 5632], P('dp', 'heads')
- up_weight_new: float32 [2048, 5632], P('dp', 'heads')
- down_weight_first_new: float32 [5632, 2048], P('heads', 'dp')
- down_weight_second_new: float32 [5632, 2048], P('heads', 'dp')
- down_weight_new: float32 [5632, 2048], P('heads', 'dp')
- norms: float32 [8, 2], replicated
The draws below stay inside these ranges and needn't reach their ends.
All inputs are finite; a program needn't handle non-finite values.
Results may differ from the reference program's by a relative error of at most 0.0003.
Values sent between devices are 32-bit elements; how exact they have to be, the bound alone decides.
A program may use at most 256 MiB of HBM per device.

```python
import math
import jax
import jax.numpy as jnp
import numpy as np
from jax import lax

D = 2048
QL = 1024
HEADS = 16
HD = 256
FF = 5632
NSEQ = 6
STEP_COUNT = 10
TOKENS = 4096
GROUP = 1024
LONGEST = 896
N_DP = 4


def rising(count):
    return 0.6 * 3.0 ** (jnp.arange(count, dtype=jnp.float32) / max(count - 1, 1))


def profile(array_shape, along):
    scaled = jnp.ones(array_shape, jnp.float32)
    for axis_dim in along:
        view = [1] * len(array_shape)
        view[axis_dim] = array_shape[axis_dim]
        scaled = scaled * rising(array_shape[axis_dim]).reshape(view)
    return scaled


def matrix(key, array_shape, fan_in, along):
    return jax.random.normal(key, array_shape, jnp.float32) * fan_in ** (-0.5) * profile(array_shape, along)


def first_moment(key, array_shape, factor, along):
    return jax.random.normal(key, array_shape, jnp.float32) * (factor * math.sqrt(TOKENS)) * profile(array_shape, along)


def second_moment(key, array_shape, factor):
    return jax.random.uniform(key, array_shape, jnp.float32, 1.0, 4.0) * (factor * factor * TOKENS)


def draw_output_grad(key, part):
    return jax.random.normal(jax.random.fold_in(key, 101), (TOKENS, D), jnp.float32) * rising(D)[None, :]


def draw_norm_gains(key, part):
    ramp = jnp.concatenate([rising(D), rising(QL), rising(D)])
    return ramp * jax.random.uniform(jax.random.fold_in(key, 102), (2 * D + QL,), jnp.float32, 0.8, 1.25)


def draw_norm_gains_first(key, part):
    return first_moment(jax.random.fold_in(key, 103), (2 * D + QL,), 1.0, [0])


def draw_norm_gains_second(key, part):
    return second_moment(jax.random.fold_in(key, 104), (2 * D + QL,), 1.0)


def draw_query_down(key, part):
    return matrix(jax.random.fold_in(key, 105), (D, QL), D, [0])


def draw_query_down_first(key, part):
    return first_moment(jax.random.fold_in(key, 106), (D, QL), 0.8, [0])


def draw_query_down_second(key, part):
    return second_moment(jax.random.fold_in(key, 107), (D, QL), 0.8)


def draw_key_value(key, part):
    return matrix(jax.random.fold_in(key, 108), (D, 2 * HD), D, [0])


def draw_key_value_first(key, part):
    return first_moment(jax.random.fold_in(key, 109), (D, 2 * HD), 2.0, [0])


def draw_key_value_second(key, part):
    return second_moment(jax.random.fold_in(key, 110), (D, 2 * HD), 2.0)


def draw_query_up(key, part):
    return matrix(jax.random.fold_in(key, 111), (QL, HEADS * HD), QL, [0, 1])


def draw_query_up_first(key, part):
    return first_moment(jax.random.fold_in(key, 112), (QL, HEADS * HD), 0.5, [0, 1])


def draw_query_up_second(key, part):
    return second_moment(jax.random.fold_in(key, 113), (QL, HEADS * HD), 0.5)


def draw_head_merge(key, part):
    return matrix(jax.random.fold_in(key, 114), (HEADS * HD, D), HEADS * HD // 16, [0, 1])


def draw_head_merge_first(key, part):
    return first_moment(jax.random.fold_in(key, 115), (HEADS * HD, D), 0.3, [0, 1])


def draw_head_merge_second(key, part):
    return second_moment(jax.random.fold_in(key, 116), (HEADS * HD, D), 0.3)


def draw_gate_weight(key, part):
    return matrix(jax.random.fold_in(key, 117), (D, FF), D, [0, 1])


def draw_gate_weight_first(key, part):
    return first_moment(jax.random.fold_in(key, 118), (D, FF), 0.8, [0, 1])


def draw_gate_weight_second(key, part):
    return second_moment(jax.random.fold_in(key, 119), (D, FF), 0.8)


def draw_up_weight(key, part):
    return matrix(jax.random.fold_in(key, 120), (D, FF), D, [0, 1])


def draw_up_weight_first(key, part):
    return first_moment(jax.random.fold_in(key, 121), (D, FF), 0.8, [0, 1])


def draw_up_weight_second(key, part):
    return second_moment(jax.random.fold_in(key, 122), (D, FF), 0.8)


def draw_down_weight(key, part):
    return matrix(jax.random.fold_in(key, 123), (FF, D), FF, [0, 1])


def draw_down_weight_first(key, part):
    return first_moment(jax.random.fold_in(key, 124), (FF, D), 1.0, [0, 1])


def draw_down_weight_second(key, part):
    return second_moment(jax.random.fold_in(key, 125), (FF, D), 1.0)


def shard_levels(rng, extent, cuts, low, top_value):
    level, own = 1.0, jax.random.fold_in(rng, 6)
    for axis_at, parts in cuts:
        heights = jnp.exp(jax.random.uniform(jax.random.fold_in(own, axis_at), (parts,), jnp.float32, low / len(cuts), top_value / len(cuts)))
        level = level * jnp.repeat(heights, extent[axis_at] // parts).reshape([-1 if axis == axis_at else 1 for axis in range(len(extent))])
    return level


def length_profile(amount, total, reach, lean):
    weights = [(1 << 20) // math.isqrt(grade ** lean) + 1 for grade in range(2, amount + 1)]
    surplus, counts = total - reach - (amount - 1), [1] * (amount - 1)
    while surplus > 0:
        candidates = [i for i in range(amount - 1) if counts[i] < reach]
        pool, left = sum([weights[i] for i in candidates]), surplus
        for i in candidates:
            extra = min(reach - counts[i], max(1, left * weights[i] // pool), surplus)
            counts[i] = counts[i] + extra
            surplus = surplus - extra
    return np.array([reach] + counts)


def ragged(stream_key, count, total, limit, slope):
    if count == 2:
        one = jax.random.randint(stream_key, (), max(1, total - limit), min(limit, total - 1) + 1)
        return jnp.stack([one, total - one])
    tallies = jnp.asarray(length_profile(count, total, limit, slope), jnp.int32)
    couples = (count - 1) // 2
    giver, sink = tallies[1:1 + 2 * couples:2], tallies[2:2 + 2 * couples:2]
    room = jnp.minimum(giver - 1, limit - sink)
    moved = jax.random.randint(jax.random.fold_in(stream_key, 1), (couples,), 0, 1 << 20) % (room + 1)
    tallies = tallies.at[1:1 + 2 * couples:2].set(giver - moved).at[2:2 + 2 * couples:2].set(sink + moved)
    return tallies[jax.random.permutation(jax.random.fold_in(stream_key, 2), count)]


def scatter_about(own_key, shape, deviation, bound, pieces=(), kind=jnp.bfloat16):
    entries = jax.random.normal(own_key, shape, jnp.float32) * deviation
    if len(pieces) > 0:
        entries = shard_levels(own_key, shape, pieces, -0.22, 0.18) * entries
    return jnp.clip(entries, min=-bound, max=bound).astype(kind)


def setup_inputs(seed: int = 0) -> dict:
    splits = jax.random.split(jax.random.key(seed), 28)
    block_input = scatter_about(splits[0], (TOKENS, D), 1.0, 6.0, ((0, 32),), jnp.float32)
    output_grad = draw_output_grad(jax.random.fold_in(splits[27], 71), 0)
    lengths = jax.vmap(lambda own: ragged(own, NSEQ, GROUP, LONGEST, 2))(jax.random.split(splits[2], N_DP)).reshape((N_DP, NSEQ)).astype(jnp.int32)
    norm_gains = draw_norm_gains(jax.random.fold_in(splits[27], 71), 0)
    norm_gains_first = draw_norm_gains_first(jax.random.fold_in(splits[27], 71), 0)
    norm_gains_second = draw_norm_gains_second(jax.random.fold_in(splits[27], 71), 0)
    query_down = draw_query_down(jax.random.fold_in(splits[27], 71), 0)
    query_down_first = draw_query_down_first(jax.random.fold_in(splits[27], 71), 0)
    query_down_second = draw_query_down_second(jax.random.fold_in(splits[27], 71), 0)
    key_value = draw_key_value(jax.random.fold_in(splits[27], 71), 0)
    key_value_first = draw_key_value_first(jax.random.fold_in(splits[27], 71), 0)
    key_value_second = draw_key_value_second(jax.random.fold_in(splits[27], 71), 0)
    query_up = draw_query_up(jax.random.fold_in(splits[27], 71), 0)
    query_up_first = draw_query_up_first(jax.random.fold_in(splits[27], 71), 0)
    query_up_second = draw_query_up_second(jax.random.fold_in(splits[27], 71), 0)
    head_merge = draw_head_merge(jax.random.fold_in(splits[27], 71), 0)
    head_merge_first = draw_head_merge_first(jax.random.fold_in(splits[27], 71), 0)
    head_merge_second = draw_head_merge_second(jax.random.fold_in(splits[27], 71), 0)
    gate_weight = draw_gate_weight(jax.random.fold_in(splits[27], 71), 0)
    gate_weight_first = draw_gate_weight_first(jax.random.fold_in(splits[27], 71), 0)
    gate_weight_second = draw_gate_weight_second(jax.random.fold_in(splits[27], 71), 0)
    up_weight = draw_up_weight(jax.random.fold_in(splits[27], 71), 0)
    up_weight_first = draw_up_weight_first(jax.random.fold_in(splits[27], 71), 0)
    up_weight_second = draw_up_weight_second(jax.random.fold_in(splits[27], 71), 0)
    down_weight = draw_down_weight(jax.random.fold_in(splits[27], 71), 0)
    down_weight_first = draw_down_weight_first(jax.random.fold_in(splits[27], 71), 0)
    down_weight_second = draw_down_weight_second(jax.random.fold_in(splits[27], 71), 0)
    return dict(block_input=block_input, output_grad=output_grad, lengths=lengths, norm_gains=norm_gains, norm_gains_first=norm_gains_first, norm_gains_second=norm_gains_second, query_down=query_down, query_down_first=query_down_first, query_down_second=query_down_second, key_value=key_value, key_value_first=key_value_first, key_value_second=key_value_second, query_up=query_up, query_up_first=query_up_first, query_up_second=query_up_second, head_merge=head_merge, head_merge_first=head_merge_first, head_merge_second=head_merge_second, gate_weight=gate_weight, gate_weight_first=gate_weight_first, gate_weight_second=gate_weight_second, up_weight=up_weight, up_weight_first=up_weight_first, up_weight_second=up_weight_second, down_weight=down_weight, down_weight_first=down_weight_first, down_weight_second=down_weight_second)


@jax.custom_vjp
def low(v):
    return lax.optimization_barrier(v.astype(jnp.bfloat16)).astype(jnp.float32)

@jax.custom_vjp
def low_back(v):
    return v

def low_keep(v):
    return (low(v), None)

def low_pass(kept, grad):
    return (grad,)

def back_keep(v):
    return (v, None)

def back_low(kept, grad):
    return (low(grad),)
low.defvjp(low_keep, low_pass)
low_back.defvjp(back_keep, back_low)
EPS_NORM = 1e-06
ROPE_BASE = 10000.0
BETA_ONE = 0.5
BETA_TWO = 0.6
ADAM_EPS = 1e-06
DECAY = 0.01
RATE = 0.5
HIGH = lax.Precision.HIGHEST

def matmul_high(left, right):
    return jnp.dot(left, right, precision=HIGH, preferred_element_type=jnp.float32)

def rms_norm(vector, gain):
    return vector * lax.rsqrt(lax.optimization_barrier(jnp.mean(vector * vector, axis=-1, keepdims=True)) + EPS_NORM) * gain

def layout(lengths_row, row_index):
    doc_ends = jnp.cumsum(lengths_row).astype(jnp.int32)
    doc_starts = (doc_ends - lengths_row).astype(jnp.int32)
    segment = lax.optimization_barrier(jnp.sum((row_index[:, None] >= doc_ends[None, :]).astype(jnp.int32), axis=1)).astype(jnp.int32)
    doc_ids = jnp.arange(doc_ends.shape[0], dtype=jnp.int32)
    start_of = lax.optimization_barrier(jnp.sum(jnp.where(segment[:, None] == doc_ids[None, :], doc_starts[None, :], 0), axis=1)).astype(jnp.int32)
    return (segment, (row_index - start_of).astype(jnp.int32))

def rotate(vector, position, sign):
    half_dim = vector.shape[-1] // 2
    frequency = ROPE_BASE ** (-jnp.arange(half_dim, dtype=jnp.float32) / half_dim)
    angles = position.astype(jnp.float32)[:, None] * frequency[None, :]
    angles = angles.reshape((angles.shape[0],) + (1,) * (vector.ndim - 2) + (half_dim,))
    cosine = jnp.cos(angles)
    sines = sign * jnp.sin(angles)
    front = vector[..., :half_dim]
    back_half = vector[..., half_dim:]
    return jnp.concatenate([front * cosine - back_half * sines, back_half * cosine + front * sines], axis=-1)

def attend(queries, key_rows, value_rows, segment):
    group_rows = queries.shape[0]
    block_rows = min(512, group_rows)
    n_blocks = group_rows // block_rows
    row_index = jnp.arange(group_rows, dtype=jnp.int32)

    @jax.checkpoint
    def one_block(inputs):
        query_block, row_block, seg_block = inputs
        scores = jnp.einsum('qhd,kd->hqk', query_block, key_rows, precision=HIGH) * HD ** (-0.5)
        allowed = (seg_block[:, None] == segment[None, :]) & (row_index[None, :] <= row_block[:, None])
        scores = jnp.where(allowed[None], scores, -1e+30)
        row_max = lax.optimization_barrier(jnp.max(scores, axis=2, keepdims=True))
        expo = jnp.exp(scores - row_max)
        probs = expo / lax.optimization_barrier(jnp.sum(expo, axis=2, keepdims=True))
        return jnp.einsum('hqk,kd->qhd', probs, value_rows, precision=HIGH)
    mixed = lax.map(one_block, (queries.reshape(n_blocks, block_rows, HEADS, HD), row_index.reshape(n_blocks, block_rows), segment.reshape(n_blocks, block_rows)))
    return mixed.reshape(group_rows, HEADS * HD)

@jax.checkpoint
def group_forward(inputs, lengths_row, norm_gains, query_down, key_value, query_up, head_merge, gate_weight, up_weight, down_weight):
    group_rows = inputs.shape[0]
    segment, position = layout(lengths_row, jnp.arange(group_rows, dtype=jnp.int32))
    gain_attn = norm_gains[:D]
    gain_query = norm_gains[D:D + QL]
    gain_ffn = norm_gains[D + QL:]
    normed_one = rms_norm(inputs, gain_attn)
    latent = rms_norm(matmul_high(normed_one, query_down), gain_query)
    pair = matmul_high(normed_one, key_value)
    key_rows = rotate(pair[:, :HD], position, 1.0)
    value_rows = pair[:, HD:]
    queries = rotate(matmul_high(latent, query_up).reshape(group_rows, HEADS, HD), position, 1.0)
    mixed = attend(queries, key_rows, value_rows, segment)
    middle = inputs + matmul_high(mixed, head_merge)
    normed_two = rms_norm(middle, gain_ffn)
    gate_pre = matmul_high(normed_two, gate_weight)
    up_pre = matmul_high(normed_two, up_weight)
    return middle + matmul_high(jax.nn.silu(gate_pre) * up_pre, down_weight)

def lamb_step(value, grad, first, second):
    first_new = BETA_ONE * first + (1.0 - BETA_ONE) * grad
    second_new = BETA_TWO * second + (1.0 - BETA_TWO) * grad * grad
    update = first_new / (1.0 - BETA_ONE ** STEP_COUNT) / (jnp.sqrt(second_new / (1.0 - BETA_TWO ** STEP_COUNT)) + ADAM_EPS) + DECAY * value
    weight_norm = jnp.sqrt(jnp.sum(value * value))
    update_norm = jnp.sqrt(jnp.sum(update * update))
    new_value = value - RATE * (weight_norm / update_norm) * update
    return (first_new, second_new, new_value, jnp.stack([weight_norm, update_norm]))

def reference(block_input, output_grad, lengths, norm_gains, norm_gains_first, norm_gains_second, query_down, query_down_first, query_down_second, key_value, key_value_first, key_value_second, query_up, query_up_first, query_up_second, head_merge, head_merge_first, head_merge_second, gate_weight, gate_weight_first, gate_weight_second, up_weight, up_weight_first, up_weight_second, down_weight, down_weight_first, down_weight_second):
    params = (norm_gains, query_down, key_value, query_up, head_merge, gate_weight, up_weight, down_weight)
    firsts = (norm_gains_first, query_down_first, key_value_first, query_up_first, head_merge_first, gate_weight_first, up_weight_first, down_weight_first)
    seconds = (norm_gains_second, query_down_second, key_value_second, query_up_second, head_merge_second, gate_weight_second, up_weight_second, down_weight_second)

    def forward(inputs, *weights):
        grouped = inputs.reshape(N_DP, GROUP, D)
        outputs = lax.map(lambda entry_pair: group_forward(entry_pair[0], entry_pair[1], *weights), (grouped, lengths))
        return outputs.reshape(TOKENS, D)
    block_output, pullback = jax.vjp(forward, block_input, *params)
    grads = pullback(output_grad)
    input_grad = grads[0]
    updated = [lamb_step(params[slot], grads[slot + 1], firsts[slot], seconds[slot]) for slot in range(8)]
    norms = jnp.stack([updated[slot][3] for slot in range(8)])
    return (block_output, input_grad, updated[0][0], updated[0][1], updated[0][2], updated[1][0], updated[1][1], updated[1][2], updated[2][0], updated[2][1], updated[2][2], updated[3][0], updated[3][1], updated[3][2], updated[4][0], updated[4][1], updated[4][2], updated[5][0], updated[5][1], updated[5][2], updated[6][0], updated[6][1], updated[6][2], updated[7][0], updated[7][1], updated[7][2], norms)
```

```python
import functools

import jax
import jax.numpy as jnp
from jax import lax
from jax.experimental import pallas as pl
from jax.experimental.pallas import tpu as pltpu
from jax.sharding import PartitionSpec as P

STEP_COUNT = 10


EPS_NORM = 1e-06
ROPE_BASE = 10000.0
BETA_ONE = 0.5
BETA_TWO = 0.6
ADAM_EPS = 1e-06
DECAY = 0.01
RATE = 0.5
HIGH = lax.Precision.HIGH
MESH = pl.DeviceIdType.MESH
RING_Z = 4


def head_at(spot, n):
    wide = n // RING_Z
    back = (spot + n - RING_Z) // n
    rest = jnp.maximum(spot - RING_Z, 0)
    row, step = rest // (wide - 1), rest % (wide - 1)
    odd = row % 2
    column = (1 - odd) * (1 + step) + odd * (wide - 1 - step)
    return (1 - back) * (spot * wide) + back * ((RING_Z - 1 - row) * wide + column)


def spot_of(head, n):
    wide = n // RING_Z
    row = RING_Z - 1 - head // wide
    column = head % wide
    odd = row % 2
    step = (1 - odd) * (column - 1) + odd * (wide - 1 - column)
    back = (column + wide - 1) // wide
    return (1 - back) * (head // wide) + back * (RING_Z + row * (wide - 1) + step)


def ring_places(n):
    me = lax.axis_index("heads")
    spot = spot_of(me, n)
    return me, lambda k: head_at(lax.rem(spot + k + 2 * n, n), n)


def greet(right, left):
    bar = pltpu.get_barrier_semaphore()
    for other in (right, left):
        pl.semaphore_signal(bar, inc=1, device_id={"heads": other}, device_id_type=MESH)
    pl.semaphore_wait(bar, 2)


def push(src, dst, send, recv, other):
    copy = pltpu.make_async_remote_copy(
        src_ref=src, dst_ref=dst, send_sem=send, recv_sem=recv, device_id={"heads": other}, device_id_type=MESH
    )
    copy.start()
    return copy


def gather_body(n, cuts, x_ref, o_ref, own_sem, send_sem, recv_sem):
    me, at = ring_places(n)
    sides = (at(1), at(-1))
    greet(*sides)
    rows = x_ref.shape[0]
    half = rows // 2
    piece = half // cuts
    own = pltpu.make_async_copy(x_ref, o_ref.at[pl.ds(me * rows, rows)], own_sem)
    own.start()
    copies = {}
    for step in range(n - 1):
        for cut in range(cuts):
            for way in (0, 1):
                if step > 0:
                    copies[way, step - 1, cut].wait_recv()
                off = way * half + cut * piece
                origin = at(-step) if way == 0 else at(step)
                dst = o_ref.at[pl.ds(origin * rows + off, piece)]
                src = x_ref.at[pl.ds(off, piece)] if step == 0 else dst
                copies[way, step, cut] = push(
                    src, dst, send_sem.at[way, step, cut], recv_sem.at[way, step, cut], sides[way]
                )
    for cut in range(cuts):
        for way in (0, 1):
            copies[way, n - 2, cut].wait_recv()
    for copy in copies.values():
        copy.wait_send()
    own.wait()


def cost(micros):
    return pl.CostEstimate(flops=0, bytes_accessed=int(micros * 3.0e6), transcendentals=0)


def ring_gather(x, n, number, cuts=2):
    rows, columns = x.shape
    cuts = min(cuts, rows // 16)
    return pl.pallas_call(
        functools.partial(gather_body, n, cuts),
        out_shape=jax.ShapeDtypeStruct((n * rows, columns), x.dtype),
        in_specs=[pl.BlockSpec(memory_space=pl.ANY)],
        out_specs=pl.BlockSpec(memory_space=pl.ANY),
        scratch_shapes=[
            pltpu.SemaphoreType.DMA,
            pltpu.SemaphoreType.DMA((2, n - 1, cuts)),
            pltpu.SemaphoreType.DMA((2, n - 1, cuts)),
        ],
        compiler_params=pltpu.CompilerParams(collective_id=number, has_side_effects=True),
        cost_estimate=cost(75.0 * columns / 2048),
        name=f"ring_gather_{number}",
    )(x)


def scatter_body(n, cuts, x_ref, o_ref, held, send_sem, recv_sem):
    me, at = ring_places(n)
    sides = (at(1), at(-1))
    greet(*sides)
    rows = o_ref.shape[0]
    half = rows // 2
    piece = half // cuts
    copies = {}
    for step in range(n - 1):
        for cut in range(cuts):
            for way in (0, 1):
                owner = at(-1 - step) if way == 0 else at(1 + step)
                part = x_ref.at[pl.ds(pl.multiple_of(owner * rows + way * half + cut * piece, piece), piece)]
                here = pl.ds(cut * piece, piece)
                src = part
                if step > 0:
                    copies[way, step - 1, cut].wait_recv()
                    src = held.at[way, step - 1, here]
                    src[...] += part[...]
                copies[way, step, cut] = push(
                    src,
                    held.at[way, step, here],
                    send_sem.at[way, step, cut],
                    recv_sem.at[way, step, cut],
                    sides[way],
                )
    for cut in range(cuts):
        for way in (0, 1):
            copies[way, n - 2, cut].wait_recv()
            off = way * half + cut * piece
            o_ref[pl.ds(off, piece)] = (
                x_ref[pl.ds(pl.multiple_of(me * rows + off, piece), piece)]
                + held[way, n - 2, pl.ds(cut * piece, piece)]
            )
    for copy in copies.values():
        copy.wait_send()


def ring_scatter(x, n, number, cuts=4):
    rows, columns = x.shape[0] // n, x.shape[1]
    cuts = min(cuts, rows // 16)
    return pl.pallas_call(
        functools.partial(scatter_body, n, cuts),
        out_shape=jax.ShapeDtypeStruct((rows, columns), x.dtype),
        in_specs=[pl.BlockSpec(memory_space=pltpu.VMEM)],
        out_specs=pl.BlockSpec(memory_space=pltpu.VMEM),
        scratch_shapes=[
            pltpu.VMEM((2, n - 1, rows // 2, columns), x.dtype),
            pltpu.SemaphoreType.DMA((2, n - 1, cuts)),
            pltpu.SemaphoreType.DMA((2, n - 1, cuts)),
        ],
        compiler_params=pltpu.CompilerParams(
            collective_id=number, has_side_effects=True, vmem_limit_bytes=40 << 20
        ),
        cost_estimate=cost(75.0 * columns / 2048),
        name=f"ring_scatter_{number}",
    )(x)


def matmul_high(left, right):
    return jnp.dot(left, right, precision=HIGH, preferred_element_type=jnp.float32)


def layout(lengths_row, row_index):
    upto = jnp.arange(lengths_row.shape[0], dtype=jnp.int32)
    doc_ends = jnp.sum(jnp.where(upto[None, :] <= upto[:, None], lengths_row[None, :], 0), axis=1)
    doc_starts = doc_ends - lengths_row
    segment = jnp.sum((row_index[:, None] >= doc_ends[None, :]).astype(jnp.int32), axis=1)
    doc_ids = jnp.arange(doc_ends.shape[0], dtype=jnp.int32)
    start_of = jnp.sum(
        jnp.where(segment[:, None] == doc_ids[None, :], doc_starts[None, :], 0), axis=1
    )
    return (segment, row_index - start_of)


def rotate(vector, position, sign):
    half_dim = vector.shape[-1] // 2
    frequency = ROPE_BASE ** (-jnp.arange(half_dim, dtype=jnp.float32) / half_dim)
    angles = position.astype(jnp.float32)[:, None] * frequency[None, :]
    angles = angles.reshape((angles.shape[0],) + (1,) * (vector.ndim - 2) + (half_dim,))
    cosine = jnp.cos(angles)
    sines = sign * jnp.sin(angles)
    front = vector[..., :half_dim]
    back_half = vector[..., half_dim:]
    return jnp.concatenate(
        [front * cosine - back_half * sines, back_half * cosine + front * sines], axis=-1
    )


def norm_back(upstream, normed, inverse, gain):
    scaled = upstream * gain
    return (
        inverse * (scaled - normed * jnp.mean(scaled * normed, axis=1, keepdims=True)),
        jnp.sum(upstream * normed, axis=0),
    )


def spread_grads(part_down, part_pair, part_up, part_merge, part_gate, part_upper, part_lower):
    return (
        lax.psum_scatter(part_down, "dp", scatter_dimension=0, tiled=True),
        lax.psum_scatter(part_pair, "dp", scatter_dimension=0, tiled=True),
        lax.psum_scatter(part_up, "dp", scatter_dimension=0, tiled=True),
        lax.psum_scatter(part_merge, "dp", scatter_dimension=1, tiled=True),
        lax.psum_scatter(part_gate, "dp", scatter_dimension=0, tiled=True),
        lax.psum_scatter(part_upper, "dp", scatter_dimension=0, tiled=True),
        lax.psum_scatter(part_lower, "dp", scatter_dimension=1, tiled=True),
    )


def moments(value, grad, first, second):
    first_new = BETA_ONE * first + (1.0 - BETA_ONE) * grad
    second_new = BETA_TWO * second + (1.0 - BETA_TWO) * grad * grad
    update = (
        first_new
        / (1.0 - BETA_ONE**STEP_COUNT)
        / (jnp.sqrt(second_new / (1.0 - BETA_TWO**STEP_COUNT)) + ADAM_EPS)
        + DECAY * value
    )
    return (first_new, second_new, update)


def on_device(
    block_input,
    output_grad,
    lengths,
    norm_gains,
    norm_gains_first,
    norm_gains_second,
    query_down,
    query_down_first,
    query_down_second,
    key_value,
    key_value_first,
    key_value_second,
    query_up,
    query_up_first,
    query_up_second,
    head_merge,
    head_merge_first,
    head_merge_second,
    gate_weight,
    gate_weight_first,
    gate_weight_second,
    up_weight,
    up_weight_first,
    up_weight_second,
    down_weight,
    down_weight_first,
    down_weight_second,
):
    tok_rows = block_input.shape[0]
    model_dim = block_input.shape[1]
    latent_dim = query_down.shape[1]
    head_dim = key_value.shape[1] // 2
    local_heads = query_up.shape[1] // head_dim
    heads_count = lax.axis_size("heads")
    group_rows = tok_rows * heads_count
    scale = head_dim ** (-0.5)
    wide_down, wide_pair, wide_up, wide_merge, wide_gate, wide_upper, wide_lower = (
        lax.all_gather(query_down, "dp", axis=0, tiled=True),
        lax.all_gather(key_value, "dp", axis=0, tiled=True),
        lax.all_gather(query_up, "dp", axis=0, tiled=True),
        lax.all_gather(head_merge, "dp", axis=1, tiled=True),
        lax.all_gather(gate_weight, "dp", axis=0, tiled=True),
        lax.all_gather(up_weight, "dp", axis=0, tiled=True),
        lax.all_gather(down_weight, "dp", axis=1, tiled=True),
    )
    grad_all = ring_gather(output_grad, heads_count, 5)
    group_index = jnp.arange(group_rows, dtype=jnp.int32)
    segment, position = layout(lengths[0], group_index)
    local_position = lax.dynamic_slice_in_dim(
        position, lax.axis_index("heads") * tok_rows, tok_rows
    )
    gain_attn = norm_gains[:model_dim]
    gain_query = norm_gains[model_dim : model_dim + latent_dim]
    gain_ffn = norm_gains[model_dim + latent_dim :]
    inv_one = lax.rsqrt(jnp.mean(block_input * block_input, axis=1, keepdims=True) + EPS_NORM)
    normed_one = block_input * inv_one
    hidden_one = normed_one * gain_attn
    latent_raw = matmul_high(hidden_one, wide_down)
    inv_query = lax.rsqrt(jnp.mean(latent_raw * latent_raw, axis=1, keepdims=True) + EPS_NORM)
    latent_hat = latent_raw * inv_query
    latent = latent_hat * gain_query
    pair_local = matmul_high(hidden_one, wide_pair)
    key_local = rotate(pair_local[:, :head_dim], local_position, 1.0)
    value_local = pair_local[:, head_dim:]
    packed_all = ring_gather(
        jnp.concatenate([latent, key_local, value_local], axis=1), heads_count, 1
    )
    latent_all = packed_all[:, :latent_dim]
    key_all = packed_all[:, latent_dim : latent_dim + head_dim]
    value_all = packed_all[:, latent_dim + head_dim :]
    query_rot = rotate(
        matmul_high(latent_all, wide_up).reshape(group_rows, local_heads, head_dim), position, 1.0
    )
    block_rows = min(512, group_rows)
    n_blocks = group_rows // block_rows
    query_blocks = query_rot.reshape(n_blocks, block_rows, local_heads, head_dim)
    index_blocks = group_index.reshape(n_blocks, block_rows)
    segment_blocks = segment.reshape(n_blocks, block_rows)

    def block_scores(query_block, row_block, seg_block):
        scores = jnp.einsum("qhd,kd->hqk", query_block, key_all, precision=HIGH) * scale
        allowed = (seg_block[:, None] == segment[None, :]) & (
            group_index[None, :] <= row_block[:, None]
        )
        return jnp.where(allowed[None], scores, -1e30)

    def forward_block(inputs):
        query_block, row_block, seg_block = inputs
        scores = block_scores(query_block, row_block, seg_block)
        row_max = jnp.max(scores, axis=2, keepdims=True)
        expo = jnp.exp(scores - row_max)
        denom = jnp.sum(expo, axis=2, keepdims=True)
        mixed_block = jnp.einsum("hqk,kd->qhd", expo / denom, value_all, precision=HIGH)
        return (mixed_block, (row_max + jnp.log(denom))[..., 0])

    mixed_blocks, lse_blocks = lax.map(forward_block, (query_blocks, index_blocks, segment_blocks))
    mixed_heads = mixed_blocks.reshape(group_rows, local_heads * head_dim)
    middle = block_input + ring_scatter(matmul_high(mixed_heads, wide_merge), heads_count, 2)
    inv_two = lax.rsqrt(jnp.mean(middle * middle, axis=1, keepdims=True) + EPS_NORM)
    normed_two = middle * inv_two
    hidden_two = normed_two * gain_ffn
    hidden_all = ring_gather(hidden_two, heads_count, 3)
    gate_pre = matmul_high(hidden_all, wide_gate)
    up_pre = matmul_high(hidden_all, wide_upper)
    sig_gate = jax.nn.sigmoid(gate_pre)
    silu_gate = gate_pre * sig_gate
    activ = silu_gate * up_pre
    block_output = middle + ring_scatter(matmul_high(activ, wide_lower), heads_count, 4)
    d_activ = matmul_high(grad_all, wide_lower.T)
    grad_lower = matmul_high(activ.T, grad_all)
    d_gate_pre = d_activ * up_pre * (sig_gate * (1.0 + gate_pre * (1.0 - sig_gate)))
    d_up_pre = d_activ * silu_gate
    grad_gate = matmul_high(hidden_all.T, d_gate_pre)
    grad_upper = matmul_high(hidden_all.T, d_up_pre)
    d_hidden_two = ring_scatter(
        matmul_high(d_gate_pre, wide_gate.T) + matmul_high(d_up_pre, wide_upper.T), heads_count, 6
    )
    d_normed_mid, grad_gain_ffn = norm_back(d_hidden_two, normed_two, inv_two, gain_ffn)
    d_middle = output_grad + d_normed_mid
    middle_all = ring_gather(d_middle, heads_count, 7)
    grad_merge = matmul_high(mixed_heads.T, middle_all)
    d_mixed = matmul_high(middle_all, wide_merge.T).reshape(
        n_blocks, block_rows, local_heads, head_dim
    )

    def backward_block(running, inputs):
        query_block, row_block, seg_block, grad_block, out_block, lse_block = inputs
        scores = block_scores(query_block, row_block, seg_block)
        probs = jnp.exp(scores - lse_block[..., None])
        d_probs = jnp.einsum("qhd,kd->hqk", grad_block, value_all, precision=HIGH)
        delta = jnp.sum(grad_block * out_block, axis=2)
        d_scores = probs * (d_probs - delta.T[:, :, None])
        d_query = jnp.einsum("hqk,kd->qhd", d_scores, key_all, precision=HIGH) * scale
        d_key = jnp.einsum("hqk,qhd->kd", d_scores, query_block, precision=HIGH) * scale
        d_value = jnp.einsum("hqk,qhd->kd", probs, grad_block, precision=HIGH)
        return ((running[0] + d_key, running[1] + d_value), d_query)

    zero_rows = jnp.zeros((group_rows, head_dim), jnp.float32)
    (d_key_sum, d_value_sum), d_query_blocks = lax.scan(
        backward_block,
        (zero_rows, zero_rows),
        (query_blocks, index_blocks, segment_blocks, d_mixed, mixed_blocks, lse_blocks),
    )
    d_query_pre = rotate(
        d_query_blocks.reshape(group_rows, local_heads, head_dim), position, -1.0
    ).reshape(group_rows, local_heads * head_dim)
    grad_up = matmul_high(latent_all.T, d_query_pre)
    d_latent_all = matmul_high(d_query_pre, wide_up.T)
    packed_grad = ring_scatter(
        jnp.concatenate([d_latent_all, d_key_sum, d_value_sum], axis=1), heads_count, 8
    )
    d_latent = packed_grad[:, :latent_dim]
    d_key_local = packed_grad[:, latent_dim : latent_dim + head_dim]
    d_value_local = packed_grad[:, latent_dim + head_dim :]
    d_pair = jnp.concatenate([rotate(d_key_local, local_position, -1.0), d_value_local], axis=1)
    d_latent_raw, grad_gain_query = norm_back(d_latent, latent_hat, inv_query, gain_query)
    grad_down = matmul_high(hidden_one.T, d_latent_raw)
    grad_pair = matmul_high(hidden_one.T, d_pair)
    d_hidden_one = matmul_high(d_latent_raw, wide_down.T) + matmul_high(d_pair, wide_pair.T)
    d_normed_in, grad_gain_attn = norm_back(d_hidden_one, normed_one, inv_one, gain_attn)
    input_grad = d_middle + d_normed_in
    grad_gains = jnp.concatenate([grad_gain_attn, grad_gain_query, grad_gain_ffn])
    spread = spread_grads(
        grad_down, grad_pair, grad_up, grad_merge, grad_gate, grad_upper, grad_lower
    )
    shared = ring_gather(
        ring_scatter(jnp.concatenate([spread[0], spread[1]], axis=1), heads_count, 9), heads_count, 10
    )
    reduced = (shared[:, :latent_dim], shared[:, latent_dim:]) + tuple(spread[2:])
    gains_total = lax.psum(grad_gains, ("dp", "heads"))
    values = (
        norm_gains,
        query_down,
        key_value,
        query_up,
        head_merge,
        gate_weight,
        up_weight,
        down_weight,
    )
    firsts = (
        norm_gains_first,
        query_down_first,
        key_value_first,
        query_up_first,
        head_merge_first,
        gate_weight_first,
        up_weight_first,
        down_weight_first,
    )
    seconds = (
        norm_gains_second,
        query_down_second,
        key_value_second,
        query_up_second,
        head_merge_second,
        gate_weight_second,
        up_weight_second,
        down_weight_second,
    )
    grads = (
        gains_total,
        reduced[0],
        reduced[1],
        reduced[2],
        reduced[3],
        reduced[4],
        reduced[5],
        reduced[6],
    )
    stepped = [moments(values[slot], grads[slot], firsts[slot], seconds[slot]) for slot in range(8)]
    replica_share = [1.0, 1.0 / heads_count, 1.0 / heads_count, 1.0, 1.0, 1.0, 1.0, 1.0]
    square_rows = jnp.stack(
        [
            jnp.stack(
                [jnp.sum(values[slot] * values[slot]), jnp.sum(stepped[slot][2] * stepped[slot][2])]
            )
            * replica_share[slot]
            for slot in range(1, 8)
        ]
    )
    summed = lax.psum(square_rows, ("dp", "heads"))
    gains_row = jnp.stack(
        [jnp.sum(norm_gains * norm_gains), jnp.sum(stepped[0][2] * stepped[0][2])]
    )
    norm_table = jnp.sqrt(jnp.concatenate([gains_row[None, :], summed], axis=0))
    new_values = [
        values[slot] - RATE * (norm_table[slot, 0] / norm_table[slot, 1]) * stepped[slot][2]
        for slot in range(8)
    ]
    return (
        block_output,
        input_grad,
        stepped[0][0],
        stepped[0][1],
        new_values[0],
        stepped[1][0],
        stepped[1][1],
        new_values[1],
        stepped[2][0],
        stepped[2][1],
        new_values[2],
        stepped[3][0],
        stepped[3][1],
        new_values[3],
        stepped[4][0],
        stepped[4][1],
        new_values[4],
        stepped[5][0],
        stepped[5][1],
        new_values[5],
        stepped[6][0],
        stepped[6][1],
        new_values[6],
        stepped[7][0],
        stepped[7][1],
        new_values[7],
        norm_table,
    )


def solution(mesh):
    placed = (
        P(("dp", "heads"), None),
        P(("dp", "heads"), None),
        P("dp", None),
        P(),
        P(),
        P(),
        P("dp", None),
        P("dp", None),
        P("dp", None),
        P("dp", None),
        P("dp", None),
        P("dp", None),
        P("dp", "heads"),
        P("dp", "heads"),
        P("dp", "heads"),
        P("heads", "dp"),
        P("heads", "dp"),
        P("heads", "dp"),
        P("dp", "heads"),
        P("dp", "heads"),
        P("dp", "heads"),
        P("dp", "heads"),
        P("dp", "heads"),
        P("dp", "heads"),
        P("heads", "dp"),
        P("heads", "dp"),
        P("heads", "dp"),
    )
    return jax.shard_map(
        on_device,
        mesh=mesh,
        in_specs=placed,
        out_specs=(
            P(("dp", "heads"), None),
            P(("dp", "heads"), None),
            P(),
            P(),
            P(),
            P("dp", None),
            P("dp", None),
            P("dp", None),
            P("dp", None),
            P("dp", None),
            P("dp", None),
            P("dp", "heads"),
            P("dp", "heads"),
            P("dp", "heads"),
            P("heads", "dp"),
            P("heads", "dp"),
            P("heads", "dp"),
            P("dp", "heads"),
            P("dp", "heads"),
            P("dp", "heads"),
            P("dp", "heads"),
            P("dp", "heads"),
            P("dp", "heads"),
            P("heads", "dp"),
            P("heads", "dp"),
            P("heads", "dp"),
            P(),
        ),
        check_vma=False,
    )
```

```python
import functools

import jax
import jax.numpy as jnp
from jax import lax
from jax.experimental import pallas as pl
from jax.experimental.pallas import tpu as pltpu
from jax.sharding import PartitionSpec as P

STEP_COUNT = 10


EPS_NORM = 1e-06
ROPE_BASE = 10000.0
BETA_ONE = 0.5
BETA_TWO = 0.6
ADAM_EPS = 1e-06
DECAY = 0.01
RATE = 0.5
HIGH = lax.Precision.HIGH
MESH = pl.DeviceIdType.MESH
RING_Z = 4


def head_at(spot, n):
    wide = n // RING_Z
    back = (spot + n - RING_Z) // n
    rest = jnp.maximum(spot - RING_Z, 0)
    row, step = rest // (wide - 1), rest % (wide - 1)
    odd = row % 2
    column = (1 - odd) * (1 + step) + odd * (wide - 1 - step)
    return (1 - back) * (spot * wide) + back * ((RING_Z - 1 - row) * wide + column)


def spot_of(head, n):
    wide = n // RING_Z
    row = RING_Z - 1 - head // wide
    column = head % wide
    odd = row % 2
    step = (1 - odd) * (column - 1) + odd * (wide - 1 - column)
    back = (column + wide - 1) // wide
    return (1 - back) * (head // wide) + back * (RING_Z + row * (wide - 1) + step)


def ring_places(n):
    me = lax.axis_index("heads")
    spot = spot_of(me, n)
    return me, lambda k: head_at(lax.rem(spot + k + 2 * n, n), n)


def others(axis):
    count = lax.axis_size(axis)
    me = lax.axis_index(axis)
    return [lax.rem(me + k, count) for k in range(1, count)]


def greet(names):
    bar = pltpu.get_barrier_semaphore()
    for name in names:
        pl.semaphore_signal(bar, inc=1, device_id=name, device_id_type=MESH)
    pl.semaphore_wait(bar, len(names))


def push(src, dst, send, recv, name):
    copy = pltpu.make_async_remote_copy(
        src_ref=src, dst_ref=dst, send_sem=send, recv_sem=recv, device_id=name, device_id_type=MESH
    )
    copy.start()
    return copy


class Ring:
    def __init__(self, n, cuts, x_ref, o_ref, sems):
        self.n, self.cuts, self.x, self.o = n, cuts, x_ref, o_ref
        self.own_sem, self.send_sem, self.recv_sem = sems
        self.me, self.at = ring_places(n)
        self.sides = ({"heads": self.at(1)}, {"heads": self.at(-1)})
        self.copies = {}

    def begin(self):
        rows = self.x.shape[0]
        self.own = pltpu.make_async_copy(self.x, self.o.at[pl.ds(self.me * rows, rows)], self.own_sem)
        self.own.start()

    def step(self, step):
        rows = self.x.shape[0]
        half = rows // 2
        piece = half // self.cuts
        for cut in range(self.cuts):
            for way in (0, 1):
                if step > 0:
                    self.copies[way, step - 1, cut].wait_recv()
                off = way * half + cut * piece
                origin = self.at(-step) if way == 0 else self.at(step)
                dst = self.o.at[pl.ds(origin * rows + off, piece)]
                src = self.x.at[pl.ds(off, piece)] if step == 0 else dst
                self.copies[way, step, cut] = push(
                    src, dst, self.send_sem.at[way, step, cut], self.recv_sem.at[way, step, cut], self.sides[way]
                )

    def end(self):
        for cut in range(self.cuts):
            for way in (0, 1):
                self.copies[way, self.n - 2, cut].wait_recv()
        for copy in self.copies.values():
            copy.wait_send()
        self.own.wait()

    @staticmethod
    def scratch(n, cuts):
        return [
            pltpu.SemaphoreType.DMA,
            pltpu.SemaphoreType.DMA((2, n - 1, cuts)),
            pltpu.SemaphoreType.DMA((2, n - 1, cuts)),
        ]


class Spread:
    def __init__(self, dp, x_ref, o_ref, sems):
        self.x, self.o, self.ny = x_ref, o_ref, dp // 2
        self.own_sem, self.y_send, self.y_recv, self.core_send, self.core_recv = sems
        me = lax.axis_index("dp")
        self.y, self.core = me // 2, me % 2
        self.me = me
        self.mate = {"dp": self.y * 2 + 1 - self.core}
        self.next = {"dp": lax.rem(self.y + 1, self.ny) * 2 + self.core}
        self.rows = x_ref.shape[0]

    def block(self, owner):
        return self.o.at[pl.ds(owner * self.rows, self.rows)]

    def begin(self):
        self.own = pltpu.make_async_copy(self.x, self.block(self.me), self.own_sem)
        self.own.start()
        self.y_copies = [push(self.x, self.block(self.me), self.y_send.at[0], self.y_recv.at[0], self.next)]
        self.core_copies = [push(self.x, self.block(self.me), self.core_send.at[0], self.core_recv.at[0], self.mate)]

    def end(self):
        for k in range(1, self.ny):
            self.y_copies[k - 1].wait_recv()
            held = self.block(lax.rem(self.y - k + self.ny, self.ny) * 2 + self.core)
            if k < self.ny - 1:
                self.y_copies.append(push(held, held, self.y_send.at[k], self.y_recv.at[k], self.next))
            self.core_copies.append(push(held, held, self.core_send.at[k], self.core_recv.at[k], self.mate))
        for copy in self.core_copies:
            copy.wait_recv()
        for copy in self.y_copies + self.core_copies:
            copy.wait_send()
        self.own.wait()

    @staticmethod
    def scratch(dp):
        ny = dp // 2
        return [
            pltpu.SemaphoreType.DMA,
            pltpu.SemaphoreType.DMA((ny - 1,)),
            pltpu.SemaphoreType.DMA((ny - 1,)),
            pltpu.SemaphoreType.DMA((ny,)),
            pltpu.SemaphoreType.DMA((ny,)),
        ]


class Swap:
    def __init__(self, dp, out, x_ref, o_ref, sems):
        self.dp, self.out, self.x, self.o = dp, out, x_ref, o_ref
        self.own_sem, self.send_sem, self.recv_sem = sems
        self.me = lax.axis_index("dp")

    def part(self, ref, index, by_columns):
        if by_columns:
            size = ref.shape[1] // self.dp
            return ref.at[:, pl.ds(pl.multiple_of(index * size, size), size)]
        size = ref.shape[0] // self.dp
        return ref.at[pl.ds(pl.multiple_of(index * size, size), size)]

    def begin(self):
        mine = self.part(self.o, self.me, not self.out)
        self.own = pltpu.make_async_copy(self.part(self.x, self.me, self.out), mine, self.own_sem)
        self.own.start()
        self.copies = [
            push(self.part(self.x, other, self.out), mine, self.send_sem.at[k], self.recv_sem.at[k], {"dp": other})
            for k, other in enumerate(others("dp"))
        ]

    def end(self):
        for copy in self.copies:
            copy.wait_recv()
        for copy in self.copies:
            copy.wait_send()
        self.own.wait()

    @staticmethod
    def scratch(dp):
        return [
            pltpu.SemaphoreType.DMA,
            pltpu.SemaphoreType.DMA((dp - 1,)),
            pltpu.SemaphoreType.DMA((dp - 1,)),
        ]


def cost(micros):
    return pl.CostEstimate(flops=0, bytes_accessed=int(micros * 3.0e6), transcendentals=0)


def spaces(count, space=pl.ANY):
    return [pl.BlockSpec(memory_space=space)] * count


def gather_body(n, cuts, x_ref, o_ref, *sems):
    ring = Ring(n, cuts, x_ref, o_ref, sems)
    greet(ring.sides)
    ring.begin()
    for step in range(n - 1):
        ring.step(step)
    ring.end()


def ring_gather(x, n, number, cuts=2):
    rows, columns = x.shape
    cuts = min(cuts, rows // 16)
    return pl.pallas_call(
        functools.partial(gather_body, n, cuts),
        out_shape=jax.ShapeDtypeStruct((n * rows, columns), x.dtype),
        in_specs=spaces(1, pltpu.VMEM),
        out_specs=pl.BlockSpec(memory_space=pl.ANY),
        scratch_shapes=Ring.scratch(n, cuts),
        compiler_params=pltpu.CompilerParams(collective_id=number, has_side_effects=True),
        cost_estimate=cost(75.0 * columns / 2048),
        name=f"ring_gather_{number}",
    )(x)


def opening_body(n, dp, cuts, grad, down, pair, hidden, grad_all, wide_down, wide_pair, hidden_turn, *sems):
    ring = Ring(n, cuts, grad, grad_all, sems[:3])
    parts = [
        Spread(dp, down, wide_down, sems[3:8]),
        Spread(dp, pair, wide_pair, sems[8:13]),
        Swap(dp, True, hidden, hidden_turn, sems[13:16]),
    ]
    greet(list(ring.sides) + [{"dp": other} for other in others("dp")])
    for part in parts:
        part.begin()
    ring.begin()
    for step in range(n - 1):
        ring.step(step)
    for part in parts:
        part.end()
    ring.end()


def opening(grad, down, pair, hidden, n, dp, number, cuts=2):
    def full(x, times):
        return jax.ShapeDtypeStruct((x.shape[0] * times, x.shape[1]), x.dtype)

    turned = jax.ShapeDtypeStruct((hidden.shape[0] * dp, hidden.shape[1] // dp), hidden.dtype)
    return pl.pallas_call(
        functools.partial(opening_body, n, dp, cuts),
        out_shape=(full(grad, n), full(down, dp), full(pair, dp), turned),
        in_specs=spaces(4, pltpu.VMEM),
        out_specs=tuple(spaces(4)),
        scratch_shapes=Ring.scratch(n, cuts) + Spread.scratch(dp) * 2 + Swap.scratch(dp),
        compiler_params=pltpu.CompilerParams(collective_id=number, has_side_effects=True),
        cost_estimate=cost(80.0),
        name="opening",
    )(grad, down, pair, hidden)


def spread_body(dp, x_ref, o_ref, *sems):
    part = Spread(dp, x_ref, o_ref, sems)
    greet([{"dp": other} for other in others("dp")])
    part.begin()
    part.end()


def dp_gather(x, dp, number):
    return pl.pallas_call(
        functools.partial(spread_body, dp),
        out_shape=jax.ShapeDtypeStruct((x.shape[0] * dp, x.shape[1]), x.dtype),
        in_specs=spaces(1, pltpu.VMEM),
        out_specs=pl.BlockSpec(memory_space=pl.ANY),
        scratch_shapes=Spread.scratch(dp),
        compiler_params=pltpu.CompilerParams(collective_id=number, has_side_effects=True),
        cost_estimate=cost(20.0),
        name=f"dp_gather_{number}",
    )(x)


class RingSum:
    def __init__(self, n, cuts, x_ref, o_ref, held, sems):
        self.n, self.cuts, self.x, self.o, self.held = n, cuts, x_ref, o_ref, held
        self.send_sem, self.recv_sem = sems
        self.me, self.at = ring_places(n)
        self.sides = ({"heads": self.at(1)}, {"heads": self.at(-1)})
        self.copies = {}
        self.rows = x_ref.shape[0] // n
        self.half = self.rows // 2
        self.piece = self.half // cuts

    def mine(self, owner, way, cut):
        return pl.ds(pl.multiple_of(owner * self.rows + way * self.half + cut * self.piece, 8), self.piece)

    def step(self, step):
        for cut in range(self.cuts):
            for way in (0, 1):
                owner = self.at(-1 - step) if way == 0 else self.at(1 + step)
                src = self.x.at[self.mine(owner, way, cut)]
                here = pl.ds(cut * self.piece, self.piece)
                if step > 0:
                    self.copies[way, step - 1, cut].wait_recv()
                    total = self.held.at[way, step - 1, here]
                    total[...] += src[...]
                    src = total
                self.copies[way, step, cut] = push(
                    src,
                    self.held.at[way, step, here],
                    self.send_sem.at[way, step, cut],
                    self.recv_sem.at[way, step, cut],
                    self.sides[way],
                )

    def end(self):
        for cut in range(self.cuts):
            for way in (0, 1):
                self.copies[way, self.n - 2, cut].wait_recv()
                self.o[pl.ds(way * self.half + cut * self.piece, self.piece)] = (
                    self.x[self.mine(self.me, way, cut)]
                    + self.held[way, self.n - 2, pl.ds(cut * self.piece, self.piece)]
                )
        for copy in self.copies.values():
            copy.wait_send()

    @staticmethod
    def scratch(n, cuts, rows, columns):
        return [
            pltpu.VMEM((2, n - 1, rows // 2, columns), jnp.float32),
            pltpu.SemaphoreType.DMA((2, n - 1, cuts)),
            pltpu.SemaphoreType.DMA((2, n - 1, cuts)),
        ]


def scatter_body(n, cuts, x_ref, o_ref, held, *sems):
    ring = RingSum(n, cuts, x_ref, o_ref, held, sems)
    greet(ring.sides)
    for step in range(n - 1):
        ring.step(step)
    ring.end()


def ring_scatter(x, n, number, cuts=4):
    rows, columns = x.shape[0] // n, x.shape[1]
    cuts = min(cuts, rows // 16)
    return pl.pallas_call(
        functools.partial(scatter_body, n, cuts),
        out_shape=jax.ShapeDtypeStruct((rows, columns), x.dtype),
        in_specs=spaces(1, pltpu.VMEM),
        out_specs=pl.BlockSpec(memory_space=pltpu.VMEM),
        scratch_shapes=RingSum.scratch(n, cuts, rows, columns),
        compiler_params=pltpu.CompilerParams(
            collective_id=number, has_side_effects=True, vmem_limit_bytes=40 << 20
        ),
        cost_estimate=cost(75.0 * columns / 2048),
        name=f"ring_scatter_{number}",
    )(x)


def turn_body(n, dp, cuts, x_ref, hidden, o_ref, hidden_turn, held, *sems):
    ring = RingSum(n, cuts, x_ref, o_ref, held, sems[:2])
    swap = Swap(dp, False, hidden, hidden_turn, sems[2:])
    greet(list(ring.sides) + [{"dp": other} for other in others("dp")])
    swap.begin()
    for step in range(n - 1):
        ring.step(step)
    swap.end()
    ring.end()


def scatter_and_turn(x, hidden, n, dp, number, cuts=2):
    rows, columns = x.shape[0] // n, x.shape[1]
    cuts = min(cuts, rows // 16)
    return pl.pallas_call(
        functools.partial(turn_body, n, dp, cuts),
        out_shape=(
            jax.ShapeDtypeStruct((rows, columns), x.dtype),
            jax.ShapeDtypeStruct((hidden.shape[0] // dp, hidden.shape[1] * dp), x.dtype),
        ),
        in_specs=spaces(2, pltpu.VMEM),
        out_specs=(pl.BlockSpec(memory_space=pltpu.VMEM), pl.BlockSpec(memory_space=pl.ANY)),
        scratch_shapes=RingSum.scratch(n, cuts, rows, columns) + Swap.scratch(dp),
        compiler_params=pltpu.CompilerParams(
            collective_id=number, has_side_effects=True, vmem_limit_bytes=40 << 20
        ),
        cost_estimate=cost(35.0),
        name="scatter_and_turn",
    )(x, hidden)


class Total:
    def __init__(self, axis, x_ref, held, sems):
        self.x, self.held = x_ref, held
        self.send_sem, self.recv_sem = sems
        self.names = [{axis: other} for other in others(axis)]
        self.count = lax.axis_size(axis)

    def begin(self):
        self.copies = [
            push(self.x, self.held.at[k], self.send_sem.at[k], self.recv_sem.at[k], name)
            for k, name in enumerate(self.names)
        ]

    def end(self):
        for copy in self.copies:
            copy.wait_recv()
        for copy in self.copies:
            copy.wait_send()

    @staticmethod
    def scratch(count, shape):
        return [
            pltpu.VMEM((count - 1,) + shape, jnp.float32),
            pltpu.SemaphoreType.DMA((count - 1,)),
            pltpu.SemaphoreType.DMA((count - 1,)),
        ]


def in_order(axis, own, held):
    count = lax.axis_size(axis)
    me = lax.axis_index(axis)
    total = None
    for device in range(count):
        term = jnp.where(me == device, own, jnp.zeros_like(own))
        for k in range(1, count):
            term = term + jnp.where(lax.rem(me - k + count, count) == device, held[k - 1], jnp.zeros_like(own))
        total = term if total is None else total + term
    return total


def sum_body(x_ref, o_ref, middle, held_heads, hs, hr, held_dp, ds, dr):
    first = Total("heads", x_ref, held_heads, (hs, hr))
    second = Total("dp", middle, held_dp, (ds, dr))
    greet(first.names + second.names)
    first.begin()
    first.end()
    middle[...] = in_order("heads", x_ref[...], held_heads)
    second.begin()
    second.end()
    o_ref[...] = in_order("dp", middle[...], held_dp)


def sum_all(x, n, dp, number):
    return pl.pallas_call(
        sum_body,
        out_shape=jax.ShapeDtypeStruct(x.shape, x.dtype),
        in_specs=spaces(1, pltpu.VMEM),
        out_specs=pl.BlockSpec(memory_space=pltpu.VMEM),
        scratch_shapes=[pltpu.VMEM(x.shape, x.dtype)] + Total.scratch(n, x.shape) + Total.scratch(dp, x.shape),
        compiler_params=pltpu.CompilerParams(collective_id=number, has_side_effects=True),
        cost_estimate=cost(8.0),
        name=f"sum_all_{number}",
    )(x)


def matmul_high(left, right):
    return jnp.dot(left, right, precision=HIGH, preferred_element_type=jnp.float32)


def layout(lengths_row, row_index):
    upto = jnp.arange(lengths_row.shape[0], dtype=jnp.int32)
    doc_ends = jnp.sum(jnp.where(upto[None, :] <= upto[:, None], lengths_row[None, :], 0), axis=1)
    doc_starts = doc_ends - lengths_row
    segment = jnp.sum((row_index[:, None] >= doc_ends[None, :]).astype(jnp.int32), axis=1)
    doc_ids = jnp.arange(doc_ends.shape[0], dtype=jnp.int32)
    start_of = jnp.sum(
        jnp.where(segment[:, None] == doc_ids[None, :], doc_starts[None, :], 0), axis=1
    )
    return (segment, row_index - start_of)


def rotate(vector, position, sign):
    half_dim = vector.shape[-1] // 2
    frequency = ROPE_BASE ** (-jnp.arange(half_dim, dtype=jnp.float32) / half_dim)
    angles = position.astype(jnp.float32)[:, None] * frequency[None, :]
    angles = angles.reshape((angles.shape[0],) + (1,) * (vector.ndim - 2) + (half_dim,))
    cosine = jnp.cos(angles)
    sines = sign * jnp.sin(angles)
    front = vector[..., :half_dim]
    back_half = vector[..., half_dim:]
    return jnp.concatenate(
        [front * cosine - back_half * sines, back_half * cosine + front * sines], axis=-1
    )


def norm_back(upstream, normed, inverse, gain):
    scaled = upstream * gain
    return (
        inverse * (scaled - normed * jnp.mean(scaled * normed, axis=1, keepdims=True)),
        jnp.sum(upstream * normed, axis=0),
    )


def owned(part, axis):
    return lax.psum_scatter(part, "dp", scatter_dimension=axis, tiled=True)


def moments(value, grad, first, second):
    first_new = BETA_ONE * first + (1.0 - BETA_ONE) * grad
    second_new = BETA_TWO * second + (1.0 - BETA_TWO) * grad * grad
    update = (
        first_new
        / (1.0 - BETA_ONE**STEP_COUNT)
        / (jnp.sqrt(second_new / (1.0 - BETA_TWO**STEP_COUNT)) + ADAM_EPS)
        + DECAY * value
    )
    return (first_new, second_new, update)


def on_device(
    block_input,
    output_grad,
    lengths,
    norm_gains,
    norm_gains_first,
    norm_gains_second,
    query_down,
    query_down_first,
    query_down_second,
    key_value,
    key_value_first,
    key_value_second,
    query_up,
    query_up_first,
    query_up_second,
    head_merge,
    head_merge_first,
    head_merge_second,
    gate_weight,
    gate_weight_first,
    gate_weight_second,
    up_weight,
    up_weight_first,
    up_weight_second,
    down_weight,
    down_weight_first,
    down_weight_second,
):
    tok_rows = block_input.shape[0]
    model_dim = block_input.shape[1]
    latent_dim = query_down.shape[1]
    head_dim = key_value.shape[1] // 2
    local_heads = query_up.shape[1] // head_dim
    heads_count = lax.axis_size("heads")
    dp_count = lax.axis_size("dp")
    group_rows = tok_rows * heads_count
    scale = head_dim ** (-0.5)
    group_index = jnp.arange(group_rows, dtype=jnp.int32)
    segment, position = layout(lengths[0], group_index)
    local_position = lax.dynamic_slice_in_dim(
        position, lax.axis_index("heads") * tok_rows, tok_rows
    )
    gain_attn = norm_gains[:model_dim]
    gain_query = norm_gains[model_dim : model_dim + latent_dim]
    gain_ffn = norm_gains[model_dim + latent_dim :]
    inv_one = lax.rsqrt(jnp.mean(block_input * block_input, axis=1, keepdims=True) + EPS_NORM)
    normed_one = block_input * inv_one
    hidden_one = normed_one * gain_attn
    grad_all, wide_down, wide_pair, hidden_turn = opening(
        output_grad, query_down, key_value, hidden_one, heads_count, dp_count, 5
    )
    query_up_in, head_merge_in, gate_in, upper_in, lower_in, grad_all = lax.optimization_barrier(
        (query_up, head_merge, gate_weight, up_weight, down_weight, grad_all)
    )
    wide_up = lax.all_gather(query_up_in, "dp", axis=0, tiled=True)
    wide_merge = lax.all_gather(head_merge_in, "dp", axis=1, tiled=True)
    latent_raw = matmul_high(hidden_one, wide_down)
    inv_query = lax.rsqrt(jnp.mean(latent_raw * latent_raw, axis=1, keepdims=True) + EPS_NORM)
    latent_hat = latent_raw * inv_query
    latent = latent_hat * gain_query
    pair_local = matmul_high(hidden_one, wide_pair)
    key_local = rotate(pair_local[:, :head_dim], local_position, 1.0)
    value_local = pair_local[:, head_dim:]
    packed_all = ring_gather(
        jnp.concatenate([latent, key_local, value_local], axis=1), heads_count, 1
    )
    gate_in, upper_in, lower_in, packed_all = lax.optimization_barrier((gate_in, upper_in, lower_in, packed_all))
    wide_gate = lax.all_gather(gate_in, "dp", axis=0, tiled=True)
    wide_upper = lax.all_gather(upper_in, "dp", axis=0, tiled=True)
    wide_lower = lax.all_gather(lower_in, "dp", axis=1, tiled=True)
    latent_all = packed_all[:, :latent_dim]
    key_all = packed_all[:, latent_dim : latent_dim + head_dim]
    value_all = packed_all[:, latent_dim + head_dim :]
    query_rot = rotate(
        matmul_high(latent_all, wide_up).reshape(group_rows, local_heads, head_dim), position, 1.0
    )
    block_rows = min(512, group_rows)
    n_blocks = group_rows // block_rows
    query_blocks = query_rot.reshape(n_blocks, block_rows, local_heads, head_dim)
    index_blocks = group_index.reshape(n_blocks, block_rows)
    segment_blocks = segment.reshape(n_blocks, block_rows)

    def block_scores(query_block, row_block, seg_block):
        scores = jnp.einsum("qhd,kd->hqk", query_block, key_all, precision=HIGH) * scale
        allowed = (seg_block[:, None] == segment[None, :]) & (
            group_index[None, :] <= row_block[:, None]
        )
        return jnp.where(allowed[None], scores, -1e30)

    def forward_block(inputs):
        query_block, row_block, seg_block = inputs
        scores = block_scores(query_block, row_block, seg_block)
        row_max = jnp.max(scores, axis=2, keepdims=True)
        expo = jnp.exp(scores - row_max)
        denom = jnp.sum(expo, axis=2, keepdims=True)
        mixed_block = jnp.einsum("hqk,kd->qhd", expo / denom, value_all, precision=HIGH)
        return (mixed_block, (row_max + jnp.log(denom))[..., 0])

    mixed_blocks, lse_blocks = lax.map(forward_block, (query_blocks, index_blocks, segment_blocks))
    mixed_heads = mixed_blocks.reshape(group_rows, local_heads * head_dim)
    middle = block_input + ring_scatter(matmul_high(mixed_heads, wide_merge), heads_count, 2)
    inv_two = lax.rsqrt(jnp.mean(middle * middle, axis=1, keepdims=True) + EPS_NORM)
    normed_two = middle * inv_two
    hidden_two = normed_two * gain_ffn
    hidden_all = ring_gather(hidden_two, heads_count, 3)
    gate_pre = matmul_high(hidden_all, wide_gate)
    up_pre = matmul_high(hidden_all, wide_upper)
    sig_gate = jax.nn.sigmoid(gate_pre)
    silu_gate = gate_pre * sig_gate
    activ = silu_gate * up_pre
    part_output, grad_lower = lax.optimization_barrier(
        (matmul_high(activ, wide_lower), matmul_high(activ.T, grad_all))
    )
    grad_lower = owned(grad_lower, 1)
    block_output = middle + ring_scatter(part_output, heads_count, 4)
    d_activ = matmul_high(grad_all, wide_lower.T)
    d_gate_pre = d_activ * up_pre * (sig_gate * (1.0 + gate_pre * (1.0 - sig_gate)))
    d_up_pre = d_activ * silu_gate
    part_two, grad_gate, block_output = lax.optimization_barrier(
        (
            matmul_high(d_gate_pre, wide_gate.T) + matmul_high(d_up_pre, wide_upper.T),
            matmul_high(hidden_all.T, d_gate_pre),
            block_output,
        )
    )
    grad_gate = owned(grad_gate, 0)
    part_two, grad_lower = lax.optimization_barrier((part_two, grad_lower))
    d_hidden_two = ring_scatter(part_two, heads_count, 6)
    d_hidden_two, grad_upper = lax.optimization_barrier(
        (d_hidden_two, matmul_high(hidden_all.T, d_up_pre))
    )
    grad_upper = owned(grad_upper, 0)
    d_normed_mid, grad_gain_ffn = norm_back(d_hidden_two, normed_two, inv_two, gain_ffn)
    d_middle = output_grad + d_normed_mid
    d_middle, grad_gate = lax.optimization_barrier((d_middle, grad_gate))
    middle_all = ring_gather(d_middle, heads_count, 7)
    part_merge, grad_upper = lax.optimization_barrier((matmul_high(mixed_heads.T, middle_all), grad_upper))
    grad_merge = owned(part_merge, 1)
    d_mixed = matmul_high(middle_all, wide_merge.T).reshape(
        n_blocks, block_rows, local_heads, head_dim
    )

    def backward_block(running, inputs):
        query_block, row_block, seg_block, grad_block, out_block, lse_block = inputs
        scores = block_scores(query_block, row_block, seg_block)
        probs = jnp.exp(scores - lse_block[..., None])
        d_probs = jnp.einsum("qhd,kd->hqk", grad_block, value_all, precision=HIGH)
        delta = jnp.sum(grad_block * out_block, axis=2)
        d_scores = probs * (d_probs - delta.T[:, :, None])
        d_query = jnp.einsum("hqk,kd->qhd", d_scores, key_all, precision=HIGH) * scale
        d_key = jnp.einsum("hqk,qhd->kd", d_scores, query_block, precision=HIGH) * scale
        d_value = jnp.einsum("hqk,qhd->kd", probs, grad_block, precision=HIGH)
        return ((running[0] + d_key, running[1] + d_value), d_query)

    zero_rows = jnp.zeros((group_rows, head_dim), jnp.float32)
    (d_key_sum, d_value_sum), d_query_blocks = lax.scan(
        backward_block,
        (zero_rows, zero_rows),
        (query_blocks, index_blocks, segment_blocks, d_mixed, mixed_blocks, lse_blocks),
    )
    d_query_pre = rotate(
        d_query_blocks.reshape(group_rows, local_heads, head_dim), position, -1.0
    ).reshape(group_rows, local_heads * head_dim)
    d_latent_all = matmul_high(d_query_pre, wide_up.T)
    packed_part, grad_up = lax.optimization_barrier(
        (
            jnp.concatenate([d_latent_all, d_key_sum, d_value_sum], axis=1),
            matmul_high(latent_all.T, d_query_pre),
        )
    )
    grad_up, grad_merge = lax.optimization_barrier((grad_up, grad_merge))
    grad_up = owned(grad_up, 0)
    packed_grad = ring_scatter(packed_part, heads_count, 8)
    d_latent = packed_grad[:, :latent_dim]
    d_key_local = packed_grad[:, latent_dim : latent_dim + head_dim]
    d_value_local = packed_grad[:, latent_dim + head_dim :]
    d_pair = jnp.concatenate([rotate(d_key_local, local_position, -1.0), d_value_local], axis=1)
    d_latent_raw, grad_gain_query = norm_back(d_latent, latent_hat, inv_query, gain_query)
    raw, grad_merge = lax.optimization_barrier((jnp.concatenate([d_latent_raw, d_pair], axis=1), grad_merge))
    raw_all = dp_gather(raw, dp_count, 11)
    part_shared = matmul_high(hidden_turn.T, raw_all)
    d_hidden_turn = matmul_high(raw_all, jnp.concatenate([query_down, key_value], axis=1).T)
    shared_cut, d_hidden_one = scatter_and_turn(part_shared, d_hidden_turn, heads_count, dp_count, 9)
    shared = ring_gather(shared_cut, heads_count, 10)
    d_normed_in, grad_gain_attn = norm_back(d_hidden_one, normed_one, inv_one, gain_attn)
    input_grad = d_middle + d_normed_in
    grad_gains = jnp.concatenate([grad_gain_attn, grad_gain_query, grad_gain_ffn])
    gains_total = sum_all(grad_gains.reshape(-1, 128), heads_count, dp_count, 12).reshape(-1)
    values = (
        norm_gains,
        query_down,
        key_value,
        query_up,
        head_merge,
        gate_weight,
        up_weight,
        down_weight,
    )
    firsts = (
        norm_gains_first,
        query_down_first,
        key_value_first,
        query_up_first,
        head_merge_first,
        gate_weight_first,
        up_weight_first,
        down_weight_first,
    )
    seconds = (
        norm_gains_second,
        query_down_second,
        key_value_second,
        query_up_second,
        head_merge_second,
        gate_weight_second,
        up_weight_second,
        down_weight_second,
    )
    grads = (
        gains_total,
        shared[:, :latent_dim],
        shared[:, latent_dim:],
        grad_up,
        grad_merge,
        grad_gate,
        grad_upper,
        grad_lower,
    )
    stepped = [moments(values[slot], grads[slot], firsts[slot], seconds[slot]) for slot in range(8)]
    replica_share = [1.0, 1.0 / heads_count, 1.0 / heads_count, 1.0, 1.0, 1.0, 1.0, 1.0]
    square_rows = jnp.stack(
        [
            jnp.stack(
                [jnp.sum(values[slot] * values[slot]), jnp.sum(stepped[slot][2] * stepped[slot][2])]
            )
            * replica_share[slot]
            for slot in range(1, 8)
        ]
    )
    square_tile = jnp.zeros((8, 128), jnp.float32).at[:7, :2].set(square_rows)
    summed = sum_all(square_tile, heads_count, dp_count, 13)[:7, :2]
    gains_row = jnp.stack(
        [jnp.sum(norm_gains * norm_gains), jnp.sum(stepped[0][2] * stepped[0][2])]
    )
    norm_table = jnp.sqrt(jnp.concatenate([gains_row[None, :], summed], axis=0))
    new_values = [
        values[slot] - RATE * (norm_table[slot, 0] / norm_table[slot, 1]) * stepped[slot][2]
        for slot in range(8)
    ]
    return (
        block_output,
        input_grad,
        stepped[0][0],
        stepped[0][1],
        new_values[0],
        stepped[1][0],
        stepped[1][1],
        new_values[1],
        stepped[2][0],
        stepped[2][1],
        new_values[2],
        stepped[3][0],
        stepped[3][1],
        new_values[3],
        stepped[4][0],
        stepped[4][1],
        new_values[4],
        stepped[5][0],
        stepped[5][1],
        new_values[5],
        stepped[6][0],
        stepped[6][1],
        new_values[6],
        stepped[7][0],
        stepped[7][1],
        new_values[7],
        norm_table,
    )


def solution(mesh):
    placed = (
        P(("dp", "heads"), None),
        P(("dp", "heads"), None),
        P("dp", None),
        P(),
        P(),
        P(),
        P("dp", None),
        P("dp", None),
        P("dp", None),
        P("dp", None),
        P("dp", None),
        P("dp", None),
        P("dp", "heads"),
        P("dp", "heads"),
        P("dp", "heads"),
        P("heads", "dp"),
        P("heads", "dp"),
        P("heads", "dp"),
        P("dp", "heads"),
        P("dp", "heads"),
        P("dp", "heads"),
        P("dp", "heads"),
        P("dp", "heads"),
        P("dp", "heads"),
        P("heads", "dp"),
        P("heads", "dp"),
        P("heads", "dp"),
    )
    return jax.shard_map(
        on_device,
        mesh=mesh,
        in_specs=placed,
        out_specs=(
            P(("dp", "heads"), None),
            P(("dp", "heads"), None),
            P(),
            P(),
            P(),
            P("dp", None),
            P("dp", None),
            P("dp", None),
            P("dp", None),
            P("dp", None),
            P("dp", None),
            P("dp", "heads"),
            P("dp", "heads"),
            P("dp", "heads"),
            P("heads", "dp"),
            P("heads", "dp"),
            P("heads", "dp"),
            P("dp", "heads"),
            P("dp", "heads"),
            P("dp", "heads"),
            P("dp", "heads"),
            P("dp", "heads"),
            P("dp", "heads"),
            P("heads", "dp"),
            P("heads", "dp"),
            P("heads", "dp"),
            P(),
        ),
        check_vma=False,
    )
```

```python
import functools

import jax
import jax.numpy as jnp
from jax import lax
from jax.experimental import pallas as pl
from jax.experimental.pallas import tpu as pltpu
from jax.sharding import PartitionSpec as P

STEP_COUNT = 10


EPS_NORM = 1e-06
ROPE_BASE = 10000.0
BETA_ONE = 0.5
BETA_TWO = 0.6
ADAM_EPS = 1e-06
DECAY = 0.01
RATE = 0.5
HIGH = lax.Precision.HIGH
MESH = pl.DeviceIdType.MESH
RING_Z = 4


def head_at(spot, n):
    wide = n // RING_Z
    back = (spot + n - RING_Z) // n
    rest = jnp.maximum(spot - RING_Z, 0)
    row, step = rest // (wide - 1), rest % (wide - 1)
    odd = row % 2
    column = (1 - odd) * (1 + step) + odd * (wide - 1 - step)
    return (1 - back) * (spot * wide) + back * ((RING_Z - 1 - row) * wide + column)


def spot_of(head, n):
    wide = n // RING_Z
    row = RING_Z - 1 - head // wide
    column = head % wide
    odd = row % 2
    step = (1 - odd) * (column - 1) + odd * (wide - 1 - column)
    back = (column + wide - 1) // wide
    return (1 - back) * (head // wide) + back * (RING_Z + row * (wide - 1) + step)


def ring_places(n):
    me = lax.axis_index("heads")
    spot = spot_of(me, n)
    return me, lambda k: head_at(lax.rem(spot + k + 2 * n, n), n)


def others(axis):
    count = lax.axis_size(axis)
    me = lax.axis_index(axis)
    return [lax.rem(me + k, count) for k in range(1, count)]


def greet(names):
    bar = pltpu.get_barrier_semaphore()
    for name in names:
        pl.semaphore_signal(bar, inc=1, device_id=name, device_id_type=MESH)
    pl.semaphore_wait(bar, len(names))


def remote(src, dst, send, recv, name):
    return pltpu.make_async_remote_copy(
        src_ref=src, dst_ref=dst, send_sem=send, recv_sem=recv, device_id=name, device_id_type=MESH
    )


def push(*what):
    copy = remote(*what)
    copy.start()
    return copy


def halves(value):
    high = value.astype(jnp.bfloat16)
    return high, (value - high.astype(jnp.float32)).astype(jnp.bfloat16)


def padded(shape, size):
    return shape[0] * -(-shape[1] // 128) * 128 * size


class Job:
    def __init__(self, form, lefts, rights, tile):
        self.form, self.lefts, self.rights, self.tile = form, lefts, rights, tile
        self.summed = len(lefts) > 1
        rows = rights[0].shape[0]
        self.chunk = next(c for c in (512, 352, 256, 128, 64, 32, 16) if rows % c == 0)
        if form == "tn":
            self.chunk = next(c for c in (256, 128) if rows % c == 0)
            self.extent = lefts[0].shape[1]
        else:
            self.extent = lefts[0].shape[0]
        self.chunks = rows // self.chunk
        self.prepare = self.chunks * len(rights)
        self.units = self.prepare + self.extent // tile
        width = {"nt": 0, "nn": 1, "tn": 1}[form]
        shapes = [
            (x.shape[1], self.extent) if form == "tn" else (self.extent, x.shape[width]) for x in rights
        ]
        self.outs = shapes[:1] if self.summed else shapes
        self.splits = [x.shape[::-1] if form == "tn" else x.shape for x in rights]

    def bare(self):
        kept = object.__new__(Job)
        kept.__dict__.update(self.__dict__)
        kept.lefts, kept.rights = len(self.lefts), len(self.rights)
        return kept

    def scratch(self):
        made = [pltpu.VMEM(x.shape, jnp.float32) for x in self.lefts + self.rights]
        for shape in self.splits:
            made += [pltpu.VMEM(shape, jnp.bfloat16)] * 2
        made += [pltpu.VMEM(shape, jnp.float32) for shape in self.outs]
        made += [pltpu.SemaphoreType.DMA((len(self.lefts) + len(self.rights),))]
        made += [pltpu.SemaphoreType.DMA((len(self.outs), self.extent // self.tile))]
        return made

    def bytes(self):
        shapes = [x.shape for x in self.lefts + self.rights] + self.splits + self.outs
        return sum(padded(shape, 4) for shape in shapes)


def limit(jobs, *shapes):
    return (8 << 20) + sum(job.bytes() for job in jobs) + sum(padded(shape, 4) for shape in shapes)


class Work:
    def __init__(self, plan, refs, firsts):
        refs = list(refs)

        def take(count):
            taken = refs[:count]
            del refs[:count]
            return taken

        sources = [take(job.lefts + job.rights) for job in plan]
        self.first = take(firsts)
        sinks = [take(len(job.outs)) for job in plan]
        self.jobs = []
        for job, source, sink in zip(plan, sources, sinks):
            held = take(job.lefts + job.rights)
            split = [take(2) for _ in range(job.rights)]
            outs = take(len(job.outs))
            in_sem, out_sem = take(2)
            self.jobs.append((job, source, sink, held, split, outs, in_sem, out_sem))
        self.rest = refs
        self.units = sum(job.units for job in plan)

    @staticmethod
    def operands(jobs):
        return [x for job in jobs for x in job.lefts + job.rights]

    @staticmethod
    def outputs(jobs):
        return [jax.ShapeDtypeStruct(shape, jnp.float32) for job in jobs for shape in job.outs]

    @staticmethod
    def scratch(jobs):
        return [x for job in jobs for x in job.scratch()]

    def loads(self):
        return [
            pltpu.make_async_copy(source[k], held[k], in_sem.at[k])
            for _, source, _, held, _, _, in_sem, _ in self.jobs
            for k in range(len(source))
        ]

    def load(self):
        for copy in self.loads():
            copy.start()

    def ready(self):
        for copy in self.loads():
            copy.wait()

    def share(self, steps, step):
        if not self.jobs:
            return

        def unit(index, carry):
            base = 0
            for entry in self.jobs:
                job = entry[0]
                for k in range(job.rights):
                    self.when(index, base + k * job.chunks, job.chunks, functools.partial(self.split, entry, k))
                self.when(
                    index, base + job.prepare, job.units - job.prepare, functools.partial(self.tile, entry)
                )
                base += job.units
            return carry

        lax.fori_loop(step * self.units // steps, (step + 1) * self.units // steps, unit, 0)

    def when(self, index, start, count, act):
        @pl.when((index >= start) & (index < start + count))
        def _():
            act(index - start)

    def split(self, entry, k, chunk):
        job, held, split = entry[0], entry[3], entry[4]
        rows = pl.ds(pl.multiple_of(chunk * job.chunk, job.chunk), job.chunk)
        value = held[job.lefts + k][rows, :]
        where = (slice(None), rows) if job.form == "tn" else (rows, slice(None))
        split[k][0][where], split[k][1][where] = halves(value.T if job.form == "tn" else value)

    def tile(self, entry, index):
        job, _, sink, held, split, outs, _, out_sem = entry
        rows = pl.ds(pl.multiple_of(index * job.tile, job.tile), job.tile)
        numbers = (((1,), (1 if job.form == "nt" else 0,)), ((), ()))
        where = (slice(None), rows) if job.form == "tn" else (rows, slice(None))

        def product(own, other):
            pair = (other, own) if job.form == "tn" else (own, other)
            return lax.dot_general(*pair, numbers, preferred_element_type=jnp.float32)

        total = None
        for k in range(job.lefts):
            high, low = halves(held[k][where])
            for j in [k] if job.summed else range(job.rights):
                right_high, right_low = split[j][0][...], split[j][1][...]
                made = product(high, right_high) + product(high, right_low) + product(low, right_high)
                if job.summed:
                    total = made if total is None else total + made
                else:
                    outs[j][where] = made
        if job.summed:
            outs[0][where] = total
        for j, out in enumerate(outs):
            pltpu.make_async_copy(out.at[where], sink[j].at[where], out_sem.at[j, index]).start()

    def end(self):
        for job, _, sink, _, _, outs, _, out_sem in self.jobs:
            for j, out in enumerate(outs):
                for index in range(job.extent // job.tile):
                    rows = pl.ds(index * job.tile, job.tile)
                    where = (slice(None), rows) if job.form == "tn" else (rows, slice(None))
                    pltpu.make_async_copy(out.at[where], sink[j].at[where], out_sem.at[j, index]).wait()


class Ring:
    def __init__(self, n, cuts, x_ref, o_ref, sems):
        self.n, self.cuts, self.x, self.o = n, cuts, x_ref, o_ref
        self.own_sem, self.send_sem, self.recv_sem = sems
        self.me, self.at = ring_places(n)
        self.sides = ({"heads": self.at(1)}, {"heads": self.at(-1)})
        self.rows = x_ref.shape[0]
        self.piece = self.rows // 2 // cuts
        self.parts = [(cut, way) for cut in range(cuts) for way in (0, 1)]

    def copy(self, step, cut, way, first=False):
        off = way * (self.rows // 2) + cut * self.piece
        origin = self.at(-step) if way == 0 else self.at(step)
        dst = self.o.at[pl.ds(pl.multiple_of(origin * self.rows + off, 8), self.piece)]
        src = self.x.at[pl.ds(off, self.piece)] if first else dst
        sems = self.send_sem.at[way, step, cut], self.recv_sem.at[way, step, cut]
        return remote(src, dst, *sems, self.sides[way])

    def own(self):
        here = self.o.at[pl.ds(pl.multiple_of(self.me * self.rows, 8), self.rows)]
        return pltpu.make_async_copy(self.x, here, self.own_sem)

    def begin(self):
        self.own().start()
        for part in self.parts:
            self.copy(0, *part, first=True).start()

    def step(self, step):
        for part in self.parts:
            self.copy(step - 1, *part).wait_recv()
            self.copy(step, *part).start()

    def end(self):
        for part in self.parts:
            self.copy(self.n - 2, *part).wait_recv()

        def sent(step, carry):
            for part in self.parts:
                self.copy(step, *part).wait_send()
            return carry

        lax.fori_loop(0, self.n - 1, sent, 0)
        self.own().wait()

    def run(self, work=None):
        def body(step, carry):
            if work is not None:
                work(step - 1)

            @pl.when(step < self.n - 1)
            def _():
                self.step(step)

            return carry

        lax.fori_loop(1, self.n, body, 0)

    @staticmethod
    def scratch(n, cuts):
        return [
            pltpu.SemaphoreType.DMA,
            pltpu.SemaphoreType.DMA((2, n - 1, cuts)),
            pltpu.SemaphoreType.DMA((2, n - 1, cuts)),
        ]


class Spread:
    def __init__(self, dp, x_ref, o_ref, sems):
        self.x, self.o, self.ny = x_ref, o_ref, dp // 2
        self.own_sem, self.y_send, self.y_recv, self.core_send, self.core_recv = sems
        me = lax.axis_index("dp")
        self.y, self.core = me // 2, me % 2
        self.me = me
        self.mate = {"dp": self.y * 2 + 1 - self.core}
        self.next = {"dp": lax.rem(self.y + 1, self.ny) * 2 + self.core}
        self.rows = x_ref.shape[0]

    def block(self, owner):
        return self.o.at[pl.ds(owner * self.rows, self.rows)]

    def begin(self):
        self.own = pltpu.make_async_copy(self.x, self.block(self.me), self.own_sem)
        self.own.start()
        self.y_copies = [push(self.x, self.block(self.me), self.y_send.at[0], self.y_recv.at[0], self.next)]
        self.core_copies = [push(self.x, self.block(self.me), self.core_send.at[0], self.core_recv.at[0], self.mate)]

    def end(self):
        for k in range(1, self.ny):
            self.y_copies[k - 1].wait_recv()
            held = self.block(lax.rem(self.y - k + self.ny, self.ny) * 2 + self.core)
            if k < self.ny - 1:
                self.y_copies.append(push(held, held, self.y_send.at[k], self.y_recv.at[k], self.next))
            self.core_copies.append(push(held, held, self.core_send.at[k], self.core_recv.at[k], self.mate))
        for copy in self.core_copies:
            copy.wait_recv()
        for copy in self.y_copies + self.core_copies:
            copy.wait_send()
        self.own.wait()

    @staticmethod
    def scratch(dp):
        ny = dp // 2
        return [
            pltpu.SemaphoreType.DMA,
            pltpu.SemaphoreType.DMA((ny - 1,)),
            pltpu.SemaphoreType.DMA((ny - 1,)),
            pltpu.SemaphoreType.DMA((ny,)),
            pltpu.SemaphoreType.DMA((ny,)),
        ]


class Swap:
    def __init__(self, dp, out, x_ref, o_ref, sems):
        self.dp, self.out, self.x, self.o = dp, out, x_ref, o_ref
        self.own_sem, self.send_sem, self.recv_sem = sems
        self.me = lax.axis_index("dp")

    def part(self, ref, index, by_columns):
        if by_columns:
            size = ref.shape[1] // self.dp
            return ref.at[:, pl.ds(pl.multiple_of(index * size, size), size)]
        size = ref.shape[0] // self.dp
        return ref.at[pl.ds(pl.multiple_of(index * size, size), size)]

    def begin(self):
        mine = self.part(self.o, self.me, not self.out)
        self.own = pltpu.make_async_copy(self.part(self.x, self.me, self.out), mine, self.own_sem)
        self.own.start()
        self.copies = [
            push(self.part(self.x, other, self.out), mine, self.send_sem.at[k], self.recv_sem.at[k], {"dp": other})
            for k, other in enumerate(others("dp"))
        ]

    def end(self):
        for copy in self.copies:
            copy.wait_recv()
        for copy in self.copies:
            copy.wait_send()
        self.own.wait()

    @staticmethod
    def scratch(dp):
        return [
            pltpu.SemaphoreType.DMA,
            pltpu.SemaphoreType.DMA((dp - 1,)),
            pltpu.SemaphoreType.DMA((dp - 1,)),
        ]


def cost(micros):
    return pl.CostEstimate(flops=0, bytes_accessed=int(micros * 3.0e6), transcendentals=0)


def spaces(count, space=pl.ANY):
    return [pl.BlockSpec(memory_space=space)] * count


def gather_body(n, cuts, plan, x_ref, *refs):
    work = Work(plan, refs, 1)
    ring = Ring(n, cuts, x_ref, work.first[0], work.rest)
    work.load()
    greet(ring.sides)
    ring.begin()
    work.ready()
    ring.run(functools.partial(work.share, n - 1))
    ring.end()
    work.end()


def ring_gather(x, n, number, jobs=(), cuts=2):
    rows, columns = x.shape
    cuts = min(cuts, rows // 16)
    plan = [job.bare() for job in jobs]
    result = pl.pallas_call(
        functools.partial(gather_body, n, cuts, plan),
        out_shape=(jax.ShapeDtypeStruct((n * rows, columns), x.dtype), *Work.outputs(jobs)),
        in_specs=spaces(1, pltpu.VMEM) + spaces(len(Work.operands(jobs))),
        out_specs=tuple(spaces(1 + len(Work.outputs(jobs)))),
        scratch_shapes=Work.scratch(jobs) + Ring.scratch(n, cuts),
        compiler_params=pltpu.CompilerParams(
            collective_id=number, has_side_effects=True, vmem_limit_bytes=limit(jobs, x.shape)
        ),
        cost_estimate=cost(75.0 * columns / 2048),
        name=f"ring_gather_{number}",
    )(x, *Work.operands(jobs))
    return result if jobs else result[0]


def opening_body(n, dp, cuts, grad, down, pair, hidden, grad_all, wide_down, wide_pair, hidden_turn, *sems):
    ring = Ring(n, cuts, grad, grad_all, sems[:3])
    parts = [
        Spread(dp, down, wide_down, sems[3:8]),
        Spread(dp, pair, wide_pair, sems[8:13]),
        Swap(dp, True, hidden, hidden_turn, sems[13:16]),
    ]
    greet(list(ring.sides) + [{"dp": other} for other in others("dp")])
    for part in parts:
        part.begin()
    ring.begin()
    ring.run()
    for part in parts:
        part.end()
    ring.end()


def opening(grad, down, pair, hidden, n, dp, number, cuts=2):
    def full(x, times):
        return jax.ShapeDtypeStruct((x.shape[0] * times, x.shape[1]), x.dtype)

    turned = jax.ShapeDtypeStruct((hidden.shape[0] * dp, hidden.shape[1] // dp), hidden.dtype)
    return pl.pallas_call(
        functools.partial(opening_body, n, dp, cuts),
        out_shape=(full(grad, n), full(down, dp), full(pair, dp), turned),
        in_specs=spaces(4, pltpu.VMEM),
        out_specs=tuple(spaces(4)),
        scratch_shapes=Ring.scratch(n, cuts) + Spread.scratch(dp) * 2 + Swap.scratch(dp),
        compiler_params=pltpu.CompilerParams(collective_id=number, has_side_effects=True),
        cost_estimate=cost(80.0),
        name="opening",
    )(grad, down, pair, hidden)


def spread_body(dp, x_ref, o_ref, *sems):
    part = Spread(dp, x_ref, o_ref, sems)
    greet([{"dp": other} for other in others("dp")])
    part.begin()
    part.end()


def dp_gather(x, dp, number):
    return pl.pallas_call(
        functools.partial(spread_body, dp),
        out_shape=jax.ShapeDtypeStruct((x.shape[0] * dp, x.shape[1]), x.dtype),
        in_specs=spaces(1, pltpu.VMEM),
        out_specs=pl.BlockSpec(memory_space=pl.ANY),
        scratch_shapes=Spread.scratch(dp),
        compiler_params=pltpu.CompilerParams(collective_id=number, has_side_effects=True),
        cost_estimate=cost(20.0),
        name=f"dp_gather_{number}",
    )(x)


class RingSum:
    def __init__(self, n, cuts, x_ref, o_ref, held, sems):
        self.n, self.cuts, self.x, self.o, self.held = n, cuts, x_ref, o_ref, held
        self.send_sem, self.recv_sem = sems
        self.me, self.at = ring_places(n)
        self.sides = ({"heads": self.at(1)}, {"heads": self.at(-1)})
        self.rows = x_ref.shape[0] // n
        self.half = self.rows // 2
        self.piece = self.half // cuts
        self.parts = [(cut, way) for cut in range(cuts) for way in (0, 1)]

    def mine(self, owner, cut, way):
        start = owner * self.rows + way * self.half + cut * self.piece
        return self.x.at[pl.ds(pl.multiple_of(start, 8), self.piece)]

    def slot(self, step, cut, way):
        return self.held.at[way, step, pl.ds(cut * self.piece, self.piece)]

    def owner(self, step, way):
        return self.at(-1 - step) if way == 0 else self.at(1 + step)

    def copy(self, step, cut, way, first=False):
        src = self.mine(self.owner(step, way), cut, way) if first else self.slot(step - 1, cut, way)
        sems = self.send_sem.at[way, step, cut], self.recv_sem.at[way, step, cut]
        return remote(src, self.slot(step, cut, way), *sems, self.sides[way])

    def begin(self):
        for part in self.parts:
            self.copy(0, *part, first=True).start()

    def step(self, step):
        for cut, way in self.parts:
            self.arrived(step - 1, cut, way)
            total = self.slot(step - 1, cut, way)
            total[...] += self.mine(self.owner(step, way), cut, way)[...]
            self.copy(step, cut, way).start()

    def arrived(self, step, cut, way):
        slot = self.slot(step, cut, way)
        sems = self.send_sem.at[way, step, cut], self.recv_sem.at[way, step, cut]
        remote(slot, slot, *sems, self.sides[way]).wait_recv()

    def end(self):
        for cut, way in self.parts:
            self.arrived(self.n - 2, cut, way)
            self.o[pl.ds(way * self.half + cut * self.piece, self.piece)] = (
                self.mine(self.me, cut, way)[...] + self.slot(self.n - 2, cut, way)[...]
            )

        def sent(step, carry):
            for cut, way in self.parts:
                slot = self.slot(step, cut, way)
                sems = self.send_sem.at[way, step, cut], self.recv_sem.at[way, step, cut]
                remote(slot, slot, *sems, self.sides[way]).wait_send()
            return carry

        lax.fori_loop(0, self.n - 1, sent, 0)

    run = Ring.run

    @staticmethod
    def scratch(n, cuts, rows, columns):
        return [
            pltpu.VMEM((2, n - 1, rows // 2, columns), jnp.float32),
            pltpu.SemaphoreType.DMA((2, n - 1, cuts)),
            pltpu.SemaphoreType.DMA((2, n - 1, cuts)),
        ]


def scatter_body(n, cuts, plan, x_ref, *refs):
    work = Work(plan, refs, 1)
    ring = RingSum(n, cuts, x_ref, work.first[0], work.rest[0], work.rest[1:])
    work.load()
    greet(ring.sides)
    ring.begin()
    work.ready()
    ring.run(functools.partial(work.share, n - 1))
    ring.end()
    work.end()


def ring_scatter(x, n, number, jobs=(), cuts=4):
    rows, columns = x.shape[0] // n, x.shape[1]
    cuts = min(cuts, rows // 16)
    plan = [job.bare() for job in jobs]
    result = pl.pallas_call(
        functools.partial(scatter_body, n, cuts, plan),
        out_shape=(jax.ShapeDtypeStruct((rows, columns), x.dtype), *Work.outputs(jobs)),
        in_specs=spaces(1, pltpu.VMEM) + spaces(len(Work.operands(jobs))),
        out_specs=tuple(spaces(1, pltpu.VMEM) + spaces(len(Work.outputs(jobs)))),
        scratch_shapes=Work.scratch(jobs) + RingSum.scratch(n, cuts, rows, columns),
        compiler_params=pltpu.CompilerParams(
            collective_id=number, has_side_effects=True, vmem_limit_bytes=limit(jobs, x.shape, x.shape, (rows, columns))
        ),
        cost_estimate=cost(75.0 * columns / 2048),
        name=f"ring_scatter_{number}",
    )(x, *Work.operands(jobs))
    return result if jobs else result[0]


def turn_body(n, dp, cuts, x_ref, hidden, o_ref, hidden_turn, held, *sems):
    ring = RingSum(n, cuts, x_ref, o_ref, held, sems[:2])
    swap = Swap(dp, False, hidden, hidden_turn, sems[2:])
    greet(list(ring.sides) + [{"dp": other} for other in others("dp")])
    swap.begin()
    ring.begin()
    ring.run()
    swap.end()
    ring.end()


def scatter_and_turn(x, hidden, n, dp, number, cuts=2):
    rows, columns = x.shape[0] // n, x.shape[1]
    cuts = min(cuts, rows // 16)
    return pl.pallas_call(
        functools.partial(turn_body, n, dp, cuts),
        out_shape=(
            jax.ShapeDtypeStruct((rows, columns), x.dtype),
            jax.ShapeDtypeStruct((hidden.shape[0] // dp, hidden.shape[1] * dp), x.dtype),
        ),
        in_specs=spaces(2, pltpu.VMEM),
        out_specs=(pl.BlockSpec(memory_space=pltpu.VMEM), pl.BlockSpec(memory_space=pl.ANY)),
        scratch_shapes=RingSum.scratch(n, cuts, rows, columns) + Swap.scratch(dp),
        compiler_params=pltpu.CompilerParams(
            collective_id=number, has_side_effects=True, vmem_limit_bytes=40 << 20
        ),
        cost_estimate=cost(35.0),
        name="scatter_and_turn",
    )(x, hidden)


class Total:
    def __init__(self, axis, x_ref, held, sems):
        self.x, self.held = x_ref, held
        self.send_sem, self.recv_sem = sems
        self.names = [{axis: other} for other in others(axis)]
        self.count = lax.axis_size(axis)

    def begin(self):
        self.copies = [
            push(self.x, self.held.at[k], self.send_sem.at[k], self.recv_sem.at[k], name)
            for k, name in enumerate(self.names)
        ]

    def end(self):
        for copy in self.copies:
            copy.wait_recv()
        for copy in self.copies:
            copy.wait_send()

    @staticmethod
    def scratch(count, shape):
        return [
            pltpu.VMEM((count - 1,) + shape, jnp.float32),
            pltpu.SemaphoreType.DMA((count - 1,)),
            pltpu.SemaphoreType.DMA((count - 1,)),
        ]


def in_order(axis, own, held):
    count = lax.axis_size(axis)
    me = lax.axis_index(axis)
    total = None
    for device in range(count):
        term = jnp.where(me == device, own, jnp.zeros_like(own))
        for k in range(1, count):
            term = term + jnp.where(lax.rem(me - k + count, count) == device, held[k - 1], jnp.zeros_like(own))
        total = term if total is None else total + term
    return total


def sum_body(x_ref, o_ref, middle, held_heads, hs, hr, held_dp, ds, dr):
    first = Total("heads", x_ref, held_heads, (hs, hr))
    second = Total("dp", middle, held_dp, (ds, dr))
    greet(first.names + second.names)
    first.begin()
    first.end()
    middle[...] = in_order("heads", x_ref[...], held_heads)
    second.begin()
    second.end()
    o_ref[...] = in_order("dp", middle[...], held_dp)


def sum_all(x, n, dp, number):
    return pl.pallas_call(
        sum_body,
        out_shape=jax.ShapeDtypeStruct(x.shape, x.dtype),
        in_specs=spaces(1, pltpu.VMEM),
        out_specs=pl.BlockSpec(memory_space=pltpu.VMEM),
        scratch_shapes=[pltpu.VMEM(x.shape, x.dtype)] + Total.scratch(n, x.shape) + Total.scratch(dp, x.shape),
        compiler_params=pltpu.CompilerParams(collective_id=number, has_side_effects=True),
        cost_estimate=cost(8.0),
        name=f"sum_all_{number}",
    )(x)


def matmul_high(left, right):
    return jnp.dot(left, right, precision=HIGH, preferred_element_type=jnp.float32)


def layout(lengths_row, row_index):
    upto = jnp.arange(lengths_row.shape[0], dtype=jnp.int32)
    doc_ends = jnp.sum(jnp.where(upto[None, :] <= upto[:, None], lengths_row[None, :], 0), axis=1)
    doc_starts = doc_ends - lengths_row
    segment = jnp.sum((row_index[:, None] >= doc_ends[None, :]).astype(jnp.int32), axis=1)
    doc_ids = jnp.arange(doc_ends.shape[0], dtype=jnp.int32)
    start_of = jnp.sum(
        jnp.where(segment[:, None] == doc_ids[None, :], doc_starts[None, :], 0), axis=1
    )
    return (segment, row_index - start_of)


def rotate(vector, position, sign):
    half_dim = vector.shape[-1] // 2
    frequency = ROPE_BASE ** (-jnp.arange(half_dim, dtype=jnp.float32) / half_dim)
    angles = position.astype(jnp.float32)[:, None] * frequency[None, :]
    angles = angles.reshape((angles.shape[0],) + (1,) * (vector.ndim - 2) + (half_dim,))
    cosine = jnp.cos(angles)
    sines = sign * jnp.sin(angles)
    front = vector[..., :half_dim]
    back_half = vector[..., half_dim:]
    return jnp.concatenate(
        [front * cosine - back_half * sines, back_half * cosine + front * sines], axis=-1
    )


def norm_back(upstream, normed, inverse, gain):
    scaled = upstream * gain
    return (
        inverse * (scaled - normed * jnp.mean(scaled * normed, axis=1, keepdims=True)),
        jnp.sum(upstream * normed, axis=0),
    )


def owned(part, axis):
    return lax.psum_scatter(part, "dp", scatter_dimension=axis, tiled=True)


def moments(value, grad, first, second):
    first_new = BETA_ONE * first + (1.0 - BETA_ONE) * grad
    second_new = BETA_TWO * second + (1.0 - BETA_TWO) * grad * grad
    update = (
        first_new
        / (1.0 - BETA_ONE**STEP_COUNT)
        / (jnp.sqrt(second_new / (1.0 - BETA_TWO**STEP_COUNT)) + ADAM_EPS)
        + DECAY * value
    )
    return (first_new, second_new, update)


def on_device(
    block_input,
    output_grad,
    lengths,
    norm_gains,
    norm_gains_first,
    norm_gains_second,
    query_down,
    query_down_first,
    query_down_second,
    key_value,
    key_value_first,
    key_value_second,
    query_up,
    query_up_first,
    query_up_second,
    head_merge,
    head_merge_first,
    head_merge_second,
    gate_weight,
    gate_weight_first,
    gate_weight_second,
    up_weight,
    up_weight_first,
    up_weight_second,
    down_weight,
    down_weight_first,
    down_weight_second,
):
    tok_rows = block_input.shape[0]
    model_dim = block_input.shape[1]
    latent_dim = query_down.shape[1]
    head_dim = key_value.shape[1] // 2
    local_heads = query_up.shape[1] // head_dim
    heads_count = lax.axis_size("heads")
    dp_count = lax.axis_size("dp")
    group_rows = tok_rows * heads_count
    scale = head_dim ** (-0.5)
    group_index = jnp.arange(group_rows, dtype=jnp.int32)
    segment, position = layout(lengths[0], group_index)
    local_position = lax.dynamic_slice_in_dim(
        position, lax.axis_index("heads") * tok_rows, tok_rows
    )
    gain_attn = norm_gains[:model_dim]
    gain_query = norm_gains[model_dim : model_dim + latent_dim]
    gain_ffn = norm_gains[model_dim + latent_dim :]
    inv_one = lax.rsqrt(jnp.mean(block_input * block_input, axis=1, keepdims=True) + EPS_NORM)
    normed_one = block_input * inv_one
    hidden_one = normed_one * gain_attn
    grad_all, wide_down, wide_pair, hidden_turn = opening(
        output_grad, query_down, key_value, hidden_one, heads_count, dp_count, 5
    )
    query_up_in, head_merge_in, gate_in, upper_in, lower_in, grad_all = lax.optimization_barrier(
        (query_up, head_merge, gate_weight, up_weight, down_weight, grad_all)
    )
    wide_up = lax.all_gather(query_up_in, "dp", axis=0, tiled=True)
    wide_merge = lax.all_gather(head_merge_in, "dp", axis=1, tiled=True)
    latent_raw = matmul_high(hidden_one, wide_down)
    inv_query = lax.rsqrt(jnp.mean(latent_raw * latent_raw, axis=1, keepdims=True) + EPS_NORM)
    latent_hat = latent_raw * inv_query
    latent = latent_hat * gain_query
    pair_local = matmul_high(hidden_one, wide_pair)
    key_local = rotate(pair_local[:, :head_dim], local_position, 1.0)
    value_local = pair_local[:, head_dim:]
    packed_all = ring_gather(
        jnp.concatenate([latent, key_local, value_local], axis=1), heads_count, 1
    )
    gate_in, upper_in, lower_in, packed_all = lax.optimization_barrier((gate_in, upper_in, lower_in, packed_all))
    turned_gate = lax.all_gather(gate_in.T, "dp", axis=1, tiled=True)
    turned_upper = lax.all_gather(upper_in.T, "dp", axis=1, tiled=True)
    wide_lower = lax.all_gather(lower_in, "dp", axis=1, tiled=True)
    latent_all = packed_all[:, :latent_dim]
    key_all = packed_all[:, latent_dim : latent_dim + head_dim]
    value_all = packed_all[:, latent_dim + head_dim :]
    query_rot = rotate(
        matmul_high(latent_all, wide_up).reshape(group_rows, local_heads, head_dim), position, 1.0
    )
    block_rows = min(512, group_rows)
    n_blocks = group_rows // block_rows
    query_blocks = query_rot.reshape(n_blocks, block_rows, local_heads, head_dim)
    index_blocks = group_index.reshape(n_blocks, block_rows)
    segment_blocks = segment.reshape(n_blocks, block_rows)

    def block_scores(query_block, row_block, seg_block):
        scores = jnp.einsum("qhd,kd->hqk", query_block, key_all, precision=HIGH) * scale
        allowed = (seg_block[:, None] == segment[None, :]) & (
            group_index[None, :] <= row_block[:, None]
        )
        return jnp.where(allowed[None], scores, -1e30)

    def forward_block(inputs):
        query_block, row_block, seg_block = inputs
        scores = block_scores(query_block, row_block, seg_block)
        row_max = jnp.max(scores, axis=2, keepdims=True)
        expo = jnp.exp(scores - row_max)
        denom = jnp.sum(expo, axis=2, keepdims=True)
        mixed_block = jnp.einsum("hqk,kd->qhd", expo / denom, value_all, precision=HIGH)
        return (mixed_block, (row_max + jnp.log(denom))[..., 0])

    mixed_blocks, lse_blocks = lax.map(forward_block, (query_blocks, index_blocks, segment_blocks))
    mixed_heads = mixed_blocks.reshape(group_rows, local_heads * head_dim)
    middle = block_input + ring_scatter(matmul_high(mixed_heads, wide_merge), heads_count, 2)
    inv_two = lax.rsqrt(jnp.mean(middle * middle, axis=1, keepdims=True) + EPS_NORM)
    normed_two = middle * inv_two
    hidden_two = normed_two * gain_ffn
    inside = group_rows <= 1024

    def job(form, lefts, rights, tile):
        return [Job(form, lefts, rights, tile)] if inside else []

    made = ring_gather(hidden_two, heads_count, 3, job("nt", [grad_all], [wide_lower], 256))
    hidden_all, d_activ = made if inside else (made, matmul_high(grad_all, wide_lower.T))
    gate_pre = matmul_high(hidden_all, turned_gate.T)
    up_pre = matmul_high(hidden_all, turned_upper.T)
    sig_gate = jax.nn.sigmoid(gate_pre)
    silu_gate = gate_pre * sig_gate
    activ = silu_gate * up_pre
    d_gate_pre = d_activ * up_pre * (sig_gate * (1.0 + gate_pre * (1.0 - sig_gate)))
    d_up_pre = d_activ * silu_gate
    part_output = matmul_high(activ, wide_lower)
    if inside:
        part_output, part_two = ring_scatter(
            part_output,
            heads_count,
            4,
            job("nn", [d_gate_pre, d_up_pre], [turned_gate, turned_upper], 128),
        )
        d_hidden_two, grad_gate, grad_lower = ring_scatter(
            part_two,
            heads_count,
            6,
            job("tn", [hidden_all], [d_gate_pre], 256) + job("tn", [grad_all], [activ], 256),
        )
    else:
        part_output = ring_scatter(part_output, heads_count, 4)
        part_two = matmul_high(d_gate_pre, turned_gate) + matmul_high(d_up_pre, turned_upper)
        d_hidden_two = ring_scatter(part_two, heads_count, 6)
        grad_gate = matmul_high(d_gate_pre.T, hidden_all)
        grad_lower = matmul_high(activ.T, grad_all)
    block_output = middle + part_output
    grad_gate = owned(grad_gate, 1)
    d_normed_mid, grad_gain_ffn = norm_back(d_hidden_two, normed_two, inv_two, gain_ffn)
    d_middle = output_grad + d_normed_mid
    made = ring_gather(d_middle, heads_count, 7, job("tn", [hidden_all], [d_up_pre], 256))
    middle_all, grad_upper = made if inside else (made, matmul_high(d_up_pre.T, hidden_all))
    middle_all, grad_gate, grad_lower = lax.optimization_barrier((middle_all, grad_gate, grad_lower))
    grad_lower = owned(grad_lower, 1)
    d_mixed = matmul_high(middle_all, wide_merge.T).reshape(
        n_blocks, block_rows, local_heads, head_dim
    )

    def backward_block(running, inputs):
        query_block, row_block, seg_block, grad_block, out_block, lse_block = inputs
        scores = block_scores(query_block, row_block, seg_block)
        probs = jnp.exp(scores - lse_block[..., None])
        d_probs = jnp.einsum("qhd,kd->hqk", grad_block, value_all, precision=HIGH)
        delta = jnp.sum(grad_block * out_block, axis=2)
        d_scores = probs * (d_probs - delta.T[:, :, None])
        d_query = jnp.einsum("hqk,kd->qhd", d_scores, key_all, precision=HIGH) * scale
        d_key = jnp.einsum("hqk,qhd->kd", d_scores, query_block, precision=HIGH) * scale
        d_value = jnp.einsum("hqk,qhd->kd", probs, grad_block, precision=HIGH)
        return ((running[0] + d_key, running[1] + d_value), d_query)

    zero_rows = jnp.zeros((group_rows, head_dim), jnp.float32)
    (d_key_sum, d_value_sum), d_query_blocks = lax.scan(
        backward_block,
        (zero_rows, zero_rows),
        (query_blocks, index_blocks, segment_blocks, d_mixed, mixed_blocks, lse_blocks),
    )
    d_query_pre = rotate(
        d_query_blocks.reshape(group_rows, local_heads, head_dim), position, -1.0
    ).reshape(group_rows, local_heads * head_dim)
    d_latent_all = matmul_high(d_query_pre, wide_up.T)
    packed_part = jnp.concatenate([d_latent_all, d_key_sum, d_value_sum], axis=1)
    packed_part, grad_lower, grad_upper = lax.optimization_barrier((packed_part, grad_lower, grad_upper))
    grad_upper = owned(grad_upper, 1)
    if inside:
        packed_grad, grad_merge, grad_up = ring_scatter(
            packed_part,
            heads_count,
            8,
            job("tn", [middle_all], [mixed_heads], 256) + job("tn", [d_query_pre], [latent_all], 256),
        )
    else:
        packed_grad = ring_scatter(packed_part, heads_count, 8)
        grad_merge = matmul_high(mixed_heads.T, middle_all)
        grad_up = matmul_high(latent_all.T, d_query_pre)
    packed_grad, grad_merge, grad_upper = lax.optimization_barrier((packed_grad, grad_merge, grad_upper))
    grad_merge = owned(grad_merge, 1)
    grad_up, grad_merge = lax.optimization_barrier((grad_up, grad_merge))
    grad_up = owned(grad_up, 0)
    d_latent = packed_grad[:, :latent_dim]
    d_key_local = packed_grad[:, latent_dim : latent_dim + head_dim]
    d_value_local = packed_grad[:, latent_dim + head_dim :]
    d_pair = jnp.concatenate([rotate(d_key_local, local_position, -1.0), d_value_local], axis=1)
    d_latent_raw, grad_gain_query = norm_back(d_latent, latent_hat, inv_query, gain_query)
    raw = jnp.concatenate([d_latent_raw, d_pair], axis=1)
    raw_all = dp_gather(raw, dp_count, 11)
    part_shared = matmul_high(hidden_turn.T, raw_all)
    d_hidden_turn = matmul_high(raw_all, jnp.concatenate([query_down, key_value], axis=1).T)
    shared_cut, d_hidden_one = scatter_and_turn(part_shared, d_hidden_turn, heads_count, dp_count, 9)
    shared = ring_gather(shared_cut, heads_count, 10)
    d_normed_in, grad_gain_attn = norm_back(d_hidden_one, normed_one, inv_one, gain_attn)
    input_grad = d_middle + d_normed_in
    grad_gains = jnp.concatenate([grad_gain_attn, grad_gain_query, grad_gain_ffn])
    gains_total = sum_all(grad_gains.reshape(-1, 128), heads_count, dp_count, 12).reshape(-1)
    values = (
        norm_gains,
        query_down,
        key_value,
        query_up,
        head_merge,
        gate_weight,
        up_weight,
        down_weight,
    )
    firsts = (
        norm_gains_first,
        query_down_first,
        key_value_first,
        query_up_first,
        head_merge_first,
        gate_weight_first,
        up_weight_first,
        down_weight_first,
    )
    seconds = (
        norm_gains_second,
        query_down_second,
        key_value_second,
        query_up_second,
        head_merge_second,
        gate_weight_second,
        up_weight_second,
        down_weight_second,
    )
    grads = (
        gains_total,
        shared[:, :latent_dim],
        shared[:, latent_dim:],
        grad_up,
        grad_merge,
        grad_gate.T,
        grad_upper.T,
        grad_lower,
    )
    stepped = [moments(values[slot], grads[slot], firsts[slot], seconds[slot]) for slot in range(8)]
    replica_share = [1.0, 1.0 / heads_count, 1.0 / heads_count, 1.0, 1.0, 1.0, 1.0, 1.0]
    square_rows = jnp.stack(
        [
            jnp.stack(
                [jnp.sum(values[slot] * values[slot]), jnp.sum(stepped[slot][2] * stepped[slot][2])]
            )
            * replica_share[slot]
            for slot in range(1, 8)
        ]
    )
    square_tile = jnp.zeros((8, 128), jnp.float32).at[:7, :2].set(square_rows)
    summed = sum_all(square_tile, heads_count, dp_count, 13)[:7, :2]
    gains_row = jnp.stack(
        [jnp.sum(norm_gains * norm_gains), jnp.sum(stepped[0][2] * stepped[0][2])]
    )
    norm_table = jnp.sqrt(jnp.concatenate([gains_row[None, :], summed], axis=0))
    new_values = [
        values[slot] - RATE * (norm_table[slot, 0] / norm_table[slot, 1]) * stepped[slot][2]
        for slot in range(8)
    ]
    return (
        block_output,
        input_grad,
        stepped[0][0],
        stepped[0][1],
        new_values[0],
        stepped[1][0],
        stepped[1][1],
        new_values[1],
        stepped[2][0],
        stepped[2][1],
        new_values[2],
        stepped[3][0],
        stepped[3][1],
        new_values[3],
        stepped[4][0],
        stepped[4][1],
        new_values[4],
        stepped[5][0],
        stepped[5][1],
        new_values[5],
        stepped[6][0],
        stepped[6][1],
        new_values[6],
        stepped[7][0],
        stepped[7][1],
        new_values[7],
        norm_table,
    )


def solution(mesh):
    placed = (
        P(("dp", "heads"), None),
        P(("dp", "heads"), None),
        P("dp", None),
        P(),
        P(),
        P(),
        P("dp", None),
        P("dp", None),
        P("dp", None),
        P("dp", None),
        P("dp", None),
        P("dp", None),
        P("dp", "heads"),
        P("dp", "heads"),
        P("dp", "heads"),
        P("heads", "dp"),
        P("heads", "dp"),
        P("heads", "dp"),
        P("dp", "heads"),
        P("dp", "heads"),
        P("dp", "heads"),
        P("dp", "heads"),
        P("dp", "heads"),
        P("dp", "heads"),
        P("heads", "dp"),
        P("heads", "dp"),
        P("heads", "dp"),
    )
    return jax.shard_map(
        on_device,
        mesh=mesh,
        in_specs=placed,
        out_specs=(
            P(("dp", "heads"), None),
            P(("dp", "heads"), None),
            P(),
            P(),
            P(),
            P("dp", None),
            P("dp", None),
            P("dp", None),
            P("dp", None),
            P("dp", None),
            P("dp", None),
            P("dp", "heads"),
            P("dp", "heads"),
            P("dp", "heads"),
            P("heads", "dp"),
            P("heads", "dp"),
            P("heads", "dp"),
            P("dp", "heads"),
            P("dp", "heads"),
            P("dp", "heads"),
            P("dp", "heads"),
            P("dp", "heads"),
            P("dp", "heads"),
            P("heads", "dp"),
            P("heads", "dp"),
            P("heads", "dp"),
            P(),
        ),
        check_vma=False,
    )
```

```python
import functools

import jax
import jax.numpy as jnp
from jax import lax
from jax.experimental import pallas as pl
from jax.experimental.pallas import tpu as pltpu
from jax.sharding import PartitionSpec as P

STEP_COUNT = 10


EPS_NORM = 1e-06
ROPE_BASE = 10000.0
BETA_ONE = 0.5
BETA_TWO = 0.6
ADAM_EPS = 1e-06
DECAY = 0.01
RATE = 0.5
HIGH = lax.Precision.HIGH
MESH = pl.DeviceIdType.MESH
RING_Z = 4


def head_at(spot, n):
    wide = n // RING_Z
    back = (spot + n - RING_Z) // n
    rest = jnp.maximum(spot - RING_Z, 0)
    row, step = rest // (wide - 1), rest % (wide - 1)
    odd = row % 2
    column = (1 - odd) * (1 + step) + odd * (wide - 1 - step)
    return (1 - back) * (spot * wide) + back * ((RING_Z - 1 - row) * wide + column)


def spot_of(head, n):
    wide = n // RING_Z
    row = RING_Z - 1 - head // wide
    column = head % wide
    odd = row % 2
    step = (1 - odd) * (column - 1) + odd * (wide - 1 - column)
    back = (column + wide - 1) // wide
    return (1 - back) * (head // wide) + back * (RING_Z + row * (wide - 1) + step)


def ring_places(n):
    me = lax.axis_index("heads")
    spot = spot_of(me, n)
    return me, lambda k: head_at(lax.rem(spot + k + 2 * n, n), n)


def others(axis):
    count = lax.axis_size(axis)
    me = lax.axis_index(axis)
    return [lax.rem(me + k, count) for k in range(1, count)]


def greet(names):
    bar = pltpu.get_barrier_semaphore()
    for name in names:
        pl.semaphore_signal(bar, inc=1, device_id=name, device_id_type=MESH)
    pl.semaphore_wait(bar, len(names))


def remote(src, dst, send, recv, name):
    return pltpu.make_async_remote_copy(
        src_ref=src, dst_ref=dst, send_sem=send, recv_sem=recv, device_id=name, device_id_type=MESH
    )


def push(*what):
    copy = remote(*what)
    copy.start()
    return copy


def halves(value):
    high = value.astype(jnp.bfloat16)
    return high, (value - high.astype(jnp.float32)).astype(jnp.bfloat16)


def padded(shape, size):
    return shape[0] * -(-shape[1] // 128) * 128 * size


class Job:
    def __init__(self, form, lefts, rights, tile, joined=False):
        self.joined = joined
        self.form, self.lefts, self.tile = form, lefts, tile
        self.whole = [x[0] if isinstance(x, tuple) else x for x in rights]
        rights = [x[1] if isinstance(x, tuple) else x for x in rights]
        self.rights = rights
        self.summed = len(lefts) > 1
        rows = rights[0].shape[0]
        self.chunk = next(c for c in (512, 352, 256, 128, 64, 32, 16) if rows % c == 0)
        if form == "tn":
            self.chunk = next(c for c in (256, 128) if rows % c == 0)
            self.extent = lefts[0].shape[1]
        else:
            self.extent = lefts[0].shape[0]
        self.chunks = rows // self.chunk
        self.prepare = self.chunks * len(rights)
        self.units = self.prepare + self.extent // tile
        width = {"nt": 0, "nn": 1, "tn": 1}[form]
        shapes = [
            (x.shape[1], self.extent) if form == "tn" else (self.extent, x.shape[width]) for x in rights
        ]
        self.outs = shapes[:1] if self.summed else shapes
        self.splits = [x.shape[::-1] if form == "tn" else x.shape for x in rights]

    def bare(self):
        kept = object.__new__(Job)
        kept.__dict__.update(self.__dict__)
        kept.lefts, kept.rights, kept.whole = len(self.lefts), len(self.rights), None
        return kept

    def scratch(self):
        made = [pltpu.VMEM(x.shape, jnp.float32) for x in self.lefts + self.rights]
        for shape in self.splits:
            made += [pltpu.VMEM(shape, jnp.bfloat16)] * 2
        made += [pltpu.VMEM(shape, jnp.float32) for shape in self.outs]
        made += [pltpu.SemaphoreType.DMA((len(self.lefts) + len(self.rights),))]
        made += [pltpu.SemaphoreType.DMA((len(self.outs), self.extent // self.tile))]
        return made

    def bytes(self):
        shapes = [x.shape for x in self.lefts + self.rights] + self.splits + self.outs
        return sum(padded(shape, 4) for shape in shapes)


def limit(jobs, *shapes):
    return (8 << 20) + sum(job.bytes() for job in jobs) + sum(padded(shape, 4) for shape in shapes)


class Work:
    def __init__(self, plan, refs, firsts):
        refs = list(refs)

        def take(count):
            taken = refs[:count]
            del refs[:count]
            return taken

        sources = [take(job.lefts + job.rights) for job in plan]
        self.first = take(firsts)
        if plan and plan[0].joined:
            [together], start, sinks = take(1), 0, []
            for job in plan:
                rows = job.outs[0][0]
                sinks.append([together.at[pl.ds(start, rows)]])
                start += rows
        else:
            sinks = [take(len(job.outs)) for job in plan]
        self.jobs = []
        for job, source, sink in zip(plan, sources, sinks):
            held = take(job.lefts + job.rights)
            split = [take(2) for _ in range(job.rights)]
            outs = take(len(job.outs))
            in_sem, out_sem = take(2)
            self.jobs.append((job, source, sink, held, split, outs, in_sem, out_sem))
        self.rest = refs
        self.units = sum(job.units for job in plan)

    @staticmethod
    def operands(jobs):
        return [x for job in jobs for x in job.lefts + job.whole]

    @staticmethod
    def outputs(jobs):
        shapes = [shape for job in jobs for shape in job.outs]
        if jobs and jobs[0].joined:
            shapes = [(sum(shape[0] for shape in shapes), shapes[0][1])]
        return [jax.ShapeDtypeStruct(shape, jnp.float32) for shape in shapes]

    @staticmethod
    def scratch(jobs):
        return [x for job in jobs for x in job.scratch()]

    def loads(self):
        return [
            pltpu.make_async_copy(source[k].at[:, : held[k].shape[1]], held[k], in_sem.at[k])
            for _, source, _, held, _, _, in_sem, _ in self.jobs
            for k in range(len(source))
        ]

    def load(self):
        for copy in self.loads():
            copy.start()

    def ready(self):
        for copy in self.loads():
            copy.wait()

    def share(self, steps, step):
        if not self.jobs:
            return

        def unit(index, carry):
            base = 0
            for entry in self.jobs:
                job = entry[0]
                for k in range(job.rights):
                    self.when(index, base + k * job.chunks, job.chunks, functools.partial(self.split, entry, k))
                self.when(
                    index, base + job.prepare, job.units - job.prepare, functools.partial(self.tile, entry)
                )
                base += job.units
            return carry

        lax.fori_loop(step * self.units // steps, (step + 1) * self.units // steps, unit, 0)

    def when(self, index, start, count, act):
        @pl.when((index >= start) & (index < start + count))
        def _():
            act(index - start)

    def split(self, entry, k, chunk):
        job, held, split = entry[0], entry[3], entry[4]
        rows = pl.ds(pl.multiple_of(chunk * job.chunk, job.chunk), job.chunk)
        value = held[job.lefts + k][rows, :]
        where = (slice(None), rows) if job.form == "tn" else (rows, slice(None))
        split[k][0][where], split[k][1][where] = halves(value.T if job.form == "tn" else value)

    def tile(self, entry, index):
        job, _, sink, held, split, outs, _, out_sem = entry
        rows = pl.ds(pl.multiple_of(index * job.tile, job.tile), job.tile)
        numbers = (((1,), (1 if job.form == "nt" else 0,)), ((), ()))
        where = (slice(None), rows) if job.form == "tn" else (rows, slice(None))

        def product(own, other):
            pair = (other, own) if job.form == "tn" else (own, other)
            return lax.dot_general(*pair, numbers, preferred_element_type=jnp.float32)

        total = None
        for k in range(job.lefts):
            high, low = halves(held[k][where])
            for j in [k] if job.summed else range(job.rights):
                right_high, right_low = split[j][0][...], split[j][1][...]
                made = product(high, right_high) + product(high, right_low) + product(low, right_high)
                if job.summed:
                    total = made if total is None else total + made
                else:
                    outs[j][where] = made
        if job.summed:
            outs[0][where] = total
        for j, out in enumerate(outs):
            pltpu.make_async_copy(out.at[where], sink[j].at[where], out_sem.at[j, index]).start()

    def end(self):
        for job, _, sink, _, _, outs, _, out_sem in self.jobs:
            for j, out in enumerate(outs):
                for index in range(job.extent // job.tile):
                    rows = pl.ds(index * job.tile, job.tile)
                    where = (slice(None), rows) if job.form == "tn" else (rows, slice(None))
                    pltpu.make_async_copy(out.at[where], sink[j].at[where], out_sem.at[j, index]).wait()


class Ring:
    def __init__(self, n, cuts, x_ref, o_ref, sems):
        self.n, self.cuts, self.x, self.o = n, cuts, x_ref, o_ref
        self.own_sem, self.send_sem, self.recv_sem = sems
        self.me, self.at = ring_places(n)
        self.sides = ({"heads": self.at(1)}, {"heads": self.at(-1)})
        self.rows = x_ref.shape[0]
        self.piece = self.rows // 2 // cuts
        self.parts = [(cut, way) for cut in range(cuts) for way in (0, 1)]

    def copy(self, step, cut, way, first=False):
        off = way * (self.rows // 2) + cut * self.piece
        origin = self.at(-step) if way == 0 else self.at(step)
        dst = self.o.at[pl.ds(pl.multiple_of(origin * self.rows + off, 8), self.piece)]
        src = self.x.at[pl.ds(off, self.piece)] if first else dst
        sems = self.send_sem.at[way, step, cut], self.recv_sem.at[way, step, cut]
        return remote(src, dst, *sems, self.sides[way])

    def own(self):
        here = self.o.at[pl.ds(pl.multiple_of(self.me * self.rows, 8), self.rows)]
        return pltpu.make_async_copy(self.x, here, self.own_sem)

    def begin(self):
        self.own().start()
        for part in self.parts:
            self.copy(0, *part, first=True).start()

    def step(self, step):
        for part in self.parts:
            self.copy(step - 1, *part).wait_recv()
            self.copy(step, *part).start()

    def end(self):
        for part in self.parts:
            self.copy(self.n - 2, *part).wait_recv()

        def sent(step, carry):
            for part in self.parts:
                self.copy(step, *part).wait_send()
            return carry

        lax.fori_loop(0, self.n - 1, sent, 0)
        self.own().wait()

    def run(self, work=None):
        def body(step, carry):
            if work is not None:
                work(step - 1)

            @pl.when(step < self.n - 1)
            def _():
                self.step(step)

            return carry

        lax.fori_loop(1, self.n, body, 0)

    @staticmethod
    def scratch(n, cuts):
        return [
            pltpu.SemaphoreType.DMA,
            pltpu.SemaphoreType.DMA((2, n - 1, cuts)),
            pltpu.SemaphoreType.DMA((2, n - 1, cuts)),
        ]


class Spread:
    def __init__(self, dp, x_ref, o_ref, sems, pieces=1):
        self.x, self.o, self.ny, self.pieces = x_ref, o_ref, dp // 2, pieces
        self.own_sem, self.y_send, self.y_recv, self.core_send, self.core_recv = sems
        me = lax.axis_index("dp")
        self.y, self.core = me // 2, me % 2
        self.me = me
        self.mate = {"dp": self.y * 2 + 1 - self.core}
        self.next = {"dp": lax.rem(self.y + 1, self.ny) * 2 + self.core}
        self.rows = x_ref.shape[0]

    def block(self, owner, piece):
        size = self.rows // self.pieces
        return self.o.at[pl.ds(pl.multiple_of(owner * self.rows + piece * size, 8), size)]

    def begin(self):
        mine = self.o.at[pl.ds(pl.multiple_of(self.me * self.rows, 8), self.rows)]
        self.own = pltpu.make_async_copy(self.x, mine, self.own_sem)
        self.own.start()
        self.y_copies, self.core_copies = {}, {}
        for piece in range(self.pieces):
            size = self.rows // self.pieces
            src, dst = self.x.at[pl.ds(piece * size, size)], self.block(self.me, piece)
            self.send(self.y_copies, src, dst, self.y_send, self.y_recv, 0, piece, self.next)
            self.send(self.core_copies, src, dst, self.core_send, self.core_recv, 0, piece, self.mate)

    def send(self, copies, src, dst, send, recv, k, piece, name):
        copies[k, piece] = push(src, dst, send.at[k, piece], recv.at[k, piece], name)

    def end(self):
        for k in range(1, self.ny):
            owner = lax.rem(self.y - k + self.ny, self.ny) * 2 + self.core
            for piece in range(self.pieces):
                self.y_copies[k - 1, piece].wait_recv()
                held = self.block(owner, piece)
                if k < self.ny - 1:
                    self.send(self.y_copies, held, held, self.y_send, self.y_recv, k, piece, self.next)
                self.send(self.core_copies, held, held, self.core_send, self.core_recv, k, piece, self.mate)
        for copy in self.core_copies.values():
            copy.wait_recv()
        for copy in [*self.y_copies.values(), *self.core_copies.values()]:
            copy.wait_send()
        self.own.wait()

    @staticmethod
    def scratch(dp, pieces=1):
        ny = dp // 2
        return [
            pltpu.SemaphoreType.DMA,
            pltpu.SemaphoreType.DMA((ny - 1, pieces)),
            pltpu.SemaphoreType.DMA((ny - 1, pieces)),
            pltpu.SemaphoreType.DMA((ny, pieces)),
            pltpu.SemaphoreType.DMA((ny, pieces)),
        ]


class Swap:
    def __init__(self, dp, out, x_ref, o_ref, sems):
        self.dp, self.out, self.x, self.o = dp, out, x_ref, o_ref
        self.own_sem, self.send_sem, self.recv_sem = sems
        self.me = lax.axis_index("dp")

    def part(self, ref, index, by_columns):
        if by_columns:
            size = ref.shape[1] // self.dp
            return ref.at[:, pl.ds(pl.multiple_of(index * size, size), size)]
        size = ref.shape[0] // self.dp
        return ref.at[pl.ds(pl.multiple_of(index * size, size), size)]

    def begin(self):
        mine = self.part(self.o, self.me, not self.out)
        self.own = pltpu.make_async_copy(self.part(self.x, self.me, self.out), mine, self.own_sem)
        self.own.start()
        self.copies = [
            push(self.part(self.x, other, self.out), mine, self.send_sem.at[k], self.recv_sem.at[k], {"dp": other})
            for k, other in enumerate(others("dp"))
        ]

    def end(self):
        for copy in self.copies:
            copy.wait_recv()
        for copy in self.copies:
            copy.wait_send()
        self.own.wait()

    @staticmethod
    def scratch(dp):
        return [
            pltpu.SemaphoreType.DMA,
            pltpu.SemaphoreType.DMA((dp - 1,)),
            pltpu.SemaphoreType.DMA((dp - 1,)),
        ]


def cost(micros):
    return pl.CostEstimate(flops=0, bytes_accessed=int(micros * 3.0e6), transcendentals=0)


def spaces(count, space=pl.ANY):
    return [pl.BlockSpec(memory_space=space)] * count


def gather_body(n, cuts, plan, x_ref, *refs):
    work = Work(plan, refs, 1)
    ring = Ring(n, cuts, x_ref, work.first[0], work.rest)
    work.load()
    greet(ring.sides)
    ring.begin()
    work.ready()
    ring.run(functools.partial(work.share, n - 1))
    ring.end()
    work.end()


def ring_gather(x, n, number, jobs=(), cuts=2):
    rows, columns = x.shape
    cuts = min(cuts, rows // 16)
    plan = [job.bare() for job in jobs]
    result = pl.pallas_call(
        functools.partial(gather_body, n, cuts, plan),
        out_shape=(jax.ShapeDtypeStruct((n * rows, columns), x.dtype), *Work.outputs(jobs)),
        in_specs=spaces(1, pltpu.VMEM) + spaces(len(Work.operands(jobs))),
        out_specs=tuple(spaces(1 + len(Work.outputs(jobs)))),
        scratch_shapes=Work.scratch(jobs) + Ring.scratch(n, cuts),
        compiler_params=pltpu.CompilerParams(
            collective_id=number, has_side_effects=True, vmem_limit_bytes=ATTEND_LIMIT if jobs else limit(jobs, x.shape)
        ),
        cost_estimate=cost(75.0 * columns / 2048),
        name=f"ring_gather_{number}",
    )(x, *Work.operands(jobs))
    return result if jobs else result[0]


def opening_body(n, dp, cuts, grad, down, pair, hidden, grad_all, wide_down, wide_pair, hidden_turn, *sems):
    ring = Ring(n, cuts, grad, grad_all, sems[:3])
    parts = [
        Spread(dp, down, wide_down, sems[3:8]),
        Spread(dp, pair, wide_pair, sems[8:13]),
        Swap(dp, True, hidden, hidden_turn, sems[13:16]),
    ]
    greet(list(ring.sides) + [{"dp": other} for other in others("dp")])
    for part in parts:
        part.begin()
    ring.begin()
    ring.run()
    for part in parts:
        part.end()
    ring.end()


def opening(grad, down, pair, hidden, n, dp, number, cuts=2):
    def full(x, times):
        return jax.ShapeDtypeStruct((x.shape[0] * times, x.shape[1]), x.dtype)

    turned = jax.ShapeDtypeStruct((hidden.shape[0] * dp, hidden.shape[1] // dp), hidden.dtype)
    return pl.pallas_call(
        functools.partial(opening_body, n, dp, cuts),
        out_shape=(full(grad, n), full(down, dp), full(pair, dp), turned),
        in_specs=spaces(4, pltpu.VMEM),
        out_specs=tuple(spaces(4)),
        scratch_shapes=Ring.scratch(n, cuts) + Spread.scratch(dp) * 2 + Swap.scratch(dp),
        compiler_params=pltpu.CompilerParams(collective_id=number, has_side_effects=True),
        cost_estimate=cost(80.0),
        name="opening",
    )(grad, down, pair, hidden)


def spread_body(dp, x_ref, o_ref, *sems):
    part = Spread(dp, x_ref, o_ref, sems, 4)
    greet([{"dp": other} for other in others("dp")])
    part.begin()
    part.end()


def dp_gather(x, dp, number):
    return pl.pallas_call(
        functools.partial(spread_body, dp),
        out_shape=jax.ShapeDtypeStruct((x.shape[0] * dp, x.shape[1]), x.dtype),
        in_specs=spaces(1, pltpu.VMEM),
        out_specs=pl.BlockSpec(memory_space=pl.ANY),
        scratch_shapes=Spread.scratch(dp, 4),
        compiler_params=pltpu.CompilerParams(collective_id=number, has_side_effects=True),
        cost_estimate=cost(20.0),
        name=f"dp_gather_{number}",
    )(x)


class RingSum:
    def __init__(self, n, cuts, x_ref, o_ref, held, sems):
        self.n, self.cuts, self.x, self.o, self.held = n, cuts, x_ref, o_ref, held
        self.send_sem, self.recv_sem = sems
        self.me, self.at = ring_places(n)
        self.sides = ({"heads": self.at(1)}, {"heads": self.at(-1)})
        self.rows = x_ref.shape[0] // n
        self.half = self.rows // 2
        self.piece = self.half // cuts
        self.parts = [(cut, way) for cut in range(cuts) for way in (0, 1)]

    def mine(self, owner, cut, way):
        start = owner * self.rows + way * self.half + cut * self.piece
        return self.x.at[pl.ds(pl.multiple_of(start, 8), self.piece)]

    def slot(self, step, cut, way):
        return self.held.at[way, step, pl.ds(cut * self.piece, self.piece)]

    def owner(self, step, way):
        return self.at(-1 - step) if way == 0 else self.at(1 + step)

    def copy(self, step, cut, way, first=False):
        src = self.mine(self.owner(step, way), cut, way) if first else self.slot(step - 1, cut, way)
        sems = self.send_sem.at[way, step, cut], self.recv_sem.at[way, step, cut]
        return remote(src, self.slot(step, cut, way), *sems, self.sides[way])

    def begin(self):
        for part in self.parts:
            self.copy(0, *part, first=True).start()

    def step(self, step):
        for cut, way in self.parts:
            self.arrived(step - 1, cut, way)
            total = self.slot(step - 1, cut, way)
            total[...] += self.mine(self.owner(step, way), cut, way)[...]
            self.copy(step, cut, way).start()

    def arrived(self, step, cut, way):
        slot = self.slot(step, cut, way)
        sems = self.send_sem.at[way, step, cut], self.recv_sem.at[way, step, cut]
        remote(slot, slot, *sems, self.sides[way]).wait_recv()

    def end(self):
        for cut, way in self.parts:
            self.arrived(self.n - 2, cut, way)
            self.o[pl.ds(way * self.half + cut * self.piece, self.piece)] = (
                self.mine(self.me, cut, way)[...] + self.slot(self.n - 2, cut, way)[...]
            )

        def sent(step, carry):
            for cut, way in self.parts:
                slot = self.slot(step, cut, way)
                sems = self.send_sem.at[way, step, cut], self.recv_sem.at[way, step, cut]
                remote(slot, slot, *sems, self.sides[way]).wait_send()
            return carry

        lax.fori_loop(0, self.n - 1, sent, 0)

    run = Ring.run

    @staticmethod
    def scratch(n, cuts, rows, columns):
        return [
            pltpu.VMEM((2, n - 1, rows // 2, columns), jnp.float32),
            pltpu.SemaphoreType.DMA((2, n - 1, cuts)),
            pltpu.SemaphoreType.DMA((2, n - 1, cuts)),
        ]


def scatter_body(n, cuts, plan, x_ref, *refs):
    work = Work(plan, refs, 1)
    ring = RingSum(n, cuts, x_ref, work.first[0], work.rest[0], work.rest[1:])
    work.load()
    greet(ring.sides)
    ring.begin()
    work.ready()
    ring.run(functools.partial(work.share, n - 1))
    ring.end()
    work.end()


def ring_scatter(x, n, number, jobs=(), cuts=4):
    rows, columns = x.shape[0] // n, x.shape[1]
    cuts = min(cuts, rows // 16)
    plan = [job.bare() for job in jobs]
    result = pl.pallas_call(
        functools.partial(scatter_body, n, cuts, plan),
        out_shape=(jax.ShapeDtypeStruct((rows, columns), x.dtype), *Work.outputs(jobs)),
        in_specs=spaces(1, pltpu.VMEM) + spaces(len(Work.operands(jobs))),
        out_specs=tuple(spaces(1, pltpu.VMEM) + spaces(len(Work.outputs(jobs)))),
        scratch_shapes=Work.scratch(jobs) + RingSum.scratch(n, cuts, rows, columns),
        compiler_params=pltpu.CompilerParams(
            collective_id=number, has_side_effects=True, vmem_limit_bytes=limit(jobs, x.shape, x.shape, (rows, columns))
        ),
        cost_estimate=cost(75.0 * columns / 2048),
        name=f"ring_scatter_{number}",
    )(x, *Work.operands(jobs))
    return result if jobs else result[0]


def turn_body(n, dp, cuts, x_ref, hidden, o_ref, hidden_turn, held, *sems):
    ring = RingSum(n, cuts, x_ref, o_ref, held, sems[:2])
    swap = Swap(dp, False, hidden, hidden_turn, sems[2:])
    greet(list(ring.sides) + [{"dp": other} for other in others("dp")])
    swap.begin()
    ring.begin()
    ring.run()
    swap.end()
    ring.end()


def scatter_and_turn(x, hidden, n, dp, number, cuts=2):
    rows, columns = x.shape[0] // n, x.shape[1]
    cuts = min(cuts, rows // 16)
    return pl.pallas_call(
        functools.partial(turn_body, n, dp, cuts),
        out_shape=(
            jax.ShapeDtypeStruct((rows, columns), x.dtype),
            jax.ShapeDtypeStruct((hidden.shape[0] // dp, hidden.shape[1] * dp), x.dtype),
        ),
        in_specs=spaces(2, pltpu.VMEM),
        out_specs=(pl.BlockSpec(memory_space=pltpu.VMEM), pl.BlockSpec(memory_space=pl.ANY)),
        scratch_shapes=RingSum.scratch(n, cuts, rows, columns) + Swap.scratch(dp),
        compiler_params=pltpu.CompilerParams(
            collective_id=number, has_side_effects=True, vmem_limit_bytes=40 << 20
        ),
        cost_estimate=cost(35.0),
        name="scatter_and_turn",
    )(x, hidden)


class Total:
    def __init__(self, axis, x_ref, held, sems):
        self.x, self.held = x_ref, held
        self.send_sem, self.recv_sem = sems
        self.names = [{axis: other} for other in others(axis)]
        self.count = lax.axis_size(axis)

    def begin(self):
        self.copies = [
            push(self.x, self.held.at[k], self.send_sem.at[k], self.recv_sem.at[k], name)
            for k, name in enumerate(self.names)
        ]

    def end(self):
        for copy in self.copies:
            copy.wait_recv()
        for copy in self.copies:
            copy.wait_send()

    @staticmethod
    def scratch(count, shape):
        return [
            pltpu.VMEM((count - 1,) + shape, jnp.float32),
            pltpu.SemaphoreType.DMA((count - 1,)),
            pltpu.SemaphoreType.DMA((count - 1,)),
        ]


def in_order(axis, own, held):
    count = lax.axis_size(axis)
    me = lax.axis_index(axis)
    total = None
    for device in range(count):
        term = jnp.where(me == device, own, jnp.zeros_like(own))
        for k in range(1, count):
            term = term + jnp.where(lax.rem(me - k + count, count) == device, held[k - 1], jnp.zeros_like(own))
        total = term if total is None else total + term
    return total


def sum_body(x_ref, o_ref, middle, held_heads, hs, hr, held_dp, ds, dr):
    first = Total("heads", x_ref, held_heads, (hs, hr))
    second = Total("dp", middle, held_dp, (ds, dr))
    greet(first.names + second.names)
    first.begin()
    first.end()
    middle[...] = in_order("heads", x_ref[...], held_heads)
    second.begin()
    second.end()
    o_ref[...] = in_order("dp", middle[...], held_dp)


def gather_and_sum_body(n, cuts, x_ref, gains, o_ref, total, *refs):
    ring = Ring(n, cuts, x_ref, o_ref, refs[:3])
    middle, held_heads, hs, hr, held_dp, ds, dr = refs[3:]
    first = Total("heads", gains, held_heads, (hs, hr))
    second = Total("dp", middle, held_dp, (ds, dr))
    greet(first.names + second.names)
    first.begin()
    ring.begin()
    first.end()
    middle[...] = in_order("heads", gains[...], held_heads)
    second.begin()
    ring.run()
    second.end()
    total[...] = in_order("dp", middle[...], held_dp)
    ring.end()


def gather_and_sum(x, gains, n, dp, number, cuts=2):
    rows, columns = x.shape
    cuts = min(cuts, rows // 16)
    return pl.pallas_call(
        functools.partial(gather_and_sum_body, n, cuts),
        out_shape=(
            jax.ShapeDtypeStruct((n * rows, columns), x.dtype),
            jax.ShapeDtypeStruct(gains.shape, gains.dtype),
        ),
        in_specs=spaces(2, pltpu.VMEM),
        out_specs=(pl.BlockSpec(memory_space=pl.ANY), pl.BlockSpec(memory_space=pltpu.VMEM)),
        scratch_shapes=Ring.scratch(n, cuts)
        + [pltpu.VMEM(gains.shape, gains.dtype)]
        + Total.scratch(n, gains.shape)
        + Total.scratch(dp, gains.shape),
        compiler_params=pltpu.CompilerParams(
            collective_id=number, has_side_effects=True, vmem_limit_bytes=16 << 20
        ),
        cost_estimate=cost(35.0),
        name="gather_and_sum",
    )(x, gains)


def sum_all(x, n, dp, number):
    return pl.pallas_call(
        sum_body,
        out_shape=jax.ShapeDtypeStruct(x.shape, x.dtype),
        in_specs=spaces(1, pltpu.VMEM),
        out_specs=pl.BlockSpec(memory_space=pltpu.VMEM),
        scratch_shapes=[pltpu.VMEM(x.shape, x.dtype)] + Total.scratch(n, x.shape) + Total.scratch(dp, x.shape),
        compiler_params=pltpu.CompilerParams(collective_id=number, has_side_effects=True),
        cost_estimate=cost(8.0),
        name=f"sum_all_{number}",
    )(x)


NT = (((1,), (1,)), ((), ()))
NN = (((1,), (0,)), ((), ()))


def thrice(left, right, numbers):
    terms = [(left[0], right[0]), (left[0], right[1]), (left[1], right[0])]
    made = [lax.dot_general(*term, numbers, preferred_element_type=jnp.float32) for term in terms]
    return made[0] + (made[1] + made[2])


def turned(front, back, cosine, sines):
    return front * cosine - back * sines, back * cosine + front * sines


def keep_halves(value, pair, where):
    pair[0][where], pair[1][where] = halves(value)


def allowed_block(start, rows, reach, seg_rows, seg_columns):
    row = start + lax.broadcasted_iota(jnp.int32, (rows, reach), 0)
    column = lax.broadcasted_iota(jnp.int32, (rows, reach), 1)
    return (seg_rows[start : start + rows, :] == seg_columns[:, :reach]) & (column <= row)


def attend_body(latent_dim, rows, raw, packed, cosine, sines, seg_rows, seg_columns, mixed, query, lse, *split):
    total, width = raw.shape
    dim = (packed.shape[1] - latent_dim) // 2
    half = dim // 2
    scale = dim ** (-0.5)
    key, value = split[:2], split[2:]
    keep_halves(packed[:, latent_dim : latent_dim + dim], key, (slice(None), slice(None)))
    keep_halves(packed[:, latent_dim + dim :], value, (slice(None), slice(None)))
    for start in range(0, total, rows):
        here = slice(start, start + rows)
        reach = start + rows
        allowed = allowed_block(start, rows, reach, seg_rows, seg_columns)
        for head in range(width // dim):
            at = head * dim
            front, back = turned(
                raw[here, at : at + half], raw[here, at + half : at + dim], cosine[here, :], sines[here, :]
            )
            query[here, at : at + half] = front
            query[here, at + half : at + dim] = back
            own = halves(query[here, at : at + dim])
            scores = thrice(own, [ref[:reach, :] for ref in key], NT) * scale
            scores = jnp.where(allowed, scores, -1e30)
            top = jnp.max(scores, axis=1, keepdims=True)
            expo = jnp.exp(scores - top)
            denom = jnp.sum(expo, axis=1, keepdims=True)
            made = thrice(halves(expo), [ref[:reach, :] for ref in value], NN)
            mixed[here, at : at + dim] = made / denom
            lse[here, head * 128 : head * 128 + 128] = jnp.broadcast_to(top + jnp.log(denom), (rows, 128))


def attend(raw, packed, cosine, sines, seg_rows, seg_columns, latent_dim):
    total, width = raw.shape
    dim = (packed.shape[1] - latent_dim) // 2
    shape = jax.ShapeDtypeStruct
    return pl.pallas_call(
        functools.partial(attend_body, latent_dim, 256),
        out_shape=(
            shape(raw.shape, jnp.float32),
            shape(raw.shape, jnp.float32),
            shape((total, width // dim * 128), jnp.float32),
        ),
        in_specs=spaces(6, pltpu.VMEM),
        out_specs=tuple(spaces(3, pltpu.VMEM)),
        scratch_shapes=[pltpu.VMEM((total, dim), jnp.bfloat16)] * 4,
        compiler_params=pltpu.CompilerParams(vmem_limit_bytes=ATTEND_LIMIT),
        cost_estimate=cost(14.0),
        name="attend",
    )(raw, packed, cosine, sines, seg_rows, seg_columns)


def attend_back_body(
    latent_dim, rows, query, packed, cosine, sines, seg_rows, seg_columns, lse, mixed, d_mixed, up, d_raw, out, *split
):
    total, width = query.shape
    dim = (packed.shape[1] - latent_dim) // 2
    half = dim // 2
    scale = dim ** (-0.5)
    key, value, weight, made = split[:2], split[2:4], split[4:6], split[6:]
    every = (slice(None), slice(None))
    keep_halves(packed[:, latent_dim : latent_dim + dim], key, every)
    keep_halves(packed[:, latent_dim + dim :], value, every)
    keep_halves(up[...], weight, every)
    out[:, latent_dim:] = jnp.zeros((total, 2 * dim), jnp.float32)
    for start in range(0, total, rows):
        here = slice(start, start + rows)
        reach = start + rows
        allowed = allowed_block(start, rows, reach, seg_rows, seg_columns)
        for head in range(width // dim):
            at = head * dim
            own = halves(query[here, at : at + dim])
            upstream = d_mixed[here, at : at + dim]
            grad = halves(upstream)
            scores = thrice(own, [ref[:reach, :] for ref in key], NT) * scale
            scores = jnp.where(allowed, scores, -1e30)
            probs = jnp.exp(scores - lse[here, head * 128 : head * 128 + 1])
            d_probs = thrice(grad, [ref[:reach, :] for ref in value], NT)
            delta = jnp.sum(upstream * mixed[here, at : at + dim], axis=1, keepdims=True)
            d_scores = probs * (d_probs - delta) * scale
            out[:reach, latent_dim + dim :] += thrice(halves(probs.T), grad, NN)
            out[:reach, latent_dim : latent_dim + dim] += thrice(halves(d_scores.T), own, NN)
            d_query = thrice(halves(d_scores), [ref[:reach, :] for ref in key], NN)
            front, back = turned(d_query[:, :half], d_query[:, half:], cosine[here, :], -sines[here, :])
            for piece, off in ((front, at), (back, at + half)):
                d_raw[here, off : off + half] = piece
                keep_halves(piece, made, (slice(None), slice(off, off + half)))
        out[here, :latent_dim] = thrice([ref[...] for ref in made], [ref[...] for ref in weight], NT)


def attend_back(query, packed, cosine, sines, seg_rows, seg_columns, lse, mixed, d_mixed, up, latent_dim):
    total, width = query.shape
    dim = (packed.shape[1] - latent_dim) // 2
    shape = jax.ShapeDtypeStruct
    rows = 256
    return pl.pallas_call(
        functools.partial(attend_back_body, latent_dim, rows),
        out_shape=(shape(query.shape, jnp.float32), shape(packed.shape, jnp.float32)),
        in_specs=spaces(10, pltpu.VMEM),
        out_specs=tuple(spaces(2, pltpu.VMEM)),
        scratch_shapes=[pltpu.VMEM((total, dim), jnp.bfloat16)] * 4
        + [pltpu.VMEM(up.shape, jnp.bfloat16)] * 2
        + [pltpu.VMEM((rows, width), jnp.bfloat16)] * 2,
        compiler_params=pltpu.CompilerParams(vmem_limit_bytes=ATTEND_LIMIT),
        cost_estimate=cost(30.0),
        name="attend_back",
    )(query, packed, cosine, sines, seg_rows, seg_columns, lse, mixed, d_mixed, up)


def rope_tables(position, head_dim):
    half_dim = head_dim // 2
    frequency = ROPE_BASE ** (-jnp.arange(half_dim, dtype=jnp.float32) / half_dim)
    angles = position.astype(jnp.float32)[:, None] * frequency[None, :]
    return jnp.cos(angles), jnp.sin(angles)


ATTEND_LIMIT = 58 << 20


def matmul_high(left, right):
    return jnp.dot(left, right, precision=HIGH, preferred_element_type=jnp.float32)


def layout(lengths_row, row_index):
    upto = jnp.arange(lengths_row.shape[0], dtype=jnp.int32)
    doc_ends = jnp.sum(jnp.where(upto[None, :] <= upto[:, None], lengths_row[None, :], 0), axis=1)
    doc_starts = doc_ends - lengths_row
    segment = jnp.sum((row_index[:, None] >= doc_ends[None, :]).astype(jnp.int32), axis=1)
    doc_ids = jnp.arange(doc_ends.shape[0], dtype=jnp.int32)
    start_of = jnp.sum(
        jnp.where(segment[:, None] == doc_ids[None, :], doc_starts[None, :], 0), axis=1
    )
    return (segment, row_index - start_of)


def rotate(vector, position, sign):
    half_dim = vector.shape[-1] // 2
    frequency = ROPE_BASE ** (-jnp.arange(half_dim, dtype=jnp.float32) / half_dim)
    angles = position.astype(jnp.float32)[:, None] * frequency[None, :]
    angles = angles.reshape((angles.shape[0],) + (1,) * (vector.ndim - 2) + (half_dim,))
    cosine = jnp.cos(angles)
    sines = sign * jnp.sin(angles)
    front = vector[..., :half_dim]
    back_half = vector[..., half_dim:]
    return jnp.concatenate(
        [front * cosine - back_half * sines, back_half * cosine + front * sines], axis=-1
    )


def norm_back(upstream, normed, inverse, gain):
    scaled = upstream * gain
    return (
        inverse * (scaled - normed * jnp.mean(scaled * normed, axis=1, keepdims=True)),
        jnp.sum(upstream * normed, axis=0),
    )


def owned(part, axis):
    return lax.psum_scatter(part, "dp", scatter_dimension=axis, tiled=True)


def moments(value, grad, first, second):
    first_new = BETA_ONE * first + (1.0 - BETA_ONE) * grad
    second_new = BETA_TWO * second + (1.0 - BETA_TWO) * grad * grad
    update = (
        first_new
        / (1.0 - BETA_ONE**STEP_COUNT)
        / (jnp.sqrt(second_new / (1.0 - BETA_TWO**STEP_COUNT)) + ADAM_EPS)
        + DECAY * value
    )
    return (first_new, second_new, update)


def on_device(
    block_input,
    output_grad,
    lengths,
    norm_gains,
    norm_gains_first,
    norm_gains_second,
    query_down,
    query_down_first,
    query_down_second,
    key_value,
    key_value_first,
    key_value_second,
    query_up,
    query_up_first,
    query_up_second,
    head_merge,
    head_merge_first,
    head_merge_second,
    gate_weight,
    gate_weight_first,
    gate_weight_second,
    up_weight,
    up_weight_first,
    up_weight_second,
    down_weight,
    down_weight_first,
    down_weight_second,
):
    tok_rows = block_input.shape[0]
    model_dim = block_input.shape[1]
    latent_dim = query_down.shape[1]
    head_dim = key_value.shape[1] // 2
    heads_count = lax.axis_size("heads")
    dp_count = lax.axis_size("dp")
    group_rows = tok_rows * heads_count
    group_index = jnp.arange(group_rows, dtype=jnp.int32)
    segment, position = layout(lengths[0], group_index)
    local_position = lax.dynamic_slice_in_dim(
        position, lax.axis_index("heads") * tok_rows, tok_rows
    )
    gain_attn = norm_gains[:model_dim]
    gain_query = norm_gains[model_dim : model_dim + latent_dim]
    gain_ffn = norm_gains[model_dim + latent_dim :]
    inv_one = lax.rsqrt(jnp.mean(block_input * block_input, axis=1, keepdims=True) + EPS_NORM)
    normed_one = block_input * inv_one
    hidden_one = normed_one * gain_attn
    grad_all, wide_down, wide_pair, hidden_turn = opening(
        output_grad, query_down, key_value, hidden_one, heads_count, dp_count, 5
    )
    query_up_in, head_merge_in, gate_in, upper_in, lower_in, grad_all = lax.optimization_barrier(
        (query_up, head_merge, gate_weight, up_weight, down_weight, grad_all)
    )
    wide_up = lax.all_gather(query_up_in, "dp", axis=0, tiled=True)
    wide_merge = lax.all_gather(head_merge_in, "dp", axis=1, tiled=True)
    latent_raw = matmul_high(hidden_one, wide_down)
    inv_query = lax.rsqrt(jnp.mean(latent_raw * latent_raw, axis=1, keepdims=True) + EPS_NORM)
    latent_hat = latent_raw * inv_query
    latent = latent_hat * gain_query
    pair_local = matmul_high(hidden_one, wide_pair)
    key_local = rotate(pair_local[:, :head_dim], local_position, 1.0)
    value_local = pair_local[:, head_dim:]
    packed_all = ring_gather(
        jnp.concatenate([latent, key_local, value_local], axis=1), heads_count, 1
    )
    gate_in, upper_in, lower_in, packed_all = lax.optimization_barrier((gate_in, upper_in, lower_in, packed_all))
    turned_gate = lax.all_gather(gate_in.T, "dp", axis=1, tiled=True)
    turned_upper = lax.all_gather(upper_in.T, "dp", axis=1, tiled=True)
    wide_lower = lax.all_gather(lower_in, "dp", axis=1, tiled=True)
    latent_all = packed_all[:, :latent_dim]
    cosine, sines = rope_tables(position, head_dim)
    seg_rows, seg_columns = segment[:, None], segment[None, :]
    mixed_heads, query_rot, lse = attend(
        matmul_high(latent_all, wide_up), packed_all, cosine, sines, seg_rows, seg_columns, latent_dim
    )
    middle = block_input + ring_scatter(matmul_high(mixed_heads, wide_merge), heads_count, 2)
    inv_two = lax.rsqrt(jnp.mean(middle * middle, axis=1, keepdims=True) + EPS_NORM)
    normed_two = middle * inv_two
    hidden_two = normed_two * gain_ffn
    inside = group_rows <= 1024

    def job(*what):
        return [Job(*what)] if inside else []

    made = ring_gather(hidden_two, heads_count, 3, job("nt", [grad_all], [wide_lower], 256))
    hidden_all, d_activ = made if inside else (made, matmul_high(grad_all, wide_lower.T))
    gate_pre = matmul_high(hidden_all, turned_gate.T)
    up_pre = matmul_high(hidden_all, turned_upper.T)
    sig_gate = jax.nn.sigmoid(gate_pre)
    silu_gate = gate_pre * sig_gate
    activ = silu_gate * up_pre
    d_gate_pre = d_activ * up_pre * (sig_gate * (1.0 + gate_pre * (1.0 - sig_gate)))
    d_up_pre = d_activ * silu_gate
    part_output = matmul_high(activ, wide_lower)
    if inside:
        part_output, part_two = ring_scatter(
            part_output,
            heads_count,
            4,
            job("nn", [d_gate_pre, d_up_pre], [turned_gate, turned_upper], 128),
        )
        d_hidden_two, grad_both = ring_scatter(
            part_two,
            heads_count,
            6,
            job("tn", [hidden_all], [d_gate_pre], 256, True) + job("tn", [grad_all], [activ], 256, True),
        )
    else:
        part_output = ring_scatter(part_output, heads_count, 4)
        part_two = matmul_high(d_gate_pre, turned_gate) + matmul_high(d_up_pre, turned_upper)
        d_hidden_two = ring_scatter(part_two, heads_count, 6)
        grad_both = jnp.concatenate(
            [matmul_high(d_gate_pre.T, hidden_all), matmul_high(activ.T, grad_all)], axis=0
        )
    block_output = middle + part_output
    grad_both = owned(grad_both, 1)
    d_normed_mid, grad_gain_ffn = norm_back(d_hidden_two, normed_two, inv_two, gain_ffn)
    d_middle = output_grad + d_normed_mid
    made = ring_gather(d_middle, heads_count, 7, job("tn", [hidden_all], [d_up_pre], 256))
    middle_all, grad_upper = made if inside else (made, matmul_high(d_up_pre.T, hidden_all))
    d_mixed = matmul_high(middle_all, wide_merge.T)
    d_query_pre, packed_part = attend_back(
        query_rot,
        packed_all,
        cosine,
        sines,
        seg_rows,
        seg_columns,
        lse,
        mixed_heads,
        d_mixed,
        wide_up,
        latent_dim,
    )
    packed_part, grad_both, grad_upper = lax.optimization_barrier((packed_part, grad_both, grad_upper))
    grad_gate, grad_lower = jnp.split(grad_both, 2, axis=0)
    grad_upper = owned(grad_upper, 1)
    if inside:
        packed_grad, grad_merge, grad_up = ring_scatter(
            packed_part,
            heads_count,
            8,
            job("tn", [middle_all], [mixed_heads], 256) + job("tn", [d_query_pre], [(packed_all, jax.ShapeDtypeStruct(latent_all.shape, jnp.float32))], 256),
        )
    else:
        packed_grad = ring_scatter(packed_part, heads_count, 8)
        grad_merge = matmul_high(mixed_heads.T, middle_all)
        grad_up = matmul_high(latent_all.T, d_query_pre)
    packed_grad, grad_upper = lax.optimization_barrier((packed_grad, grad_upper))
    d_latent = packed_grad[:, :latent_dim]
    d_key_local = packed_grad[:, latent_dim : latent_dim + head_dim]
    d_value_local = packed_grad[:, latent_dim + head_dim :]
    d_pair = jnp.concatenate([rotate(d_key_local, local_position, -1.0), d_value_local], axis=1)
    d_latent_raw, grad_gain_query = norm_back(d_latent, latent_hat, inv_query, gain_query)
    raw = jnp.concatenate([d_latent_raw, d_pair], axis=1)
    raw_all = dp_gather(raw, dp_count, 11)
    raw_all, grad_merge, grad_up = lax.optimization_barrier((raw_all, grad_merge, grad_up))
    grad_up = owned(grad_up, 0)
    part_shared = matmul_high(hidden_turn.T, raw_all)
    d_hidden_turn = matmul_high(raw_all, jnp.concatenate([query_down, key_value], axis=1).T)
    shared_cut, d_hidden_one = scatter_and_turn(part_shared, d_hidden_turn, heads_count, dp_count, 9)
    d_normed_in, grad_gain_attn = norm_back(d_hidden_one, normed_one, inv_one, gain_attn)
    input_grad = d_middle + d_normed_in
    grad_gains = jnp.concatenate([grad_gain_attn, grad_gain_query, grad_gain_ffn])
    shared_cut, grad_merge, grad_up = lax.optimization_barrier((shared_cut, grad_merge, grad_up))
    grad_merge = owned(grad_merge, 1)
    shared, gains_total = gather_and_sum(
        shared_cut, grad_gains.reshape(-1, 128), heads_count, dp_count, 10
    )
    gains_total = gains_total.reshape(-1)
    values = (
        norm_gains,
        query_down,
        key_value,
        query_up,
        head_merge,
        gate_weight,
        up_weight,
        down_weight,
    )
    firsts = (
        norm_gains_first,
        query_down_first,
        key_value_first,
        query_up_first,
        head_merge_first,
        gate_weight_first,
        up_weight_first,
        down_weight_first,
    )
    seconds = (
        norm_gains_second,
        query_down_second,
        key_value_second,
        query_up_second,
        head_merge_second,
        gate_weight_second,
        up_weight_second,
        down_weight_second,
    )
    grads = (
        gains_total,
        shared[:, :latent_dim],
        shared[:, latent_dim:],
        grad_up,
        grad_merge,
        grad_gate.T,
        grad_upper.T,
        grad_lower,
    )
    stepped = [moments(values[slot], grads[slot], firsts[slot], seconds[slot]) for slot in range(8)]
    replica_share = [1.0, 1.0 / heads_count, 1.0 / heads_count, 1.0, 1.0, 1.0, 1.0, 1.0]
    square_rows = jnp.stack(
        [
            jnp.stack(
                [jnp.sum(values[slot] * values[slot]), jnp.sum(stepped[slot][2] * stepped[slot][2])]
            )
            * replica_share[slot]
            for slot in range(1, 8)
        ]
    )
    square_tile = jnp.zeros((8, 128), jnp.float32).at[:7, :2].set(square_rows)
    summed = sum_all(square_tile, heads_count, dp_count, 13)[:7, :2]
    gains_row = jnp.stack(
        [jnp.sum(norm_gains * norm_gains), jnp.sum(stepped[0][2] * stepped[0][2])]
    )
    norm_table = jnp.sqrt(jnp.concatenate([gains_row[None, :], summed], axis=0))
    new_values = [
        values[slot] - RATE * (norm_table[slot, 0] / norm_table[slot, 1]) * stepped[slot][2]
        for slot in range(8)
    ]
    return (
        block_output,
        input_grad,
        stepped[0][0],
        stepped[0][1],
        new_values[0],
        stepped[1][0],
        stepped[1][1],
        new_values[1],
        stepped[2][0],
        stepped[2][1],
        new_values[2],
        stepped[3][0],
        stepped[3][1],
        new_values[3],
        stepped[4][0],
        stepped[4][1],
        new_values[4],
        stepped[5][0],
        stepped[5][1],
        new_values[5],
        stepped[6][0],
        stepped[6][1],
        new_values[6],
        stepped[7][0],
        stepped[7][1],
        new_values[7],
        norm_table,
    )


def solution(mesh):
    placed = (
        P(("dp", "heads"), None),
        P(("dp", "heads"), None),
        P("dp", None),
        P(),
        P(),
        P(),
        P("dp", None),
        P("dp", None),
        P("dp", None),
        P("dp", None),
        P("dp", None),
        P("dp", None),
        P("dp", "heads"),
        P("dp", "heads"),
        P("dp", "heads"),
        P("heads", "dp"),
        P("heads", "dp"),
        P("heads", "dp"),
        P("dp", "heads"),
        P("dp", "heads"),
        P("dp", "heads"),
        P("dp", "heads"),
        P("dp", "heads"),
        P("dp", "heads"),
        P("heads", "dp"),
        P("heads", "dp"),
        P("heads", "dp"),
    )
    return jax.shard_map(
        on_device,
        mesh=mesh,
        in_specs=placed,
        out_specs=(
            P(("dp", "heads"), None),
            P(("dp", "heads"), None),
            P(),
            P(),
            P(),
            P("dp", None),
            P("dp", None),
            P("dp", None),
            P("dp", None),
            P("dp", None),
            P("dp", None),
            P("dp", "heads"),
            P("dp", "heads"),
            P("dp", "heads"),
            P("heads", "dp"),
            P("heads", "dp"),
            P("heads", "dp"),
            P("dp", "heads"),
            P("dp", "heads"),
            P("dp", "heads"),
            P("dp", "heads"),
            P("dp", "heads"),
            P("dp", "heads"),
            P("heads", "dp"),
            P("heads", "dp"),
            P("heads", "dp"),
            P(),
        ),
        check_vma=False,
    )
```

```python
import functools

import jax
import jax.numpy as jnp
from jax import lax
from jax.experimental import pallas as pl
from jax.experimental.pallas import tpu as pltpu
from jax.sharding import PartitionSpec as P

STEP_COUNT = 10


EPS_NORM = 1e-06
ROPE_BASE = 10000.0
BETA_ONE = 0.5
BETA_TWO = 0.6
ADAM_EPS = 1e-06
DECAY = 0.01
RATE = 0.5
HIGH = lax.Precision.HIGH
MESH = pl.DeviceIdType.MESH
RING_Z = 4


def head_at(spot, n):
    wide = n // RING_Z
    back = (spot + n - RING_Z) // n
    rest = jnp.maximum(spot - RING_Z, 0)
    row, step = rest // (wide - 1), rest % (wide - 1)
    odd = row % 2
    column = (1 - odd) * (1 + step) + odd * (wide - 1 - step)
    return (1 - back) * (spot * wide) + back * ((RING_Z - 1 - row) * wide + column)


def spot_of(head, n):
    wide = n // RING_Z
    row = RING_Z - 1 - head // wide
    column = head % wide
    odd = row % 2
    step = (1 - odd) * (column - 1) + odd * (wide - 1 - column)
    back = (column + wide - 1) // wide
    return (1 - back) * (head // wide) + back * (RING_Z + row * (wide - 1) + step)


def ring_places(n):
    me = lax.axis_index("heads")
    spot = spot_of(me, n)
    return me, lambda k: head_at(lax.rem(spot + k + 2 * n, n), n)


def others(axis):
    count = lax.axis_size(axis)
    me = lax.axis_index(axis)
    return [lax.rem(me + k, count) for k in range(1, count)]


def greet(names):
    bar = pltpu.get_barrier_semaphore()
    for name in names:
        pl.semaphore_signal(bar, inc=1, device_id=name, device_id_type=MESH)
    pl.semaphore_wait(bar, len(names))


def remote(src, dst, send, recv, name):
    return pltpu.make_async_remote_copy(
        src_ref=src, dst_ref=dst, send_sem=send, recv_sem=recv, device_id=name, device_id_type=MESH
    )


def push(*what):
    copy = remote(*what)
    copy.start()
    return copy


def halves(value):
    high = value.astype(jnp.bfloat16)
    return high, (value - high.astype(jnp.float32)).astype(jnp.bfloat16)


def padded(shape, size):
    return shape[0] * -(-shape[1] // 128) * 128 * size


class Job:
    def __init__(self, form, lefts, rights, tile, joined=False):
        self.joined = joined
        self.form, self.lefts, self.tile = form, lefts, tile
        self.whole = [x[0] if isinstance(x, tuple) else x for x in rights]
        rights = [x[1] if isinstance(x, tuple) else x for x in rights]
        self.rights = rights
        self.summed = len(lefts) > 1
        rows = rights[0].shape[0]
        self.chunk = next(c for c in (512, 352, 256, 128, 64, 32, 16) if rows % c == 0)
        if form == "tn":
            self.chunk = next(c for c in (256, 128) if rows % c == 0)
            self.extent = lefts[0].shape[1]
        else:
            self.extent = lefts[0].shape[0]
        self.chunks = rows // self.chunk
        self.prepare = self.chunks * len(rights)
        self.units = self.prepare + self.extent // tile
        width = {"nt": 0, "nn": 1, "tn": 1}[form]
        shapes = [
            (x.shape[1], self.extent) if form == "tn" else (self.extent, x.shape[width]) for x in rights
        ]
        self.outs = shapes[:1] if self.summed else shapes
        self.splits = [x.shape[::-1] if form == "tn" else x.shape for x in rights]

    def bare(self):
        kept = object.__new__(Job)
        kept.__dict__.update(self.__dict__)
        kept.lefts, kept.rights, kept.whole = len(self.lefts), len(self.rights), None
        return kept

    def scratch(self):
        made = [pltpu.VMEM(x.shape, jnp.float32) for x in self.lefts + self.rights]
        for shape in self.splits:
            made += [pltpu.VMEM(shape, jnp.bfloat16)] * 2
        made += [pltpu.VMEM(shape, jnp.float32) for shape in self.outs]
        made += [pltpu.SemaphoreType.DMA((len(self.lefts) + len(self.rights),))]
        made += [pltpu.SemaphoreType.DMA((len(self.outs), self.extent // self.tile))]
        return made

    def bytes(self):
        shapes = [x.shape for x in self.lefts + self.rights] + self.splits + self.outs
        return sum(padded(shape, 4) for shape in shapes)


def limit(jobs, *shapes):
    return (8 << 20) + sum(job.bytes() for job in jobs) + sum(padded(shape, 4) for shape in shapes)


class Work:
    def __init__(self, plan, refs, firsts):
        refs = list(refs)

        def take(count):
            taken = refs[:count]
            del refs[:count]
            return taken

        sources = [take(job.lefts + job.rights) for job in plan]
        self.first = take(firsts)
        if plan and plan[0].joined:
            [together], start, sinks = take(1), 0, []
            for job in plan:
                rows = job.outs[0][0]
                sinks.append([together.at[pl.ds(start, rows)]])
                start += rows
        else:
            sinks = [take(len(job.outs)) for job in plan]
        self.jobs = []
        for job, source, sink in zip(plan, sources, sinks):
            held = take(job.lefts + job.rights)
            split = [take(2) for _ in range(job.rights)]
            outs = take(len(job.outs))
            in_sem, out_sem = take(2)
            self.jobs.append((job, source, sink, held, split, outs, in_sem, out_sem))
        self.rest = refs
        self.units = sum(job.units for job in plan)

    @staticmethod
    def operands(jobs):
        return [x for job in jobs for x in job.lefts + job.whole]

    @staticmethod
    def outputs(jobs):
        shapes = [shape for job in jobs for shape in job.outs]
        if jobs and jobs[0].joined:
            shapes = [(sum(shape[0] for shape in shapes), shapes[0][1])]
        return [jax.ShapeDtypeStruct(shape, jnp.float32) for shape in shapes]

    @staticmethod
    def scratch(jobs):
        return [x for job in jobs for x in job.scratch()]

    def loads(self):
        return [
            pltpu.make_async_copy(source[k].at[:, : held[k].shape[1]], held[k], in_sem.at[k])
            for _, source, _, held, _, _, in_sem, _ in self.jobs
            for k in range(len(source))
        ]

    def load(self):
        for copy in self.loads():
            copy.start()

    def ready(self):
        for copy in self.loads():
            copy.wait()

    def share(self, steps, step):
        if not self.jobs:
            return

        def unit(index, carry):
            base = 0
            for entry in self.jobs:
                job = entry[0]
                for k in range(job.rights):
                    self.when(index, base + k * job.chunks, job.chunks, functools.partial(self.split, entry, k))
                self.when(
                    index, base + job.prepare, job.units - job.prepare, functools.partial(self.tile, entry)
                )
                base += job.units
            return carry

        lax.fori_loop(step * self.units // steps, (step + 1) * self.units // steps, unit, 0)

    def when(self, index, start, count, act):
        @pl.when((index >= start) & (index < start + count))
        def _():
            act(index - start)

    def split(self, entry, k, chunk):
        job, held, split = entry[0], entry[3], entry[4]
        rows = pl.ds(pl.multiple_of(chunk * job.chunk, job.chunk), job.chunk)
        value = held[job.lefts + k][rows, :]
        where = (slice(None), rows) if job.form == "tn" else (rows, slice(None))
        split[k][0][where], split[k][1][where] = halves(value.T if job.form == "tn" else value)

    def tile(self, entry, index):
        job, _, sink, held, split, outs, _, out_sem = entry
        rows = pl.ds(pl.multiple_of(index * job.tile, job.tile), job.tile)
        numbers = (((1,), (1 if job.form == "nt" else 0,)), ((), ()))
        where = (slice(None), rows) if job.form == "tn" else (rows, slice(None))

        def product(own, other):
            pair = (other, own) if job.form == "tn" else (own, other)
            return lax.dot_general(*pair, numbers, preferred_element_type=jnp.float32)

        total = None
        for k in range(job.lefts):
            high, low = halves(held[k][where])
            for j in [k] if job.summed else range(job.rights):
                right_high, right_low = split[j][0][...], split[j][1][...]
                made = product(high, right_high) + product(high, right_low) + product(low, right_high)
                if job.summed:
                    total = made if total is None else total + made
                else:
                    outs[j][where] = made
        if job.summed:
            outs[0][where] = total
        for j, out in enumerate(outs):
            pltpu.make_async_copy(out.at[where], sink[j].at[where], out_sem.at[j, index]).start()

    def end(self):
        for job, _, sink, _, _, outs, _, out_sem in self.jobs:
            for j, out in enumerate(outs):
                for index in range(job.extent // job.tile):
                    rows = pl.ds(index * job.tile, job.tile)
                    where = (slice(None), rows) if job.form == "tn" else (rows, slice(None))
                    pltpu.make_async_copy(out.at[where], sink[j].at[where], out_sem.at[j, index]).wait()


class Ring:
    def __init__(self, n, cuts, x_ref, o_ref, sems):
        self.n, self.cuts, self.x, self.o = n, cuts, x_ref, o_ref
        self.own_sem, self.send_sem, self.recv_sem = sems
        self.me, self.at = ring_places(n)
        self.sides = ({"heads": self.at(1)}, {"heads": self.at(-1)})
        self.rows = x_ref.shape[0]
        self.piece = self.rows // 2 // cuts
        self.parts = [(cut, way) for cut in range(cuts) for way in (0, 1)]

    def copy(self, step, cut, way, first=False):
        off = way * (self.rows // 2) + cut * self.piece
        origin = self.at(-step) if way == 0 else self.at(step)
        dst = self.o.at[pl.ds(pl.multiple_of(origin * self.rows + off, 8), self.piece)]
        src = self.x.at[pl.ds(off, self.piece)] if first else dst
        sems = self.send_sem.at[way, step, cut], self.recv_sem.at[way, step, cut]
        return remote(src, dst, *sems, self.sides[way])

    def own(self):
        here = self.o.at[pl.ds(pl.multiple_of(self.me * self.rows, 8), self.rows)]
        return pltpu.make_async_copy(self.x, here, self.own_sem)

    def begin(self):
        self.own().start()
        for part in self.parts:
            self.copy(0, *part, first=True).start()

    def step(self, step):
        for part in self.parts:
            self.copy(step - 1, *part).wait_recv()
            self.copy(step, *part).start()

    def received(self):
        for part in self.parts:
            self.copy(self.n - 2, *part).wait_recv()

    def end(self):
        self.received()
        self.sent()

    def sent(self):
        def sent(step, carry):
            for part in self.parts:
                self.copy(step, *part).wait_send()
            return carry

        lax.fori_loop(0, self.n - 1, sent, 0)
        self.own().wait()

    def run(self, work=None):
        def body(step, carry):
            if work is not None:
                work(step - 1)

            @pl.when(step < self.n - 1)
            def _():
                self.step(step)

            return carry

        lax.fori_loop(1, self.n, body, 0)

    @staticmethod
    def scratch(n, cuts):
        return [
            pltpu.SemaphoreType.DMA,
            pltpu.SemaphoreType.DMA((2, n - 1, cuts)),
            pltpu.SemaphoreType.DMA((2, n - 1, cuts)),
        ]


class Spread:
    def __init__(self, dp, x_ref, o_ref, sems, pieces=1):
        self.x, self.o, self.ny, self.pieces = x_ref, o_ref, dp // 2, pieces
        self.own_sem, self.y_send, self.y_recv, self.core_send, self.core_recv = sems
        me = lax.axis_index("dp")
        self.y, self.core = me // 2, me % 2
        self.me = me
        self.mate = {"dp": self.y * 2 + 1 - self.core}
        self.next = {"dp": lax.rem(self.y + 1, self.ny) * 2 + self.core}
        self.rows = x_ref.shape[0]

    def block(self, owner, piece):
        size = self.rows // self.pieces
        return self.o.at[pl.ds(pl.multiple_of(owner * self.rows + piece * size, 8), size)]

    def begin(self):
        mine = self.o.at[pl.ds(pl.multiple_of(self.me * self.rows, 8), self.rows)]
        self.own = pltpu.make_async_copy(self.x, mine, self.own_sem)
        self.own.start()
        self.y_copies, self.core_copies = {}, {}
        for piece in range(self.pieces):
            size = self.rows // self.pieces
            src, dst = self.x.at[pl.ds(piece * size, size)], self.block(self.me, piece)
            self.send(self.y_copies, src, dst, self.y_send, self.y_recv, 0, piece, self.next)
            self.send(self.core_copies, src, dst, self.core_send, self.core_recv, 0, piece, self.mate)

    def send(self, copies, src, dst, send, recv, k, piece, name):
        copies[k, piece] = push(src, dst, send.at[k, piece], recv.at[k, piece], name)

    def end(self):
        for k in range(1, self.ny):
            owner = lax.rem(self.y - k + self.ny, self.ny) * 2 + self.core
            for piece in range(self.pieces):
                self.y_copies[k - 1, piece].wait_recv()
                held = self.block(owner, piece)
                if k < self.ny - 1:
                    self.send(self.y_copies, held, held, self.y_send, self.y_recv, k, piece, self.next)
                self.send(self.core_copies, held, held, self.core_send, self.core_recv, k, piece, self.mate)
        for copy in self.core_copies.values():
            copy.wait_recv()
        for copy in [*self.y_copies.values(), *self.core_copies.values()]:
            copy.wait_send()
        self.own.wait()

    @staticmethod
    def scratch(dp, pieces=1):
        ny = dp // 2
        return [
            pltpu.SemaphoreType.DMA,
            pltpu.SemaphoreType.DMA((ny - 1, pieces)),
            pltpu.SemaphoreType.DMA((ny - 1, pieces)),
            pltpu.SemaphoreType.DMA((ny, pieces)),
            pltpu.SemaphoreType.DMA((ny, pieces)),
        ]


class Swap:
    def __init__(self, dp, out, x_ref, o_ref, sems):
        self.dp, self.out, self.x, self.o = dp, out, x_ref, o_ref
        self.own_sem, self.send_sem, self.recv_sem = sems
        self.me = lax.axis_index("dp")

    def part(self, ref, index, by_columns):
        if by_columns:
            size = ref.shape[1] // self.dp
            return ref.at[:, pl.ds(pl.multiple_of(index * size, size), size)]
        size = ref.shape[0] // self.dp
        return ref.at[pl.ds(pl.multiple_of(index * size, size), size)]

    def begin(self):
        mine = self.part(self.o, self.me, not self.out)
        self.own = pltpu.make_async_copy(self.part(self.x, self.me, self.out), mine, self.own_sem)
        self.own.start()
        self.copies = [
            push(self.part(self.x, other, self.out), mine, self.send_sem.at[k], self.recv_sem.at[k], {"dp": other})
            for k, other in enumerate(others("dp"))
        ]

    def end(self):
        for copy in self.copies:
            copy.wait_recv()
        for copy in self.copies:
            copy.wait_send()
        self.own.wait()

    @staticmethod
    def scratch(dp):
        return [
            pltpu.SemaphoreType.DMA,
            pltpu.SemaphoreType.DMA((dp - 1,)),
            pltpu.SemaphoreType.DMA((dp - 1,)),
        ]


def cost(micros):
    return pl.CostEstimate(flops=0, bytes_accessed=int(micros * 3.0e6), transcendentals=0)


def spaces(count, space=pl.ANY):
    return [pl.BlockSpec(memory_space=space)] * count


class Arrive:
    def __init__(self, ring, rights, refs):
        count = len(rights)
        self.ring, self.sources, self.sinks = ring, rights, refs[:count]
        self.buffer, self.stage = refs[count : count + 2]
        self.split = [refs[count + 2 + 2 * k : count + 4 + 2 * k] for k in range(count)]
        self.made = refs[count + 2 + 2 * count : count + 2 + 3 * count]
        self.load_sem, self.stage_sem, self.out_sem = refs[count + 2 + 3 * count :]

    def load(self, unit):
        height = self.buffer.shape[1]
        source = self.sources[unit // 4].at[pl.ds(unit % 4 * height, height)]
        return pltpu.make_async_copy(source, self.buffer.at[unit % 2], self.load_sem.at[unit % 2])

    def prepare(self):
        units = 4 * len(self.sources)
        for unit in range(units):
            if unit + 1 < units:
                self.load(unit + 1).start()
            self.load(unit).wait()
            height = self.buffer.shape[1]
            high, low = self.split[unit // 4]

            def part(index, carry, unit=unit, high=high, low=low, height=height):
                here = pl.multiple_of(index * 16, 16)
                rows = pl.ds(pl.multiple_of(unit % 4 * height + index * 16, 16), 16)
                high[rows, :], low[rows, :] = halves(self.buffer[unit % 2, pl.ds(here, 16), :])
                return carry

            lax.fori_loop(0, height // 16, part, 0)

    def places(self, index):
        rows = self.ring.rows
        half = rows // 2
        return [
            (pl.ds(pl.multiple_of(self.ring.at(-index) * rows, 8), half), pl.ds(0, half)),
            (pl.ds(pl.multiple_of(self.ring.at(index) * rows + half, 8), half), pl.ds(half, half)),
        ]

    def outgoing(self, index):
        return [
            pltpu.make_async_copy(made.at[index % 2, here], sink.at[there], self.out_sem.at[k, index % 2, way])
            for k, (made, sink) in enumerate(zip(self.made, self.sinks))
            for way, (there, here) in enumerate(self.places(index))
        ]

    def take(self, index, own):
        if own:
            self.stage[...] = self.ring.x[...]
        else:
            copies = [
                pltpu.make_async_copy(self.ring.o.at[there], self.stage.at[here], self.stage_sem.at[way])
                for way, (there, here) in enumerate(self.places(index))
            ]
            for copy in copies:
                copy.start()
            for copy in copies:
                copy.wait()

    def work(self, index):
        def free():
            for copy in self.outgoing(index - 2):
                copy.wait()

        pl.when(index >= 2)(free)
        high, low = halves(self.stage[...])
        for made, split in zip(self.made, self.split):
            made[index % 2] = thrice((high, low), (split[0][...], split[1][...]), NT)
        for copy in self.outgoing(index):
            copy.start()

    def step(self, index):
        @pl.when(index == 0)
        def _():
            self.take(index, True)

        @pl.when(index > 0)
        def _():
            self.take(index, False)

        self.work(index)

    def end(self):
        for index in (self.ring.n - 2, self.ring.n - 1):
            for copy in self.outgoing(index):
                copy.wait()

    @staticmethod
    def outputs(n, x, rights):
        return [jax.ShapeDtypeStruct((n * x.shape[0], right.shape[0]), jnp.float32) for right in rights]

    @staticmethod
    def scratch(n, x, rights):
        if not rights:
            return []
        height, columns = rights[0].shape
        made = [pltpu.VMEM((2, height // 4, columns), jnp.float32), pltpu.VMEM(x.shape, jnp.float32)]
        for right in rights:
            made += [pltpu.VMEM(right.shape, jnp.bfloat16)] * 2
        made += [pltpu.VMEM((2, x.shape[0], right.shape[0]), jnp.float32) for right in rights]
        return made + [
            pltpu.SemaphoreType.DMA((2,)),
            pltpu.SemaphoreType.DMA((2,)),
            pltpu.SemaphoreType.DMA((len(rights), 2, 2)),
        ]


def gather_body(n, cuts, plan, count, x_ref, *refs):
    rights, refs = refs[:count], refs[count:]
    work = Work(plan, refs, 1 + count)
    rest = list(work.rest)
    ring = Ring(n, cuts, x_ref, work.first[0], rest[:3])
    arrive = Arrive(ring, rights, work.first[1:] + rest[3:]) if count else None
    work.load()
    if count:
        arrive.load(0).start()
    greet(ring.sides)
    ring.begin()
    if count:
        arrive.prepare()
    work.ready()

    def share(step):
        if count:
            arrive.step(step)
        work.share(n - 1, step)

    ring.run(share)
    ring.received()
    if count:
        arrive.take(n - 1, False)
        arrive.work(n - 1)
    ring.sent()
    work.end()
    if count:
        arrive.end()


def ring_gather(x, n, number, jobs=(), rights=(), cuts=2):
    rows, columns = x.shape
    cuts = min(cuts, rows // 16)
    plan = [job.bare() for job in jobs]
    rights = list(rights)
    made = [jax.ShapeDtypeStruct((n * rows, columns), x.dtype), *Arrive.outputs(n, x, rights)]
    result = pl.pallas_call(
        functools.partial(gather_body, n, cuts, plan, len(rights)),
        out_shape=(*made, *Work.outputs(jobs)),
        in_specs=spaces(1, pltpu.VMEM) + spaces(len(rights) + len(Work.operands(jobs))),
        out_specs=tuple(spaces(len(made) + len(Work.outputs(jobs)))),
        scratch_shapes=Work.scratch(jobs) + Ring.scratch(n, cuts) + Arrive.scratch(n, x, rights),
        compiler_params=pltpu.CompilerParams(
            collective_id=number,
            has_side_effects=True,
            vmem_limit_bytes=(60 << 20) if jobs or rights else limit(jobs, x.shape),
        ),
        cost_estimate=cost(75.0 * columns / 2048),
        name=f"ring_gather_{number}",
    )(x, *rights, *Work.operands(jobs))
    return result if jobs or rights else result[0]


def opening_body(n, dp, cuts, grad, down, pair, hidden, grad_all, wide_down, wide_pair, hidden_turn, *sems):
    ring = Ring(n, cuts, grad, grad_all, sems[:3])
    parts = [
        Spread(dp, down, wide_down, sems[3:8]),
        Spread(dp, pair, wide_pair, sems[8:13]),
        Swap(dp, True, hidden, hidden_turn, sems[13:16]),
    ]
    greet(list(ring.sides) + [{"dp": other} for other in others("dp")])
    for part in parts:
        part.begin()
    ring.begin()
    ring.run()
    for part in parts:
        part.end()
    ring.end()


def opening(grad, down, pair, hidden, n, dp, number, cuts=2):
    def full(x, times):
        return jax.ShapeDtypeStruct((x.shape[0] * times, x.shape[1]), x.dtype)

    turned = jax.ShapeDtypeStruct((hidden.shape[0] * dp, hidden.shape[1] // dp), hidden.dtype)
    return pl.pallas_call(
        functools.partial(opening_body, n, dp, cuts),
        out_shape=(full(grad, n), full(down, dp), full(pair, dp), turned),
        in_specs=spaces(4, pltpu.VMEM),
        out_specs=tuple(spaces(4)),
        scratch_shapes=Ring.scratch(n, cuts) + Spread.scratch(dp) * 2 + Swap.scratch(dp),
        compiler_params=pltpu.CompilerParams(collective_id=number, has_side_effects=True),
        cost_estimate=cost(80.0),
        name="opening",
    )(grad, down, pair, hidden)


def spread_body(dp, x_ref, o_ref, *sems):
    part = Spread(dp, x_ref, o_ref, sems, 4)
    greet([{"dp": other} for other in others("dp")])
    part.begin()
    part.end()


def dp_gather(x, dp, number):
    return pl.pallas_call(
        functools.partial(spread_body, dp),
        out_shape=jax.ShapeDtypeStruct((x.shape[0] * dp, x.shape[1]), x.dtype),
        in_specs=spaces(1, pltpu.VMEM),
        out_specs=pl.BlockSpec(memory_space=pl.ANY),
        scratch_shapes=Spread.scratch(dp, 4),
        compiler_params=pltpu.CompilerParams(collective_id=number, has_side_effects=True),
        cost_estimate=cost(20.0),
        name=f"dp_gather_{number}",
    )(x)


class RingSum:
    def __init__(self, n, cuts, x_ref, o_ref, held, sems):
        self.n, self.cuts, self.x, self.o, self.held = n, cuts, x_ref, o_ref, held
        self.send_sem, self.recv_sem = sems
        self.me, self.at = ring_places(n)
        self.sides = ({"heads": self.at(1)}, {"heads": self.at(-1)})
        self.rows = x_ref.shape[0] // n
        self.half = self.rows // 2
        self.piece = self.half // cuts
        self.parts = [(cut, way) for cut in range(cuts) for way in (0, 1)]

    def mine(self, owner, cut, way):
        start = owner * self.rows + way * self.half + cut * self.piece
        return self.x.at[pl.ds(pl.multiple_of(start, 8), self.piece)]

    def slot(self, step, cut, way):
        return self.held.at[way, step, pl.ds(cut * self.piece, self.piece)]

    def owner(self, step, way):
        return self.at(-1 - step) if way == 0 else self.at(1 + step)

    def copy(self, step, cut, way, first=False):
        src = self.mine(self.owner(step, way), cut, way) if first else self.slot(step - 1, cut, way)
        sems = self.send_sem.at[way, step, cut], self.recv_sem.at[way, step, cut]
        return remote(src, self.slot(step, cut, way), *sems, self.sides[way])

    def begin(self):
        for part in self.parts:
            self.copy(0, *part, first=True).start()

    def step(self, step):
        for cut, way in self.parts:
            self.arrived(step - 1, cut, way)
            total = self.slot(step - 1, cut, way)
            total[...] += self.mine(self.owner(step, way), cut, way)[...]
            self.copy(step, cut, way).start()

    def arrived(self, step, cut, way):
        slot = self.slot(step, cut, way)
        sems = self.send_sem.at[way, step, cut], self.recv_sem.at[way, step, cut]
        remote(slot, slot, *sems, self.sides[way]).wait_recv()

    def end(self):
        for cut, way in self.parts:
            self.arrived(self.n - 2, cut, way)
            self.o[pl.ds(way * self.half + cut * self.piece, self.piece)] = (
                self.mine(self.me, cut, way)[...] + self.slot(self.n - 2, cut, way)[...]
            )

        def sent(step, carry):
            for cut, way in self.parts:
                slot = self.slot(step, cut, way)
                sems = self.send_sem.at[way, step, cut], self.recv_sem.at[way, step, cut]
                remote(slot, slot, *sems, self.sides[way]).wait_send()
            return carry

        lax.fori_loop(0, self.n - 1, sent, 0)

    run = Ring.run

    @staticmethod
    def scratch(n, cuts, rows, columns):
        return [
            pltpu.VMEM((2, n - 1, rows // 2, columns), jnp.float32),
            pltpu.SemaphoreType.DMA((2, n - 1, cuts)),
            pltpu.SemaphoreType.DMA((2, n - 1, cuts)),
        ]


def scatter_body(n, cuts, plan, x_ref, *refs):
    work = Work(plan, refs, 1)
    ring = RingSum(n, cuts, x_ref, work.first[0], work.rest[0], work.rest[1:])
    work.load()
    greet(ring.sides)
    ring.begin()
    work.ready()
    ring.run(functools.partial(work.share, n - 1))
    ring.end()
    work.end()


def ring_scatter(x, n, number, jobs=(), cuts=4):
    rows, columns = x.shape[0] // n, x.shape[1]
    cuts = min(cuts, rows // 16)
    plan = [job.bare() for job in jobs]
    result = pl.pallas_call(
        functools.partial(scatter_body, n, cuts, plan),
        out_shape=(jax.ShapeDtypeStruct((rows, columns), x.dtype), *Work.outputs(jobs)),
        in_specs=spaces(1, pltpu.VMEM) + spaces(len(Work.operands(jobs))),
        out_specs=tuple(spaces(1, pltpu.VMEM) + spaces(len(Work.outputs(jobs)))),
        scratch_shapes=Work.scratch(jobs) + RingSum.scratch(n, cuts, rows, columns),
        compiler_params=pltpu.CompilerParams(
            collective_id=number, has_side_effects=True, vmem_limit_bytes=limit(jobs, x.shape, x.shape, (rows, columns))
        ),
        cost_estimate=cost(75.0 * columns / 2048),
        name=f"ring_scatter_{number}",
    )(x, *Work.operands(jobs))
    return result if jobs else result[0]


def turn_body(n, dp, cuts, x_ref, hidden, o_ref, hidden_turn, held, *sems):
    ring = RingSum(n, cuts, x_ref, o_ref, held, sems[:2])
    swap = Swap(dp, False, hidden, hidden_turn, sems[2:])
    greet(list(ring.sides) + [{"dp": other} for other in others("dp")])
    swap.begin()
    ring.begin()
    ring.run()
    swap.end()
    ring.end()


def scatter_and_turn(x, hidden, n, dp, number, cuts=2):
    rows, columns = x.shape[0] // n, x.shape[1]
    cuts = min(cuts, rows // 16)
    return pl.pallas_call(
        functools.partial(turn_body, n, dp, cuts),
        out_shape=(
            jax.ShapeDtypeStruct((rows, columns), x.dtype),
            jax.ShapeDtypeStruct((hidden.shape[0] // dp, hidden.shape[1] * dp), x.dtype),
        ),
        in_specs=spaces(2, pltpu.VMEM),
        out_specs=(pl.BlockSpec(memory_space=pltpu.VMEM), pl.BlockSpec(memory_space=pl.ANY)),
        scratch_shapes=RingSum.scratch(n, cuts, rows, columns) + Swap.scratch(dp),
        compiler_params=pltpu.CompilerParams(
            collective_id=number, has_side_effects=True, vmem_limit_bytes=40 << 20
        ),
        cost_estimate=cost(35.0),
        name="scatter_and_turn",
    )(x, hidden)


class Total:
    def __init__(self, axis, x_ref, held, sems):
        self.x, self.held = x_ref, held
        self.send_sem, self.recv_sem = sems
        self.names = [{axis: other} for other in others(axis)]
        self.count = lax.axis_size(axis)

    def begin(self):
        self.copies = [
            push(self.x, self.held.at[k], self.send_sem.at[k], self.recv_sem.at[k], name)
            for k, name in enumerate(self.names)
        ]

    def end(self):
        for copy in self.copies:
            copy.wait_recv()
        for copy in self.copies:
            copy.wait_send()

    @staticmethod
    def scratch(count, shape):
        return [
            pltpu.VMEM((count - 1,) + shape, jnp.float32),
            pltpu.SemaphoreType.DMA((count - 1,)),
            pltpu.SemaphoreType.DMA((count - 1,)),
        ]


def in_order(axis, own, held):
    count = lax.axis_size(axis)
    me = lax.axis_index(axis)
    total = None
    for device in range(count):
        term = jnp.where(me == device, own, jnp.zeros_like(own))
        for k in range(1, count):
            term = term + jnp.where(lax.rem(me - k + count, count) == device, held[k - 1], jnp.zeros_like(own))
        total = term if total is None else total + term
    return total


def sum_body(x_ref, o_ref, middle, held_heads, hs, hr, held_dp, ds, dr):
    first = Total("heads", x_ref, held_heads, (hs, hr))
    second = Total("dp", middle, held_dp, (ds, dr))
    greet(first.names + second.names)
    first.begin()
    first.end()
    middle[...] = in_order("heads", x_ref[...], held_heads)
    second.begin()
    second.end()
    o_ref[...] = in_order("dp", middle[...], held_dp)


def gather_and_sum_body(n, cuts, x_ref, gains, o_ref, total, *refs):
    ring = Ring(n, cuts, x_ref, o_ref, refs[:3])
    middle, held_heads, hs, hr, held_dp, ds, dr = refs[3:]
    first = Total("heads", gains, held_heads, (hs, hr))
    second = Total("dp", middle, held_dp, (ds, dr))
    greet(first.names + second.names)
    first.begin()
    ring.begin()
    first.end()
    middle[...] = in_order("heads", gains[...], held_heads)
    second.begin()
    ring.run()
    second.end()
    total[...] = in_order("dp", middle[...], held_dp)
    ring.end()


def gather_and_sum(x, gains, n, dp, number, cuts=2):
    rows, columns = x.shape
    cuts = min(cuts, rows // 16)
    return pl.pallas_call(
        functools.partial(gather_and_sum_body, n, cuts),
        out_shape=(
            jax.ShapeDtypeStruct((n * rows, columns), x.dtype),
            jax.ShapeDtypeStruct(gains.shape, gains.dtype),
        ),
        in_specs=spaces(2, pltpu.VMEM),
        out_specs=(pl.BlockSpec(memory_space=pl.ANY), pl.BlockSpec(memory_space=pltpu.VMEM)),
        scratch_shapes=Ring.scratch(n, cuts)
        + [pltpu.VMEM(gains.shape, gains.dtype)]
        + Total.scratch(n, gains.shape)
        + Total.scratch(dp, gains.shape),
        compiler_params=pltpu.CompilerParams(
            collective_id=number, has_side_effects=True, vmem_limit_bytes=16 << 20
        ),
        cost_estimate=cost(35.0),
        name="gather_and_sum",
    )(x, gains)


def sum_all(x, n, dp, number):
    return pl.pallas_call(
        sum_body,
        out_shape=jax.ShapeDtypeStruct(x.shape, x.dtype),
        in_specs=spaces(1, pltpu.VMEM),
        out_specs=pl.BlockSpec(memory_space=pltpu.VMEM),
        scratch_shapes=[pltpu.VMEM(x.shape, x.dtype)] + Total.scratch(n, x.shape) + Total.scratch(dp, x.shape),
        compiler_params=pltpu.CompilerParams(collective_id=number, has_side_effects=True),
        cost_estimate=cost(8.0),
        name=f"sum_all_{number}",
    )(x)


NT = (((1,), (1,)), ((), ()))
NN = (((1,), (0,)), ((), ()))


def thrice(left, right, numbers):
    terms = [(left[0], right[0]), (left[0], right[1]), (left[1], right[0])]
    made = [lax.dot_general(*term, numbers, preferred_element_type=jnp.float32) for term in terms]
    return made[0] + (made[1] + made[2])


def turned(front, back, cosine, sines):
    return front * cosine - back * sines, back * cosine + front * sines


def keep_halves(value, pair, where):
    pair[0][where], pair[1][where] = halves(value)


def allowed_block(start, rows, reach, seg_rows, seg_columns):
    row = start + lax.broadcasted_iota(jnp.int32, (rows, reach), 0)
    column = lax.broadcasted_iota(jnp.int32, (rows, reach), 1)
    return (seg_rows[start : start + rows, :] == seg_columns[:, :reach]) & (column <= row)


def attend_body(latent_dim, rows, raw, packed, cosine, sines, seg_rows, seg_columns, mixed, query, lse, *split):
    total, width = raw.shape
    dim = (packed.shape[1] - latent_dim) // 2
    half = dim // 2
    scale = dim ** (-0.5)
    key, value = split[:2], split[2:]
    keep_halves(packed[:, latent_dim : latent_dim + dim], key, (slice(None), slice(None)))
    keep_halves(packed[:, latent_dim + dim :], value, (slice(None), slice(None)))
    for start in range(0, total, rows):
        here = slice(start, start + rows)
        reach = start + rows
        allowed = allowed_block(start, rows, reach, seg_rows, seg_columns)
        for head in range(width // dim):
            at = head * dim
            front, back = turned(
                raw[here, at : at + half], raw[here, at + half : at + dim], cosine[here, :], sines[here, :]
            )
            query[here, at : at + half] = front
            query[here, at + half : at + dim] = back
            own = halves(query[here, at : at + dim])
            scores = thrice(own, [ref[:reach, :] for ref in key], NT) * scale
            scores = jnp.where(allowed, scores, -1e30)
            top = jnp.max(scores, axis=1, keepdims=True)
            expo = jnp.exp(scores - top)
            denom = jnp.sum(expo, axis=1, keepdims=True)
            made = thrice(halves(expo), [ref[:reach, :] for ref in value], NN)
            mixed[here, at : at + dim] = made / denom
            lse[here, head * 128 : head * 128 + 128] = jnp.broadcast_to(top + jnp.log(denom), (rows, 128))


def attend(raw, packed, cosine, sines, seg_rows, seg_columns, latent_dim):
    total, width = raw.shape
    dim = (packed.shape[1] - latent_dim) // 2
    shape = jax.ShapeDtypeStruct
    return pl.pallas_call(
        functools.partial(attend_body, latent_dim, 256),
        out_shape=(
            shape(raw.shape, jnp.float32),
            shape(raw.shape, jnp.float32),
            shape((total, width // dim * 128), jnp.float32),
        ),
        in_specs=spaces(6, pltpu.VMEM),
        out_specs=tuple(spaces(3, pltpu.VMEM)),
        scratch_shapes=[pltpu.VMEM((total, dim), jnp.bfloat16)] * 4,
        compiler_params=pltpu.CompilerParams(vmem_limit_bytes=ATTEND_LIMIT),
        cost_estimate=cost(14.0),
        name="attend",
    )(raw, packed, cosine, sines, seg_rows, seg_columns)


def attend_back_body(
    latent_dim, rows, query, packed, cosine, sines, seg_rows, seg_columns, lse, mixed, d_mixed, up, d_raw, out, *split
):
    total, width = query.shape
    dim = (packed.shape[1] - latent_dim) // 2
    half = dim // 2
    scale = dim ** (-0.5)
    key, value, weight, made = split[:2], split[2:4], split[4:6], split[6:]
    every = (slice(None), slice(None))
    keep_halves(packed[:, latent_dim : latent_dim + dim], key, every)
    keep_halves(packed[:, latent_dim + dim :], value, every)
    keep_halves(up[...], weight, every)
    out[:, latent_dim:] = jnp.zeros((total, 2 * dim), jnp.float32)
    for start in range(0, total, rows):
        here = slice(start, start + rows)
        reach = start + rows
        allowed = allowed_block(start, rows, reach, seg_rows, seg_columns)
        for head in range(width // dim):
            at = head * dim
            own = halves(query[here, at : at + dim])
            upstream = d_mixed[here, at : at + dim]
            grad = halves(upstream)
            scores = thrice(own, [ref[:reach, :] for ref in key], NT) * scale
            scores = jnp.where(allowed, scores, -1e30)
            probs = jnp.exp(scores - lse[here, head * 128 : head * 128 + 1])
            d_probs = thrice(grad, [ref[:reach, :] for ref in value], NT)
            delta = jnp.sum(upstream * mixed[here, at : at + dim], axis=1, keepdims=True)
            d_scores = probs * (d_probs - delta) * scale
            out[:reach, latent_dim + dim :] += thrice(halves(probs.T), grad, NN)
            out[:reach, latent_dim : latent_dim + dim] += thrice(halves(d_scores.T), own, NN)
            d_query = thrice(halves(d_scores), [ref[:reach, :] for ref in key], NN)
            front, back = turned(d_query[:, :half], d_query[:, half:], cosine[here, :], -sines[here, :])
            for piece, off in ((front, at), (back, at + half)):
                d_raw[here, off : off + half] = piece
                keep_halves(piece, made, (slice(None), slice(off, off + half)))
        out[here, :latent_dim] = thrice([ref[...] for ref in made], [ref[...] for ref in weight], NT)


def attend_back(query, packed, cosine, sines, seg_rows, seg_columns, lse, mixed, d_mixed, up, latent_dim):
    total, width = query.shape
    dim = (packed.shape[1] - latent_dim) // 2
    shape = jax.ShapeDtypeStruct
    rows = 256
    return pl.pallas_call(
        functools.partial(attend_back_body, latent_dim, rows),
        out_shape=(shape(query.shape, jnp.float32), shape(packed.shape, jnp.float32)),
        in_specs=spaces(10, pltpu.VMEM),
        out_specs=tuple(spaces(2, pltpu.VMEM)),
        scratch_shapes=[pltpu.VMEM((total, dim), jnp.bfloat16)] * 4
        + [pltpu.VMEM(up.shape, jnp.bfloat16)] * 2
        + [pltpu.VMEM((rows, width), jnp.bfloat16)] * 2,
        compiler_params=pltpu.CompilerParams(vmem_limit_bytes=ATTEND_LIMIT),
        cost_estimate=cost(30.0),
        name="attend_back",
    )(query, packed, cosine, sines, seg_rows, seg_columns, lse, mixed, d_mixed, up)


def rope_tables(position, head_dim):
    half_dim = head_dim // 2
    frequency = ROPE_BASE ** (-jnp.arange(half_dim, dtype=jnp.float32) / half_dim)
    angles = position.astype(jnp.float32)[:, None] * frequency[None, :]
    return jnp.cos(angles), jnp.sin(angles)


ATTEND_LIMIT = 58 << 20


def matmul_high(left, right):
    return jnp.dot(left, right, precision=HIGH, preferred_element_type=jnp.float32)


def layout(lengths_row, row_index):
    upto = jnp.arange(lengths_row.shape[0], dtype=jnp.int32)
    doc_ends = jnp.sum(jnp.where(upto[None, :] <= upto[:, None], lengths_row[None, :], 0), axis=1)
    doc_starts = doc_ends - lengths_row
    segment = jnp.sum((row_index[:, None] >= doc_ends[None, :]).astype(jnp.int32), axis=1)
    doc_ids = jnp.arange(doc_ends.shape[0], dtype=jnp.int32)
    start_of = jnp.sum(
        jnp.where(segment[:, None] == doc_ids[None, :], doc_starts[None, :], 0), axis=1
    )
    return (segment, row_index - start_of)


def rotate(vector, position, sign):
    half_dim = vector.shape[-1] // 2
    frequency = ROPE_BASE ** (-jnp.arange(half_dim, dtype=jnp.float32) / half_dim)
    angles = position.astype(jnp.float32)[:, None] * frequency[None, :]
    angles = angles.reshape((angles.shape[0],) + (1,) * (vector.ndim - 2) + (half_dim,))
    cosine = jnp.cos(angles)
    sines = sign * jnp.sin(angles)
    front = vector[..., :half_dim]
    back_half = vector[..., half_dim:]
    return jnp.concatenate(
        [front * cosine - back_half * sines, back_half * cosine + front * sines], axis=-1
    )


def norm_back(upstream, normed, inverse, gain):
    scaled = upstream * gain
    return (
        inverse * (scaled - normed * jnp.mean(scaled * normed, axis=1, keepdims=True)),
        jnp.sum(upstream * normed, axis=0),
    )


def owned(part, axis):
    return lax.psum_scatter(part, "dp", scatter_dimension=axis, tiled=True)


def moments(value, grad, first, second):
    first_new = BETA_ONE * first + (1.0 - BETA_ONE) * grad
    second_new = BETA_TWO * second + (1.0 - BETA_TWO) * grad * grad
    update = (
        first_new
        * (1.0 / (1.0 - BETA_ONE**STEP_COUNT))
        / (jnp.sqrt(second_new * (1.0 / (1.0 - BETA_TWO**STEP_COUNT))) + ADAM_EPS)
        + DECAY * value
    )
    return (first_new, second_new, update)


def chunk_of(rows):
    return next(c for c in (64, 32, 16, 8) if rows % c == 0)


def moments_body(slots, shares, offsets, count_grads, *refs):
    count = len(slots)
    values, firsts, seconds = refs[:count], refs[count : 2 * count], refs[2 * count : 3 * count]
    grads = refs[3 * count : 3 * count + count_grads]
    outs = refs[3 * count + count_grads : -1]
    table = refs[-1]
    row = lax.broadcasted_iota(jnp.int32, table.shape, 0)
    lane = lax.broadcasted_iota(jnp.int32, table.shape, 1)
    sums = jnp.zeros(table.shape, jnp.float32)
    for k, slot in enumerate(slots):
        height, width = values[k].shape
        chunk = chunk_of(height)
        which, offset, below = offsets[k]

        def part(index, carry, k=k, chunk=chunk, width=width, which=which, offset=offset, below=below):
            rows = pl.ds(pl.multiple_of(index * chunk, chunk), chunk)
            under = pl.ds(pl.multiple_of(below + index * chunk, 8), chunk)
            value = values[k][rows, :]
            first, second, update = moments(
                value, grads[which][under, offset : offset + width], firsts[k][rows, :], seconds[k][rows, :]
            )
            for out, made in zip(outs[3 * k : 3 * k + 3], (first, second, update)):
                out[rows, :] = made

            def folded(x):
                return jnp.sum((x * x).reshape(chunk // 8, 8, width), axis=0)

            return carry[0] + folded(value), carry[1] + folded(update)

        zero = jnp.zeros((8, width), jnp.float32)
        for at, square in enumerate(lax.fori_loop(0, height // chunk, part, (zero, zero))):
            total = jnp.sum(jnp.sum(square, axis=1, keepdims=True), axis=0, keepdims=True) * shares[k]
            sums += jnp.where((row == slot) & (lane == at), total, 0.0)
    table[...] = sums


def all_moments(slots, shares, offsets, values, firsts, seconds, grads):
    shape = jax.ShapeDtypeStruct
    made = pl.pallas_call(
        functools.partial(moments_body, slots, shares, offsets, len(grads)),
        out_shape=(
            *[shape(value.shape, jnp.float32) for value in values for _ in range(3)],
            shape((8, 128), jnp.float32),
        ),
        in_specs=spaces(3 * len(values) + len(grads), pltpu.VMEM),
        out_specs=tuple(spaces(3 * len(values) + 1, pltpu.VMEM)),
        compiler_params=pltpu.CompilerParams(vmem_limit_bytes=52 << 20),
        cost_estimate=cost(12.0),
        name=f"moments_{slots[0]}",
    )(*values, *firsts, *seconds, *grads)
    return [made[3 * k : 3 * k + 3] for k in range(len(values))], made[-1]


def finish_body(count, table, *refs):
    values, updates, outs, norms = refs[:count], refs[count : 2 * count], refs[2 * count : -1], refs[-1]
    norms[...] = jnp.sqrt(table[...])
    for k in range(count):
        ratio = RATE * (norms[k : k + 1, 0:1] / norms[k : k + 1, 1:2])
        height = values[k].shape[0]
        chunk = chunk_of(height)

        def part(index, carry, k=k, chunk=chunk, ratio=ratio):
            rows = pl.ds(pl.multiple_of(index * chunk, chunk), chunk)
            outs[k][rows, :] = values[k][rows, :] - ratio * updates[k][rows, :]
            return carry

        lax.fori_loop(0, height // chunk, part, 0)


def finish(table, values, updates):
    shape = jax.ShapeDtypeStruct
    made = pl.pallas_call(
        functools.partial(finish_body, len(values)),
        out_shape=(*[shape(value.shape, jnp.float32) for value in values], shape(table.shape, jnp.float32)),
        in_specs=spaces(2 * len(values) + 1, pltpu.VMEM),
        out_specs=tuple(spaces(len(values) + 1, pltpu.VMEM)),
        compiler_params=pltpu.CompilerParams(vmem_limit_bytes=48 << 20),
        cost_estimate=cost(9.0),
        name="finish",
    )(table, *values, *updates)
    return made[:-1], made[-1]


def on_device(
    block_input,
    output_grad,
    lengths,
    norm_gains,
    norm_gains_first,
    norm_gains_second,
    query_down,
    query_down_first,
    query_down_second,
    key_value,
    key_value_first,
    key_value_second,
    query_up,
    query_up_first,
    query_up_second,
    head_merge,
    head_merge_first,
    head_merge_second,
    gate_weight,
    gate_weight_first,
    gate_weight_second,
    up_weight,
    up_weight_first,
    up_weight_second,
    down_weight,
    down_weight_first,
    down_weight_second,
):
    tok_rows = block_input.shape[0]
    model_dim = block_input.shape[1]
    latent_dim = query_down.shape[1]
    head_dim = key_value.shape[1] // 2
    heads_count = lax.axis_size("heads")
    dp_count = lax.axis_size("dp")
    group_rows = tok_rows * heads_count
    group_index = jnp.arange(group_rows, dtype=jnp.int32)
    segment, position = layout(lengths[0], group_index)
    local_position = lax.dynamic_slice_in_dim(
        position, lax.axis_index("heads") * tok_rows, tok_rows
    )
    gain_attn = norm_gains[:model_dim]
    gain_query = norm_gains[model_dim : model_dim + latent_dim]
    gain_ffn = norm_gains[model_dim + latent_dim :]
    inv_one = lax.rsqrt(jnp.mean(block_input * block_input, axis=1, keepdims=True) + EPS_NORM)
    normed_one = block_input * inv_one
    hidden_one = normed_one * gain_attn
    grad_all, wide_down, wide_pair, hidden_turn = opening(
        output_grad, query_down, key_value, hidden_one, heads_count, dp_count, 5
    )
    query_up_in, head_merge_in, gate_in, upper_in, lower_in, grad_all = lax.optimization_barrier(
        (query_up, head_merge, gate_weight, up_weight, down_weight, grad_all)
    )
    wide_up = lax.all_gather(query_up_in, "dp", axis=0, tiled=True)
    wide_merge = lax.all_gather(head_merge_in, "dp", axis=1, tiled=True)
    latent_raw = matmul_high(hidden_one, wide_down)
    inv_query = lax.rsqrt(jnp.mean(latent_raw * latent_raw, axis=1, keepdims=True) + EPS_NORM)
    latent_hat = latent_raw * inv_query
    latent = latent_hat * gain_query
    pair_local = matmul_high(hidden_one, wide_pair)
    key_local = rotate(pair_local[:, :head_dim], local_position, 1.0)
    value_local = pair_local[:, head_dim:]
    packed = jnp.concatenate([latent, key_local, value_local], axis=1)
    lower_in, packed = lax.optimization_barrier((lower_in, packed))
    wide_lower = lax.all_gather(lower_in, "dp", axis=1, tiled=True)
    packed_all = ring_gather(packed, heads_count, 1)
    gate_in, upper_in, packed_all = lax.optimization_barrier((gate_in, upper_in, packed_all))
    turned_gate = lax.all_gather(gate_in.T, "dp", axis=1, tiled=True)
    turned_upper = lax.all_gather(upper_in.T, "dp", axis=1, tiled=True)
    latent_all = packed_all[:, :latent_dim]
    cosine, sines = rope_tables(position, head_dim)
    seg_rows, seg_columns = segment[:, None], segment[None, :]
    mixed_heads, query_rot, lse = attend(
        matmul_high(latent_all, wide_up), packed_all, cosine, sines, seg_rows, seg_columns, latent_dim
    )
    inside = group_rows <= 1024

    def job(*what):
        return [Job(*what)] if inside else []

    part_middle = matmul_high(mixed_heads, wide_merge)
    if inside:
        part_middle, d_activ = ring_scatter(
            part_middle, heads_count, 2, job("nt", [grad_all], [wide_lower], 256)
        )
    else:
        part_middle = ring_scatter(part_middle, heads_count, 2)
        d_activ = matmul_high(grad_all, wide_lower.T)
    middle = block_input + part_middle
    inv_two = lax.rsqrt(jnp.mean(middle * middle, axis=1, keepdims=True) + EPS_NORM)
    normed_two = middle * inv_two
    hidden_two = normed_two * gain_ffn
    if inside:
        hidden_all, gate_pre, up_pre = ring_gather(
            hidden_two, heads_count, 3, rights=[turned_gate, turned_upper]
        )
    else:
        hidden_all = ring_gather(hidden_two, heads_count, 3)
        gate_pre = matmul_high(hidden_all, turned_gate.T)
        up_pre = matmul_high(hidden_all, turned_upper.T)
    sig_gate = jax.nn.sigmoid(gate_pre)
    silu_gate = gate_pre * sig_gate
    activ = silu_gate * up_pre
    d_gate_pre = d_activ * up_pre * (sig_gate * (1.0 + gate_pre * (1.0 - sig_gate)))
    d_up_pre = d_activ * silu_gate
    part_output = matmul_high(activ, wide_lower)
    if inside:
        part_output, part_two = ring_scatter(
            part_output,
            heads_count,
            4,
            job("nn", [d_gate_pre, d_up_pre], [turned_gate, turned_upper], 128),
        )
        d_hidden_two, grad_both = ring_scatter(
            part_two,
            heads_count,
            6,
            job("tn", [hidden_all], [d_gate_pre], 256, True) + job("tn", [grad_all], [activ], 256, True),
        )
    else:
        part_output = ring_scatter(part_output, heads_count, 4)
        part_two = matmul_high(d_gate_pre, turned_gate) + matmul_high(d_up_pre, turned_upper)
        d_hidden_two = ring_scatter(part_two, heads_count, 6)
        grad_both = jnp.concatenate(
            [matmul_high(d_gate_pre.T, hidden_all), matmul_high(activ.T, grad_all)], axis=0
        )
    block_output = middle + part_output
    grad_both = owned(grad_both, 1)
    d_normed_mid, grad_gain_ffn = norm_back(d_hidden_two, normed_two, inv_two, gain_ffn)
    d_middle = output_grad + d_normed_mid
    if inside:
        middle_all, d_mixed, grad_upper = ring_gather(
            d_middle, heads_count, 7, job("tn", [hidden_all], [d_up_pre], 256), [wide_merge]
        )
    else:
        middle_all = ring_gather(d_middle, heads_count, 7)
        d_mixed = matmul_high(middle_all, wide_merge.T)
        grad_upper = matmul_high(d_up_pre.T, hidden_all)
    d_query_pre, packed_part = attend_back(
        query_rot,
        packed_all,
        cosine,
        sines,
        seg_rows,
        seg_columns,
        lse,
        mixed_heads,
        d_mixed,
        wide_up,
        latent_dim,
    )
    packed_part, grad_both, grad_upper = lax.optimization_barrier((packed_part, grad_both, grad_upper))
    grad_upper = owned(grad_upper, 1)
    if inside:
        packed_grad, grad_merge, grad_up = ring_scatter(
            packed_part,
            heads_count,
            8,
            job("tn", [middle_all], [mixed_heads], 256) + job("tn", [d_query_pre], [(packed_all, jax.ShapeDtypeStruct(latent_all.shape, jnp.float32))], 256),
        )
    else:
        packed_grad = ring_scatter(packed_part, heads_count, 8)
        grad_merge = matmul_high(mixed_heads.T, middle_all)
        grad_up = matmul_high(latent_all.T, d_query_pre)
    packed_grad, grad_upper = lax.optimization_barrier((packed_grad, grad_upper))
    d_latent = packed_grad[:, :latent_dim]
    d_key_local = packed_grad[:, latent_dim : latent_dim + head_dim]
    d_value_local = packed_grad[:, latent_dim + head_dim :]
    d_pair = jnp.concatenate([rotate(d_key_local, local_position, -1.0), d_value_local], axis=1)
    d_latent_raw, grad_gain_query = norm_back(d_latent, latent_hat, inv_query, gain_query)
    raw = jnp.concatenate([d_latent_raw, d_pair], axis=1)
    raw_all = dp_gather(raw, dp_count, 11)
    raw_all, grad_merge, grad_up = lax.optimization_barrier((raw_all, grad_merge, grad_up))
    grad_up = owned(grad_up, 0)
    part_shared = matmul_high(hidden_turn.T, raw_all)
    d_hidden_turn = matmul_high(raw_all, jnp.concatenate([query_down, key_value], axis=1).T)
    shared_cut, d_hidden_one = scatter_and_turn(part_shared, d_hidden_turn, heads_count, dp_count, 9)
    d_normed_in, grad_gain_attn = norm_back(d_hidden_one, normed_one, inv_one, gain_attn)
    input_grad = d_middle + d_normed_in
    grad_gains = jnp.concatenate([grad_gain_attn, grad_gain_query, grad_gain_ffn])
    shared_cut, grad_merge, grad_up = lax.optimization_barrier((shared_cut, grad_merge, grad_up))
    grad_merge = owned(grad_merge, 1)
    shared, gains_total = gather_and_sum(
        shared_cut, grad_gains.reshape(-1, 128), heads_count, dp_count, 10
    )
    gains_total = gains_total.reshape(-1)
    def flat(gains):
        return gains.reshape(-1, 128)

    everyone = 1.0 / (heads_count * dp_count)
    early, early_sums = all_moments(
        (5, 6, 7),
        (1.0, 1.0, 1.0),
        ((0, 0, 0), (1, 0, 0), (0, 0, down_weight.shape[0])),
        (gate_weight.T, up_weight.T, down_weight),
        (gate_weight_first.T, up_weight_first.T, down_weight_first),
        (gate_weight_second.T, up_weight_second.T, down_weight_second),
        (grad_both, grad_upper),
    )
    late, late_sums = all_moments(
        (0, 1, 2, 3, 4),
        (everyone, 1.0 / heads_count, 1.0 / heads_count, 1.0, 1.0),
        ((0, 0, 0), (1, 0, 0), (1, latent_dim, 0), (2, 0, 0), (3, 0, 0)),
        (flat(norm_gains), query_down, key_value, query_up, head_merge),
        (flat(norm_gains_first), query_down_first, key_value_first, query_up_first, head_merge_first),
        (flat(norm_gains_second), query_down_second, key_value_second, query_up_second, head_merge_second),
        (flat(gains_total), shared, grad_up, grad_merge),
    )
    stepped = late + early
    table = sum_all(early_sums + late_sums, heads_count, dp_count, 13)
    new_values, norms = finish(
        table,
        (
            flat(norm_gains),
            query_down,
            key_value,
            query_up,
            head_merge,
            gate_weight.T,
            up_weight.T,
            down_weight,
        ),
        [entry[2] for entry in stepped],
    )
    results = []
    for slot in range(8):
        entry = (stepped[slot][0], stepped[slot][1], new_values[slot])
        if slot == 0:
            entry = tuple(x.reshape(-1) for x in entry)
        if slot in (5, 6):
            entry = tuple(x.T for x in entry)
        results.extend(entry)
    return (block_output, input_grad, *results, norms[:, :2])


def solution(mesh):
    placed = (
        P(("dp", "heads"), None),
        P(("dp", "heads"), None),
        P("dp", None),
        P(),
        P(),
        P(),
        P("dp", None),
        P("dp", None),
        P("dp", None),
        P("dp", None),
        P("dp", None),
        P("dp", None),
        P("dp", "heads"),
        P("dp", "heads"),
        P("dp", "heads"),
        P("heads", "dp"),
        P("heads", "dp"),
        P("heads", "dp"),
        P("dp", "heads"),
        P("dp", "heads"),
        P("dp", "heads"),
        P("dp", "heads"),
        P("dp", "heads"),
        P("dp", "heads"),
        P("heads", "dp"),
        P("heads", "dp"),
        P("heads", "dp"),
    )
    return jax.shard_map(
        on_device,
        mesh=mesh,
        in_specs=placed,
        out_specs=(
            P(("dp", "heads"), None),
            P(("dp", "heads"), None),
            P(),
            P(),
            P(),
            P("dp", None),
            P("dp", None),
            P("dp", None),
            P("dp", None),
            P("dp", None),
            P("dp", None),
            P("dp", "heads"),
            P("dp", "heads"),
            P("dp", "heads"),
            P("heads", "dp"),
            P("heads", "dp"),
            P("heads", "dp"),
            P("dp", "heads"),
            P("dp", "heads"),
            P("dp", "heads"),
            P("dp", "heads"),
            P("dp", "heads"),
            P("dp", "heads"),
            P("heads", "dp"),
            P("heads", "dp"),
            P("heads", "dp"),
            P(),
        ),
        check_vma=False,
    )
```

```python
import functools

import jax
import jax.numpy as jnp
from jax import lax
from jax.experimental import pallas as pl
from jax.experimental.pallas import tpu as pltpu
from jax.sharding import PartitionSpec as P

STEP_COUNT = 10


EPS_NORM = 1e-06
ROPE_BASE = 10000.0
BETA_ONE = 0.5
BETA_TWO = 0.6
ADAM_EPS = 1e-06
DECAY = 0.01
RATE = 0.5
HIGH = lax.Precision.HIGH
MESH = pl.DeviceIdType.MESH
RING_Z = 4


def head_at(spot, n):
    wide = n // RING_Z
    back = (spot + n - RING_Z) // n
    rest = jnp.maximum(spot - RING_Z, 0)
    row, step = rest // (wide - 1), rest % (wide - 1)
    odd = row % 2
    column = (1 - odd) * (1 + step) + odd * (wide - 1 - step)
    return (1 - back) * (spot * wide) + back * ((RING_Z - 1 - row) * wide + column)


def spot_of(head, n):
    wide = n // RING_Z
    row = RING_Z - 1 - head // wide
    column = head % wide
    odd = row % 2
    step = (1 - odd) * (column - 1) + odd * (wide - 1 - column)
    back = (column + wide - 1) // wide
    return (1 - back) * (head // wide) + back * (RING_Z + row * (wide - 1) + step)


def ring_places(n):
    me = lax.axis_index("heads")
    spot = spot_of(me, n)
    return me, lambda k: head_at(lax.rem(spot + k + 2 * n, n), n)


def others(axis):
    count = lax.axis_size(axis)
    me = lax.axis_index(axis)
    return [lax.rem(me + k, count) for k in range(1, count)]


def greet(names):
    bar = pltpu.get_barrier_semaphore()
    for name in names:
        pl.semaphore_signal(bar, inc=1, device_id=name, device_id_type=MESH)
    pl.semaphore_wait(bar, len(names))


def remote(src, dst, send, recv, name):
    return pltpu.make_async_remote_copy(
        src_ref=src, dst_ref=dst, send_sem=send, recv_sem=recv, device_id=name, device_id_type=MESH
    )


def push(*what):
    copy = remote(*what)
    copy.start()
    return copy


def halves(value):
    high = value.astype(jnp.bfloat16)
    return high, (value - high.astype(jnp.float32)).astype(jnp.bfloat16)


def padded(shape, size):
    return shape[0] * -(-shape[1] // 128) * 128 * size


class Job:
    def __init__(self, form, lefts, rights, tile, joined=False):
        self.joined = joined
        self.form, self.lefts, self.tile = form, lefts, tile
        self.whole = [x[0] if isinstance(x, tuple) else x for x in rights]
        rights = [x[1] if isinstance(x, tuple) else x for x in rights]
        self.rights = rights
        self.summed = len(lefts) > 1
        rows = rights[0].shape[0]
        self.chunk = next(c for c in (512, 352, 256, 128, 64, 32, 16) if rows % c == 0)
        if form == "tn":
            self.chunk = next(c for c in (256, 128) if rows % c == 0)
            self.extent = lefts[0].shape[1]
        else:
            self.extent = lefts[0].shape[0]
        self.chunks = rows // self.chunk
        self.prepare = self.chunks * len(rights)
        self.units = self.prepare + self.extent // tile
        width = {"nt": 0, "nn": 1, "tn": 1}[form]
        shapes = [
            (x.shape[1], self.extent) if form == "tn" else (self.extent, x.shape[width]) for x in rights
        ]
        self.outs = shapes[:1] if self.summed else shapes
        self.splits = [x.shape[::-1] if form == "tn" else x.shape for x in rights]

    def bare(self):
        kept = object.__new__(Job)
        kept.__dict__.update(self.__dict__)
        kept.lefts, kept.rights, kept.whole = len(self.lefts), len(self.rights), None
        return kept

    def scratch(self):
        made = [pltpu.VMEM(x.shape, jnp.float32) for x in self.lefts + self.rights]
        for shape in self.splits:
            made += [pltpu.VMEM(shape, jnp.bfloat16)] * 2
        made += [pltpu.VMEM(shape, jnp.float32) for shape in self.outs]
        made += [pltpu.SemaphoreType.DMA((len(self.lefts) + len(self.rights),))]
        made += [pltpu.SemaphoreType.DMA((len(self.outs), self.extent // self.tile))]
        return made

    def bytes(self):
        shapes = [x.shape for x in self.lefts + self.rights] + self.splits + self.outs
        return sum(padded(shape, 4) for shape in shapes)


def limit(jobs, *shapes):
    return (8 << 20) + sum(job.bytes() for job in jobs) + sum(padded(shape, 4) for shape in shapes)


class Work:
    def __init__(self, plan, refs, firsts):
        refs = list(refs)

        def take(count):
            taken = refs[:count]
            del refs[:count]
            return taken

        sources = [take(job.lefts + job.rights) for job in plan]
        self.first = take(firsts)
        if plan and plan[0].joined:
            [together], start, sinks = take(1), 0, []
            for job in plan:
                rows = job.outs[0][0]
                sinks.append([together.at[pl.ds(start, rows)]])
                start += rows
        else:
            sinks = [take(len(job.outs)) for job in plan]
        self.jobs = []
        for job, source, sink in zip(plan, sources, sinks):
            held = take(job.lefts + job.rights)
            split = [take(2) for _ in range(job.rights)]
            outs = take(len(job.outs))
            in_sem, out_sem = take(2)
            self.jobs.append((job, source, sink, held, split, outs, in_sem, out_sem))
        self.rest = refs
        self.units = sum(job.units for job in plan)

    @staticmethod
    def operands(jobs):
        return [x for job in jobs for x in job.lefts + job.whole]

    @staticmethod
    def outputs(jobs):
        shapes = [shape for job in jobs for shape in job.outs]
        if jobs and jobs[0].joined:
            shapes = [(sum(shape[0] for shape in shapes), shapes[0][1])]
        return [jax.ShapeDtypeStruct(shape, jnp.float32) for shape in shapes]

    @staticmethod
    def scratch(jobs):
        return [x for job in jobs for x in job.scratch()]

    def loads(self):
        return [
            pltpu.make_async_copy(source[k].at[:, : held[k].shape[1]], held[k], in_sem.at[k])
            for _, source, _, held, _, _, in_sem, _ in self.jobs
            for k in range(len(source))
        ]

    def load(self):
        for copy in self.loads():
            copy.start()

    def ready(self):
        for copy in self.loads():
            copy.wait()

    def share(self, steps, step):
        if not self.jobs:
            return

        def unit(index, carry):
            base = 0
            for entry in self.jobs:
                job = entry[0]
                for k in range(job.rights):
                    self.when(index, base + k * job.chunks, job.chunks, functools.partial(self.split, entry, k))
                self.when(
                    index, base + job.prepare, job.units - job.prepare, functools.partial(self.tile, entry)
                )
                base += job.units
            return carry

        lax.fori_loop(step * self.units // steps, (step + 1) * self.units // steps, unit, 0)

    def when(self, index, start, count, act):
        @pl.when((index >= start) & (index < start + count))
        def _():
            act(index - start)

    def split(self, entry, k, chunk):
        job, held, split = entry[0], entry[3], entry[4]
        rows = pl.ds(pl.multiple_of(chunk * job.chunk, job.chunk), job.chunk)
        value = held[job.lefts + k][rows, :]
        where = (slice(None), rows) if job.form == "tn" else (rows, slice(None))
        split[k][0][where], split[k][1][where] = halves(value.T if job.form == "tn" else value)

    def tile(self, entry, index):
        job, _, sink, held, split, outs, _, out_sem = entry
        rows = pl.ds(pl.multiple_of(index * job.tile, job.tile), job.tile)
        numbers = (((1,), (1 if job.form == "nt" else 0,)), ((), ()))
        where = (slice(None), rows) if job.form == "tn" else (rows, slice(None))

        def product(own, other):
            pair = (other, own) if job.form == "tn" else (own, other)
            return lax.dot_general(*pair, numbers, preferred_element_type=jnp.float32)

        total = None
        for k in range(job.lefts):
            high, low = halves(held[k][where])
            for j in [k] if job.summed else range(job.rights):
                right_high, right_low = split[j][0][...], split[j][1][...]
                made = product(high, right_high) + product(high, right_low) + product(low, right_high)
                if job.summed:
                    total = made if total is None else total + made
                else:
                    outs[j][where] = made
        if job.summed:
            outs[0][where] = total
        for j, out in enumerate(outs):
            pltpu.make_async_copy(out.at[where], sink[j].at[where], out_sem.at[j, index]).start()

    def end(self):
        for job, _, sink, _, _, outs, _, out_sem in self.jobs:
            for j, out in enumerate(outs):
                for index in range(job.extent // job.tile):
                    rows = pl.ds(index * job.tile, job.tile)
                    where = (slice(None), rows) if job.form == "tn" else (rows, slice(None))
                    pltpu.make_async_copy(out.at[where], sink[j].at[where], out_sem.at[j, index]).wait()


class Ring:
    def __init__(self, n, cuts, x_ref, o_ref, sems):
        self.n, self.cuts, self.x, self.o = n, cuts, x_ref, o_ref
        self.own_sem, self.send_sem, self.recv_sem = sems
        self.me, self.at = ring_places(n)
        self.sides = ({"heads": self.at(1)}, {"heads": self.at(-1)})
        self.rows = x_ref.shape[0]
        self.piece = self.rows // 2 // cuts
        self.parts = [(cut, way) for cut in range(cuts) for way in (0, 1)]

    def copy(self, step, cut, way, first=False):
        off = way * (self.rows // 2) + cut * self.piece
        origin = self.at(-step) if way == 0 else self.at(step)
        dst = self.o.at[pl.ds(pl.multiple_of(origin * self.rows + off, 8), self.piece)]
        src = self.x.at[pl.ds(off, self.piece)] if first else dst
        sems = self.send_sem.at[way, step, cut], self.recv_sem.at[way, step, cut]
        return remote(src, dst, *sems, self.sides[way])

    def own(self):
        here = self.o.at[pl.ds(pl.multiple_of(self.me * self.rows, 8), self.rows)]
        return pltpu.make_async_copy(self.x, here, self.own_sem)

    def begin(self):
        self.own().start()
        for part in self.parts:
            self.copy(0, *part, first=True).start()

    def step(self, step):
        for part in self.parts:
            self.copy(step - 1, *part).wait_recv()
            self.copy(step, *part).start()

    def received(self):
        for part in self.parts:
            self.copy(self.n - 2, *part).wait_recv()

    def end(self):
        self.received()
        self.sent()

    def sent(self):
        def sent(step, carry):
            for part in self.parts:
                self.copy(step, *part).wait_send()
            return carry

        lax.fori_loop(0, self.n - 1, sent, 0)
        self.own().wait()

    def run(self, work=None):
        def body(step, carry):
            if work is not None:
                work(step - 1)

            @pl.when(step < self.n - 1)
            def _():
                self.step(step)

            return carry

        lax.fori_loop(1, self.n, body, 0)

    @staticmethod
    def scratch(n, cuts):
        return [
            pltpu.SemaphoreType.DMA,
            pltpu.SemaphoreType.DMA((2, n - 1, cuts)),
            pltpu.SemaphoreType.DMA((2, n - 1, cuts)),
        ]


class Spread:
    def __init__(self, dp, x_ref, o_ref, sems, pieces=1):
        self.x, self.o, self.ny, self.pieces = x_ref, o_ref, dp // 2, pieces
        self.own_sem, self.y_send, self.y_recv, self.core_send, self.core_recv = sems
        me = lax.axis_index("dp")
        self.y, self.core = me // 2, me % 2
        self.me = me
        self.mate = {"dp": self.y * 2 + 1 - self.core}
        self.next = {"dp": lax.rem(self.y + 1, self.ny) * 2 + self.core}
        self.rows = x_ref.shape[0]

    def block(self, owner, piece):
        size = self.rows // self.pieces
        return self.o.at[pl.ds(pl.multiple_of(owner * self.rows + piece * size, 8), size)]

    def begin(self):
        mine = self.o.at[pl.ds(pl.multiple_of(self.me * self.rows, 8), self.rows)]
        self.own = pltpu.make_async_copy(self.x, mine, self.own_sem)
        self.own.start()
        self.y_copies, self.core_copies = {}, {}
        for piece in range(self.pieces):
            size = self.rows // self.pieces
            src, dst = self.x.at[pl.ds(piece * size, size)], self.block(self.me, piece)
            self.send(self.y_copies, src, dst, self.y_send, self.y_recv, 0, piece, self.next)
            self.send(self.core_copies, src, dst, self.core_send, self.core_recv, 0, piece, self.mate)

    def send(self, copies, src, dst, send, recv, k, piece, name):
        copies[k, piece] = push(src, dst, send.at[k, piece], recv.at[k, piece], name)

    def end(self):
        for k in range(1, self.ny):
            owner = lax.rem(self.y - k + self.ny, self.ny) * 2 + self.core
            for piece in range(self.pieces):
                self.y_copies[k - 1, piece].wait_recv()
                held = self.block(owner, piece)
                if k < self.ny - 1:
                    self.send(self.y_copies, held, held, self.y_send, self.y_recv, k, piece, self.next)
                self.send(self.core_copies, held, held, self.core_send, self.core_recv, k, piece, self.mate)
        for copy in self.core_copies.values():
            copy.wait_recv()
        for copy in [*self.y_copies.values(), *self.core_copies.values()]:
            copy.wait_send()
        self.own.wait()

    @staticmethod
    def scratch(dp, pieces=1):
        ny = dp // 2
        return [
            pltpu.SemaphoreType.DMA,
            pltpu.SemaphoreType.DMA((ny - 1, pieces)),
            pltpu.SemaphoreType.DMA((ny - 1, pieces)),
            pltpu.SemaphoreType.DMA((ny, pieces)),
            pltpu.SemaphoreType.DMA((ny, pieces)),
        ]


class Swap:
    def __init__(self, dp, out, x_ref, o_ref, sems):
        self.dp, self.out, self.x, self.o = dp, out, x_ref, o_ref
        self.own_sem, self.send_sem, self.recv_sem = sems
        self.me = lax.axis_index("dp")

    def part(self, ref, index, by_columns):
        if by_columns:
            size = ref.shape[1] // self.dp
            return ref.at[:, pl.ds(pl.multiple_of(index * size, size), size)]
        size = ref.shape[0] // self.dp
        return ref.at[pl.ds(pl.multiple_of(index * size, size), size)]

    def begin(self):
        mine = self.part(self.o, self.me, not self.out)
        self.own = pltpu.make_async_copy(self.part(self.x, self.me, self.out), mine, self.own_sem)
        self.own.start()
        self.copies = [
            push(self.part(self.x, other, self.out), mine, self.send_sem.at[k], self.recv_sem.at[k], {"dp": other})
            for k, other in enumerate(others("dp"))
        ]

    def end(self):
        for copy in self.copies:
            copy.wait_recv()
        for copy in self.copies:
            copy.wait_send()
        self.own.wait()

    @staticmethod
    def scratch(dp):
        return [
            pltpu.SemaphoreType.DMA,
            pltpu.SemaphoreType.DMA((dp - 1,)),
            pltpu.SemaphoreType.DMA((dp - 1,)),
        ]


def cost(micros):
    return pl.CostEstimate(flops=0, bytes_accessed=int(micros * 3.0e6), transcendentals=0)


def spaces(count, space=pl.ANY):
    return [pl.BlockSpec(memory_space=space)] * count


class Arrive:
    def __init__(self, ring, rights, refs):
        count = len(rights)
        self.ring, self.sources, self.sinks = ring, rights, refs[:count]
        self.buffer, self.stage = refs[count : count + 2]
        self.split = [refs[count + 2 + 2 * k : count + 4 + 2 * k] for k in range(count)]
        self.made = refs[count + 2 + 2 * count : count + 2 + 3 * count]
        self.load_sem, self.stage_sem, self.out_sem = refs[count + 2 + 3 * count :]

    def load(self, unit):
        height = self.buffer.shape[1]
        source = self.sources[unit // 4].at[pl.ds(unit % 4 * height, height)]
        return pltpu.make_async_copy(source, self.buffer.at[unit % 2], self.load_sem.at[unit % 2])

    def prepare(self):
        units = 4 * len(self.sources)
        for unit in range(units):
            if unit + 1 < units:
                self.load(unit + 1).start()
            self.load(unit).wait()
            height = self.buffer.shape[1]
            high, low = self.split[unit // 4]

            def part(index, carry, unit=unit, high=high, low=low, height=height):
                here = pl.multiple_of(index * 16, 16)
                rows = pl.ds(pl.multiple_of(unit % 4 * height + index * 16, 16), 16)
                high[rows, :], low[rows, :] = halves(self.buffer[unit % 2, pl.ds(here, 16), :])
                return carry

            lax.fori_loop(0, height // 16, part, 0)

    def places(self, index):
        rows = self.ring.rows
        half = rows // 2
        return [
            (pl.ds(pl.multiple_of(self.ring.at(-index) * rows, 8), half), pl.ds(0, half)),
            (pl.ds(pl.multiple_of(self.ring.at(index) * rows + half, 8), half), pl.ds(half, half)),
        ]

    def outgoing(self, index):
        return [
            pltpu.make_async_copy(made.at[index % 2, here], sink.at[there], self.out_sem.at[k, index % 2, way])
            for k, (made, sink) in enumerate(zip(self.made, self.sinks))
            for way, (there, here) in enumerate(self.places(index))
        ]

    def take(self, index, own):
        if own:
            self.stage[...] = self.ring.x[...]
        else:
            copies = [
                pltpu.make_async_copy(self.ring.o.at[there], self.stage.at[here], self.stage_sem.at[way])
                for way, (there, here) in enumerate(self.places(index))
            ]
            for copy in copies:
                copy.start()
            for copy in copies:
                copy.wait()

    def work(self, index):
        def free():
            for copy in self.outgoing(index - 2):
                copy.wait()

        pl.when(index >= 2)(free)
        high, low = halves(self.stage[...])
        for made, split in zip(self.made, self.split):
            made[index % 2] = thrice((high, low), (split[0][...], split[1][...]), NT)
        for copy in self.outgoing(index):
            copy.start()

    def step(self, index):
        @pl.when(index == 0)
        def _():
            self.take(index, True)

        @pl.when(index > 0)
        def _():
            self.take(index, False)

        self.work(index)

    def end(self):
        for index in (self.ring.n - 2, self.ring.n - 1):
            for copy in self.outgoing(index):
                copy.wait()

    @staticmethod
    def outputs(n, x, rights):
        return [jax.ShapeDtypeStruct((n * x.shape[0], right.shape[0]), jnp.float32) for right in rights]

    @staticmethod
    def scratch(n, x, rights):
        if not rights:
            return []
        height, columns = rights[0].shape
        made = [pltpu.VMEM((2, height // 4, columns), jnp.float32), pltpu.VMEM(x.shape, jnp.float32)]
        for right in rights:
            made += [pltpu.VMEM(right.shape, jnp.bfloat16)] * 2
        made += [pltpu.VMEM((2, x.shape[0], right.shape[0]), jnp.float32) for right in rights]
        return made + [
            pltpu.SemaphoreType.DMA((2,)),
            pltpu.SemaphoreType.DMA((2,)),
            pltpu.SemaphoreType.DMA((len(rights), 2, 2)),
        ]


def gather_body(n, cuts, plan, count, x_ref, *refs):
    rights, refs = refs[:count], refs[count:]
    work = Work(plan, refs, 1 + count)
    rest = list(work.rest)
    ring = Ring(n, cuts, x_ref, work.first[0], rest[:3])
    arrive = Arrive(ring, rights, work.first[1:] + rest[3:]) if count else None
    work.load()
    if count:
        arrive.load(0).start()
    greet(ring.sides)
    ring.begin()
    if count:
        arrive.prepare()
    work.ready()

    def share(step):
        if count:
            arrive.step(step)
        work.share(n - 1, step)

    ring.run(share)
    ring.received()
    if count:
        arrive.take(n - 1, False)
        arrive.work(n - 1)
    ring.sent()
    work.end()
    if count:
        arrive.end()


def ring_gather(x, n, number, jobs=(), rights=(), cuts=2):
    rows, columns = x.shape
    cuts = min(cuts, rows // 16)
    plan = [job.bare() for job in jobs]
    rights = list(rights)
    made = [jax.ShapeDtypeStruct((n * rows, columns), x.dtype), *Arrive.outputs(n, x, rights)]
    result = pl.pallas_call(
        functools.partial(gather_body, n, cuts, plan, len(rights)),
        out_shape=(*made, *Work.outputs(jobs)),
        in_specs=spaces(1, pltpu.VMEM) + spaces(len(rights) + len(Work.operands(jobs))),
        out_specs=tuple(spaces(len(made) + len(Work.outputs(jobs)))),
        scratch_shapes=Work.scratch(jobs) + Ring.scratch(n, cuts) + Arrive.scratch(n, x, rights),
        compiler_params=pltpu.CompilerParams(
            collective_id=number,
            has_side_effects=True,
            vmem_limit_bytes=(60 << 20) if jobs or rights else limit(jobs, x.shape),
        ),
        cost_estimate=cost(75.0 * columns / 2048),
        name=f"ring_gather_{number}",
    )(x, *rights, *Work.operands(jobs))
    return result if jobs or rights else result[0]


def opening_body(n, dp, cuts, grad, down, pair, hidden, grad_all, wide_down, wide_pair, hidden_turn, *sems):
    ring = Ring(n, cuts, grad, grad_all, sems[:3])
    parts = [
        Spread(dp, down, wide_down, sems[3:8]),
        Spread(dp, pair, wide_pair, sems[8:13]),
        Swap(dp, True, hidden, hidden_turn, sems[13:16]),
    ]
    greet(list(ring.sides) + [{"dp": other} for other in others("dp")])
    for part in parts:
        part.begin()
    ring.begin()
    ring.run()
    for part in parts:
        part.end()
    ring.end()


def opening(grad, down, pair, hidden, n, dp, number, cuts=2):
    def full(x, times):
        return jax.ShapeDtypeStruct((x.shape[0] * times, x.shape[1]), x.dtype)

    turned = jax.ShapeDtypeStruct((hidden.shape[0] * dp, hidden.shape[1] // dp), hidden.dtype)
    return pl.pallas_call(
        functools.partial(opening_body, n, dp, cuts),
        out_shape=(full(grad, n), full(down, dp), full(pair, dp), turned),
        in_specs=spaces(4, pltpu.VMEM),
        out_specs=tuple(spaces(4)),
        scratch_shapes=Ring.scratch(n, cuts) + Spread.scratch(dp) * 2 + Swap.scratch(dp),
        compiler_params=pltpu.CompilerParams(collective_id=number, has_side_effects=True),
        cost_estimate=cost(80.0),
        name="opening",
    )(grad, down, pair, hidden)


def spread_body(dp, x_ref, o_ref, *sems):
    part = Spread(dp, x_ref, o_ref, sems, 4)
    greet([{"dp": other} for other in others("dp")])
    part.begin()
    part.end()


def dp_gather(x, dp, number):
    return pl.pallas_call(
        functools.partial(spread_body, dp),
        out_shape=jax.ShapeDtypeStruct((x.shape[0] * dp, x.shape[1]), x.dtype),
        in_specs=spaces(1, pltpu.VMEM),
        out_specs=pl.BlockSpec(memory_space=pl.ANY),
        scratch_shapes=Spread.scratch(dp, 4),
        compiler_params=pltpu.CompilerParams(collective_id=number, has_side_effects=True),
        cost_estimate=cost(20.0),
        name=f"dp_gather_{number}",
    )(x)


class RingSum:
    def __init__(self, n, cuts, x_ref, o_ref, held, sems):
        self.n, self.cuts, self.x, self.o, self.held = n, cuts, x_ref, o_ref, held
        self.send_sem, self.recv_sem = sems
        self.me, self.at = ring_places(n)
        self.sides = ({"heads": self.at(1)}, {"heads": self.at(-1)})
        self.rows = x_ref.shape[0] // n
        self.half = self.rows // 2
        self.piece = self.half // cuts
        self.parts = [(cut, way) for cut in range(cuts) for way in (0, 1)]

    def mine(self, owner, cut, way):
        start = owner * self.rows + way * self.half + cut * self.piece
        return self.x.at[pl.ds(pl.multiple_of(start, 8), self.piece)]

    def slot(self, step, cut, way):
        return self.held.at[way, step, pl.ds(cut * self.piece, self.piece)]

    def owner(self, step, way):
        return self.at(-1 - step) if way == 0 else self.at(1 + step)

    def copy(self, step, cut, way, first=False):
        src = self.mine(self.owner(step, way), cut, way) if first else self.slot(step - 1, cut, way)
        sems = self.send_sem.at[way, step, cut], self.recv_sem.at[way, step, cut]
        return remote(src, self.slot(step, cut, way), *sems, self.sides[way])

    def begin(self):
        for part in self.parts:
            self.copy(0, *part, first=True).start()

    def step(self, step):
        for cut, way in self.parts:
            self.arrived(step - 1, cut, way)
            total = self.slot(step - 1, cut, way)
            total[...] += self.mine(self.owner(step, way), cut, way)[...]
            self.copy(step, cut, way).start()

    def arrived(self, step, cut, way):
        slot = self.slot(step, cut, way)
        sems = self.send_sem.at[way, step, cut], self.recv_sem.at[way, step, cut]
        remote(slot, slot, *sems, self.sides[way]).wait_recv()

    def end(self):
        for cut, way in self.parts:
            self.arrived(self.n - 2, cut, way)
            self.o[pl.ds(way * self.half + cut * self.piece, self.piece)] = (
                self.mine(self.me, cut, way)[...] + self.slot(self.n - 2, cut, way)[...]
            )

        def sent(step, carry):
            for cut, way in self.parts:
                slot = self.slot(step, cut, way)
                sems = self.send_sem.at[way, step, cut], self.recv_sem.at[way, step, cut]
                remote(slot, slot, *sems, self.sides[way]).wait_send()
            return carry

        lax.fori_loop(0, self.n - 1, sent, 0)

    run = Ring.run

    @staticmethod
    def scratch(n, cuts, rows, columns):
        return [
            pltpu.VMEM((2, n - 1, rows // 2, columns), jnp.float32),
            pltpu.SemaphoreType.DMA((2, n - 1, cuts)),
            pltpu.SemaphoreType.DMA((2, n - 1, cuts)),
        ]


def scatter_body(n, cuts, plan, x_ref, *refs):
    work = Work(plan, refs, 1)
    ring = RingSum(n, cuts, x_ref, work.first[0], work.rest[0], work.rest[1:])
    work.load()
    greet(ring.sides)
    ring.begin()
    work.ready()
    ring.run(functools.partial(work.share, n - 1))
    ring.end()
    work.end()


def ring_scatter(x, n, number, jobs=(), cuts=4):
    rows, columns = x.shape[0] // n, x.shape[1]
    cuts = min(cuts, rows // 16)
    plan = [job.bare() for job in jobs]
    result = pl.pallas_call(
        functools.partial(scatter_body, n, cuts, plan),
        out_shape=(jax.ShapeDtypeStruct((rows, columns), x.dtype), *Work.outputs(jobs)),
        in_specs=spaces(1, pltpu.VMEM) + spaces(len(Work.operands(jobs))),
        out_specs=tuple(spaces(1, pltpu.VMEM) + spaces(len(Work.outputs(jobs)))),
        scratch_shapes=Work.scratch(jobs) + RingSum.scratch(n, cuts, rows, columns),
        compiler_params=pltpu.CompilerParams(
            collective_id=number, has_side_effects=True, vmem_limit_bytes=limit(jobs, x.shape, x.shape, (rows, columns))
        ),
        cost_estimate=cost(75.0 * columns / 2048),
        name=f"ring_scatter_{number}",
    )(x, *Work.operands(jobs))
    return result if jobs else result[0]


def turn_body(n, dp, cuts, x_ref, hidden, o_ref, hidden_turn, held, *sems):
    ring = RingSum(n, cuts, x_ref, o_ref, held, sems[:2])
    swap = Swap(dp, False, hidden, hidden_turn, sems[2:])
    greet(list(ring.sides) + [{"dp": other} for other in others("dp")])
    swap.begin()
    ring.begin()
    ring.run()
    swap.end()
    ring.end()


def scatter_and_turn(x, hidden, n, dp, number, cuts=4):
    rows, columns = x.shape[0] // n, x.shape[1]
    cuts = min(cuts, rows // 16)
    return pl.pallas_call(
        functools.partial(turn_body, n, dp, cuts),
        out_shape=(
            jax.ShapeDtypeStruct((rows, columns), x.dtype),
            jax.ShapeDtypeStruct((hidden.shape[0] // dp, hidden.shape[1] * dp), x.dtype),
        ),
        in_specs=spaces(2, pltpu.VMEM),
        out_specs=(pl.BlockSpec(memory_space=pltpu.VMEM), pl.BlockSpec(memory_space=pl.ANY)),
        scratch_shapes=RingSum.scratch(n, cuts, rows, columns) + Swap.scratch(dp),
        compiler_params=pltpu.CompilerParams(
            collective_id=number, has_side_effects=True, vmem_limit_bytes=40 << 20
        ),
        cost_estimate=cost(35.0),
        name="scatter_and_turn",
    )(x, hidden)


class Total:
    def __init__(self, axis, x_ref, held, sems):
        self.x, self.held = x_ref, held
        self.send_sem, self.recv_sem = sems
        self.names = [{axis: other} for other in others(axis)]
        self.count = lax.axis_size(axis)

    def begin(self):
        self.copies = [
            push(self.x, self.held.at[k], self.send_sem.at[k], self.recv_sem.at[k], name)
            for k, name in enumerate(self.names)
        ]

    def end(self):
        for copy in self.copies:
            copy.wait_recv()
        for copy in self.copies:
            copy.wait_send()

    @staticmethod
    def scratch(count, shape):
        return [
            pltpu.VMEM((count - 1,) + shape, jnp.float32),
            pltpu.SemaphoreType.DMA((count - 1,)),
            pltpu.SemaphoreType.DMA((count - 1,)),
        ]


def in_order(axis, own, held):
    count = lax.axis_size(axis)
    me = lax.axis_index(axis)
    total = None
    for device in range(count):
        term = jnp.where(me == device, own, jnp.zeros_like(own))
        for k in range(1, count):
            term = term + jnp.where(lax.rem(me - k + count, count) == device, held[k - 1], jnp.zeros_like(own))
        total = term if total is None else total + term
    return total


def sum_body(x_ref, o_ref, middle, held_heads, hs, hr, held_dp, ds, dr):
    first = Total("heads", x_ref, held_heads, (hs, hr))
    second = Total("dp", middle, held_dp, (ds, dr))
    greet(first.names + second.names)
    first.begin()
    first.end()
    middle[...] = in_order("heads", x_ref[...], held_heads)
    second.begin()
    second.end()
    o_ref[...] = in_order("dp", middle[...], held_dp)


def gather_and_sum_body(n, cuts, x_ref, gains, o_ref, total, *refs):
    ring = Ring(n, cuts, x_ref, o_ref, refs[:3])
    middle, held_heads, hs, hr, held_dp, ds, dr = refs[3:]
    first = Total("heads", gains, held_heads, (hs, hr))
    second = Total("dp", middle, held_dp, (ds, dr))
    greet(first.names + second.names)
    first.begin()
    ring.begin()
    first.end()
    middle[...] = in_order("heads", gains[...], held_heads)
    second.begin()
    ring.run()
    second.end()
    total[...] = in_order("dp", middle[...], held_dp)
    ring.end()


def gather_and_sum(x, gains, n, dp, number, cuts=2):
    rows, columns = x.shape
    cuts = min(cuts, rows // 16)
    return pl.pallas_call(
        functools.partial(gather_and_sum_body, n, cuts),
        out_shape=(
            jax.ShapeDtypeStruct((n * rows, columns), x.dtype),
            jax.ShapeDtypeStruct(gains.shape, gains.dtype),
        ),
        in_specs=spaces(2, pltpu.VMEM),
        out_specs=(pl.BlockSpec(memory_space=pl.ANY), pl.BlockSpec(memory_space=pltpu.VMEM)),
        scratch_shapes=Ring.scratch(n, cuts)
        + [pltpu.VMEM(gains.shape, gains.dtype)]
        + Total.scratch(n, gains.shape)
        + Total.scratch(dp, gains.shape),
        compiler_params=pltpu.CompilerParams(
            collective_id=number, has_side_effects=True, vmem_limit_bytes=16 << 20
        ),
        cost_estimate=cost(35.0),
        name="gather_and_sum",
    )(x, gains)


def sum_all(x, n, dp, number):
    return pl.pallas_call(
        sum_body,
        out_shape=jax.ShapeDtypeStruct(x.shape, x.dtype),
        in_specs=spaces(1, pltpu.VMEM),
        out_specs=pl.BlockSpec(memory_space=pltpu.VMEM),
        scratch_shapes=[pltpu.VMEM(x.shape, x.dtype)] + Total.scratch(n, x.shape) + Total.scratch(dp, x.shape),
        compiler_params=pltpu.CompilerParams(collective_id=number, has_side_effects=True),
        cost_estimate=cost(8.0),
        name=f"sum_all_{number}",
    )(x)


NT = (((1,), (1,)), ((), ()))
NN = (((1,), (0,)), ((), ()))


def thrice(left, right, numbers):
    terms = [(left[0], right[0]), (left[0], right[1]), (left[1], right[0])]
    made = [lax.dot_general(*term, numbers, preferred_element_type=jnp.float32) for term in terms]
    return made[0] + (made[1] + made[2])


def turned(front, back, cosine, sines):
    return front * cosine - back * sines, back * cosine + front * sines


def keep_halves(value, pair, where):
    pair[0][where], pair[1][where] = halves(value)


def allowed_block(start, rows, reach, seg_rows, seg_columns):
    row = start + lax.broadcasted_iota(jnp.int32, (rows, reach), 0)
    column = lax.broadcasted_iota(jnp.int32, (rows, reach), 1)
    return (seg_rows[start : start + rows, :] == seg_columns[:, :reach]) & (column <= row)


def attend_body(latent_dim, rows, raw, packed, cosine, sines, seg_rows, seg_columns, mixed, query, lse, *split):
    total, width = raw.shape
    dim = (packed.shape[1] - latent_dim) // 2
    half = dim // 2
    scale = dim ** (-0.5)
    key, value = split[:2], split[2:]
    keep_halves(packed[:, latent_dim : latent_dim + dim], key, (slice(None), slice(None)))
    keep_halves(packed[:, latent_dim + dim :], value, (slice(None), slice(None)))
    for start in range(0, total, rows):
        here = slice(start, start + rows)
        reach = start + rows
        allowed = allowed_block(start, rows, reach, seg_rows, seg_columns)
        for head in range(width // dim):
            at = head * dim
            front, back = turned(
                raw[here, at : at + half], raw[here, at + half : at + dim], cosine[here, :], sines[here, :]
            )
            query[here, at : at + half] = front
            query[here, at + half : at + dim] = back
            own = halves(query[here, at : at + dim])
            scores = thrice(own, [ref[:reach, :] for ref in key], NT) * scale
            scores = jnp.where(allowed, scores, -1e30)
            top = jnp.max(scores, axis=1, keepdims=True)
            expo = jnp.exp(scores - top)
            denom = jnp.sum(expo, axis=1, keepdims=True)
            made = thrice(halves(expo), [ref[:reach, :] for ref in value], NN)
            mixed[here, at : at + dim] = made / denom
            lse[here, head * 128 : head * 128 + 128] = jnp.broadcast_to(top + jnp.log(denom), (rows, 128))


def attend(raw, packed, cosine, sines, seg_rows, seg_columns, latent_dim):
    total, width = raw.shape
    dim = (packed.shape[1] - latent_dim) // 2
    shape = jax.ShapeDtypeStruct
    return pl.pallas_call(
        functools.partial(attend_body, latent_dim, 256),
        out_shape=(
            shape(raw.shape, jnp.float32),
            shape(raw.shape, jnp.float32),
            shape((total, width // dim * 128), jnp.float32),
        ),
        in_specs=spaces(6, pltpu.VMEM),
        out_specs=tuple(spaces(3, pltpu.VMEM)),
        scratch_shapes=[pltpu.VMEM((total, dim), jnp.bfloat16)] * 4,
        compiler_params=pltpu.CompilerParams(vmem_limit_bytes=ATTEND_LIMIT),
        cost_estimate=cost(14.0),
        name="attend",
    )(raw, packed, cosine, sines, seg_rows, seg_columns)


def attend_back_body(
    latent_dim, rows, query, packed, cosine, sines, seg_rows, seg_columns, lse, mixed, d_mixed, up, d_raw, out, *split
):
    total, width = query.shape
    dim = (packed.shape[1] - latent_dim) // 2
    half = dim // 2
    scale = dim ** (-0.5)
    key, value, weight, made = split[:2], split[2:4], split[4:6], split[6:]
    every = (slice(None), slice(None))
    keep_halves(packed[:, latent_dim : latent_dim + dim], key, every)
    keep_halves(packed[:, latent_dim + dim :], value, every)
    keep_halves(up[...], weight, every)
    out[:, latent_dim:] = jnp.zeros((total, 2 * dim), jnp.float32)
    for start in range(0, total, rows):
        here = slice(start, start + rows)
        reach = start + rows
        allowed = allowed_block(start, rows, reach, seg_rows, seg_columns)
        for head in range(width // dim):
            at = head * dim
            own = halves(query[here, at : at + dim])
            upstream = d_mixed[here, at : at + dim]
            grad = halves(upstream)
            scores = thrice(own, [ref[:reach, :] for ref in key], NT) * scale
            scores = jnp.where(allowed, scores, -1e30)
            probs = jnp.exp(scores - lse[here, head * 128 : head * 128 + 1])
            d_probs = thrice(grad, [ref[:reach, :] for ref in value], NT)
            delta = jnp.sum(upstream * mixed[here, at : at + dim], axis=1, keepdims=True)
            d_scores = probs * (d_probs - delta) * scale
            out[:reach, latent_dim + dim :] += thrice(halves(probs.T), grad, NN)
            out[:reach, latent_dim : latent_dim + dim] += thrice(halves(d_scores.T), own, NN)
            d_query = thrice(halves(d_scores), [ref[:reach, :] for ref in key], NN)
            front, back = turned(d_query[:, :half], d_query[:, half:], cosine[here, :], -sines[here, :])
            for piece, off in ((front, at), (back, at + half)):
                d_raw[here, off : off + half] = piece
                keep_halves(piece, made, (slice(None), slice(off, off + half)))
        out[here, :latent_dim] = thrice([ref[...] for ref in made], [ref[...] for ref in weight], NT)


def attend_back(query, packed, cosine, sines, seg_rows, seg_columns, lse, mixed, d_mixed, up, latent_dim):
    total, width = query.shape
    dim = (packed.shape[1] - latent_dim) // 2
    shape = jax.ShapeDtypeStruct
    rows = 256
    return pl.pallas_call(
        functools.partial(attend_back_body, latent_dim, rows),
        out_shape=(shape(query.shape, jnp.float32), shape(packed.shape, jnp.float32)),
        in_specs=spaces(10, pltpu.VMEM),
        out_specs=tuple(spaces(2, pltpu.VMEM)),
        scratch_shapes=[pltpu.VMEM((total, dim), jnp.bfloat16)] * 4
        + [pltpu.VMEM(up.shape, jnp.bfloat16)] * 2
        + [pltpu.VMEM((rows, width), jnp.bfloat16)] * 2,
        compiler_params=pltpu.CompilerParams(vmem_limit_bytes=ATTEND_LIMIT),
        cost_estimate=cost(30.0),
        name="attend_back",
    )(query, packed, cosine, sines, seg_rows, seg_columns, lse, mixed, d_mixed, up)


def rope_tables(position, head_dim):
    half_dim = head_dim // 2
    frequency = ROPE_BASE ** (-jnp.arange(half_dim, dtype=jnp.float32) / half_dim)
    angles = position.astype(jnp.float32)[:, None] * frequency[None, :]
    return jnp.cos(angles), jnp.sin(angles)


ATTEND_LIMIT = 58 << 20


def matmul_high(left, right):
    return jnp.dot(left, right, precision=HIGH, preferred_element_type=jnp.float32)


def layout(lengths_row, row_index):
    upto = jnp.arange(lengths_row.shape[0], dtype=jnp.int32)
    doc_ends = jnp.sum(jnp.where(upto[None, :] <= upto[:, None], lengths_row[None, :], 0), axis=1)
    doc_starts = doc_ends - lengths_row
    segment = jnp.sum((row_index[:, None] >= doc_ends[None, :]).astype(jnp.int32), axis=1)
    doc_ids = jnp.arange(doc_ends.shape[0], dtype=jnp.int32)
    start_of = jnp.sum(
        jnp.where(segment[:, None] == doc_ids[None, :], doc_starts[None, :], 0), axis=1
    )
    return (segment, row_index - start_of)


def rotate(vector, position, sign):
    half_dim = vector.shape[-1] // 2
    frequency = ROPE_BASE ** (-jnp.arange(half_dim, dtype=jnp.float32) / half_dim)
    angles = position.astype(jnp.float32)[:, None] * frequency[None, :]
    angles = angles.reshape((angles.shape[0],) + (1,) * (vector.ndim - 2) + (half_dim,))
    cosine = jnp.cos(angles)
    sines = sign * jnp.sin(angles)
    front = vector[..., :half_dim]
    back_half = vector[..., half_dim:]
    return jnp.concatenate(
        [front * cosine - back_half * sines, back_half * cosine + front * sines], axis=-1
    )


def norm_back(upstream, normed, inverse, gain):
    scaled = upstream * gain
    return (
        inverse * (scaled - normed * jnp.mean(scaled * normed, axis=1, keepdims=True)),
        jnp.sum(upstream * normed, axis=0),
    )


def owned(part, axis):
    return lax.psum_scatter(part, "dp", scatter_dimension=axis, tiled=True)


def moments(value, grad, first, second):
    first_new = BETA_ONE * first + (1.0 - BETA_ONE) * grad
    second_new = BETA_TWO * second + (1.0 - BETA_TWO) * grad * grad
    update = (
        first_new
        * (1.0 / (1.0 - BETA_ONE**STEP_COUNT))
        / (jnp.sqrt(second_new * (1.0 / (1.0 - BETA_TWO**STEP_COUNT))) + ADAM_EPS)
        + DECAY * value
    )
    return (first_new, second_new, update)


def chunk_of(rows):
    return next(c for c in (64, 32, 16, 8) if rows % c == 0)


def lamb_limit(times, values, grads):
    sizes = [times * padded(x.shape, 4) for x in values] + [padded(x.shape, 4) for x in grads]
    return (4 << 20) + sum(sizes)


def moments_body(slots, shares, offsets, count_grads, *refs):
    count = len(slots)
    values, firsts, seconds = refs[:count], refs[count : 2 * count], refs[2 * count : 3 * count]
    grads = refs[3 * count : 3 * count + count_grads]
    outs = refs[3 * count + count_grads : -1]
    table = refs[-1]
    row = lax.broadcasted_iota(jnp.int32, table.shape, 0)
    lane = lax.broadcasted_iota(jnp.int32, table.shape, 1)
    sums = jnp.zeros(table.shape, jnp.float32)
    for k, slot in enumerate(slots):
        height, width = values[k].shape
        chunk = chunk_of(height)
        which, offset, below = offsets[k]

        def part(index, carry, k=k, chunk=chunk, width=width, which=which, offset=offset, below=below):
            rows = pl.ds(pl.multiple_of(index * chunk, chunk), chunk)
            under = pl.ds(pl.multiple_of(below + index * chunk, 8), chunk)
            value = values[k][rows, :]
            first, second, update = moments(
                value, grads[which][under, offset : offset + width], firsts[k][rows, :], seconds[k][rows, :]
            )
            for out, made in zip(outs[3 * k : 3 * k + 3], (first, second, update)):
                out[rows, :] = made

            def folded(x):
                return jnp.sum((x * x).reshape(chunk // 8, 8, width), axis=0)

            return carry[0] + folded(value), carry[1] + folded(update)

        zero = jnp.zeros((8, width), jnp.float32)
        for at, square in enumerate(lax.fori_loop(0, height // chunk, part, (zero, zero))):
            total = jnp.sum(jnp.sum(square, axis=1, keepdims=True), axis=0, keepdims=True) * shares[k]
            sums += jnp.where((row == slot) & (lane == at), total, 0.0)
    table[...] = sums


def all_moments(slots, shares, offsets, values, firsts, seconds, grads):
    shape = jax.ShapeDtypeStruct
    made = pl.pallas_call(
        functools.partial(moments_body, slots, shares, offsets, len(grads)),
        out_shape=(
            *[shape(value.shape, jnp.float32) for value in values for _ in range(3)],
            shape((8, 128), jnp.float32),
        ),
        in_specs=spaces(3 * len(values) + len(grads), pltpu.VMEM),
        out_specs=tuple(spaces(3 * len(values) + 1, pltpu.VMEM)),
        compiler_params=pltpu.CompilerParams(vmem_limit_bytes=lamb_limit(6, values, grads)),
        cost_estimate=cost(12.0),
        name=f"moments_{slots[0]}",
    )(*values, *firsts, *seconds, *grads)
    return [made[3 * k : 3 * k + 3] for k in range(len(values))], made[-1]


def finish_body(count, table, *refs):
    values, updates, outs, norms = refs[:count], refs[count : 2 * count], refs[2 * count : -1], refs[-1]
    norms[...] = jnp.sqrt(table[...])
    for k in range(count):
        ratio = RATE * (norms[k : k + 1, 0:1] / norms[k : k + 1, 1:2])
        height = values[k].shape[0]
        chunk = chunk_of(height)

        def part(index, carry, k=k, chunk=chunk, ratio=ratio):
            rows = pl.ds(pl.multiple_of(index * chunk, chunk), chunk)
            outs[k][rows, :] = values[k][rows, :] - ratio * updates[k][rows, :]
            return carry

        lax.fori_loop(0, height // chunk, part, 0)


def finish(table, values, updates):
    shape = jax.ShapeDtypeStruct
    made = pl.pallas_call(
        functools.partial(finish_body, len(values)),
        out_shape=(*[shape(value.shape, jnp.float32) for value in values], shape(table.shape, jnp.float32)),
        in_specs=spaces(2 * len(values) + 1, pltpu.VMEM),
        out_specs=tuple(spaces(len(values) + 1, pltpu.VMEM)),
        compiler_params=pltpu.CompilerParams(vmem_limit_bytes=lamb_limit(3, values, ())),
        cost_estimate=cost(9.0),
        name="finish",
    )(table, *values, *updates)
    return made[:-1], made[-1]


def on_device(
    block_input,
    output_grad,
    lengths,
    norm_gains,
    norm_gains_first,
    norm_gains_second,
    query_down,
    query_down_first,
    query_down_second,
    key_value,
    key_value_first,
    key_value_second,
    query_up,
    query_up_first,
    query_up_second,
    head_merge,
    head_merge_first,
    head_merge_second,
    gate_weight,
    gate_weight_first,
    gate_weight_second,
    up_weight,
    up_weight_first,
    up_weight_second,
    down_weight,
    down_weight_first,
    down_weight_second,
):
    tok_rows = block_input.shape[0]
    model_dim = block_input.shape[1]
    latent_dim = query_down.shape[1]
    head_dim = key_value.shape[1] // 2
    heads_count = lax.axis_size("heads")
    dp_count = lax.axis_size("dp")
    group_rows = tok_rows * heads_count
    group_index = jnp.arange(group_rows, dtype=jnp.int32)
    segment, position = layout(lengths[0], group_index)
    local_position = lax.dynamic_slice_in_dim(
        position, lax.axis_index("heads") * tok_rows, tok_rows
    )
    gain_attn = norm_gains[:model_dim]
    gain_query = norm_gains[model_dim : model_dim + latent_dim]
    gain_ffn = norm_gains[model_dim + latent_dim :]
    inv_one = lax.rsqrt(jnp.mean(block_input * block_input, axis=1, keepdims=True) + EPS_NORM)
    normed_one = block_input * inv_one
    hidden_one = normed_one * gain_attn
    grad_all, wide_down, wide_pair, hidden_turn = opening(
        output_grad, query_down, key_value, hidden_one, heads_count, dp_count, 5
    )
    query_up_in, head_merge_in, gate_in, upper_in, lower_in, grad_all = lax.optimization_barrier(
        (query_up, head_merge, gate_weight, up_weight, down_weight, grad_all)
    )
    wide_up = lax.all_gather(query_up_in, "dp", axis=0, tiled=True)
    wide_merge = lax.all_gather(head_merge_in, "dp", axis=1, tiled=True)
    latent_raw = matmul_high(hidden_one, wide_down)
    inv_query = lax.rsqrt(jnp.mean(latent_raw * latent_raw, axis=1, keepdims=True) + EPS_NORM)
    latent_hat = latent_raw * inv_query
    latent = latent_hat * gain_query
    pair_local = matmul_high(hidden_one, wide_pair)
    key_local = rotate(pair_local[:, :head_dim], local_position, 1.0)
    value_local = pair_local[:, head_dim:]
    packed = jnp.concatenate([latent, key_local, value_local], axis=1)
    lower_in, packed = lax.optimization_barrier((lower_in, packed))
    wide_lower = lax.all_gather(lower_in, "dp", axis=1, tiled=True)
    packed_all = ring_gather(packed, heads_count, 1)
    gate_in, upper_in, packed_all = lax.optimization_barrier((gate_in, upper_in, packed_all))
    turned_gate = lax.all_gather(gate_in.T, "dp", axis=1, tiled=True)
    turned_upper = lax.all_gather(upper_in.T, "dp", axis=1, tiled=True)
    latent_all = packed_all[:, :latent_dim]
    cosine, sines = rope_tables(position, head_dim)
    seg_rows, seg_columns = segment[:, None], segment[None, :]
    mixed_heads, query_rot, lse = attend(
        matmul_high(latent_all, wide_up), packed_all, cosine, sines, seg_rows, seg_columns, latent_dim
    )
    inside = group_rows <= 1024

    def job(*what):
        return [Job(*what)] if inside else []

    part_middle = matmul_high(mixed_heads, wide_merge)
    if inside:
        part_middle, d_activ = ring_scatter(
            part_middle, heads_count, 2, job("nt", [grad_all], [wide_lower], 256)
        )
    else:
        part_middle = ring_scatter(part_middle, heads_count, 2)
        d_activ = matmul_high(grad_all, wide_lower.T)
    middle = block_input + part_middle
    inv_two = lax.rsqrt(jnp.mean(middle * middle, axis=1, keepdims=True) + EPS_NORM)
    normed_two = middle * inv_two
    hidden_two = normed_two * gain_ffn
    if inside:
        hidden_all, gate_pre, up_pre = ring_gather(
            hidden_two, heads_count, 3, rights=[turned_gate, turned_upper]
        )
    else:
        hidden_all = ring_gather(hidden_two, heads_count, 3)
        gate_pre = matmul_high(hidden_all, turned_gate.T)
        up_pre = matmul_high(hidden_all, turned_upper.T)
    sig_gate = jax.nn.sigmoid(gate_pre)
    silu_gate = gate_pre * sig_gate
    activ = silu_gate * up_pre
    d_gate_pre = d_activ * up_pre * (sig_gate * (1.0 + gate_pre * (1.0 - sig_gate)))
    d_up_pre = d_activ * silu_gate
    part_output = matmul_high(activ, wide_lower)
    if inside:
        part_output, part_two = ring_scatter(
            part_output,
            heads_count,
            4,
            job("nn", [d_gate_pre, d_up_pre], [turned_gate, turned_upper], 128),
        )
        d_hidden_two, grad_both = ring_scatter(
            part_two,
            heads_count,
            6,
            job("tn", [hidden_all], [d_gate_pre], 256, True) + job("tn", [grad_all], [activ], 256, True),
        )
    else:
        part_output = ring_scatter(part_output, heads_count, 4)
        part_two = matmul_high(d_gate_pre, turned_gate) + matmul_high(d_up_pre, turned_upper)
        d_hidden_two = ring_scatter(part_two, heads_count, 6)
        grad_both = jnp.concatenate(
            [matmul_high(d_gate_pre.T, hidden_all), matmul_high(activ.T, grad_all)], axis=0
        )
    block_output = middle + part_output
    grad_both = owned(grad_both, 1)
    d_normed_mid, grad_gain_ffn = norm_back(d_hidden_two, normed_two, inv_two, gain_ffn)
    d_middle = output_grad + d_normed_mid
    if inside:
        middle_all, d_mixed, grad_upper = ring_gather(
            d_middle, heads_count, 7, job("tn", [hidden_all], [d_up_pre], 256), [wide_merge]
        )
    else:
        middle_all = ring_gather(d_middle, heads_count, 7)
        d_mixed = matmul_high(middle_all, wide_merge.T)
        grad_upper = matmul_high(d_up_pre.T, hidden_all)
    d_query_pre, packed_part = attend_back(
        query_rot,
        packed_all,
        cosine,
        sines,
        seg_rows,
        seg_columns,
        lse,
        mixed_heads,
        d_mixed,
        wide_up,
        latent_dim,
    )
    packed_part, grad_both, grad_upper = lax.optimization_barrier((packed_part, grad_both, grad_upper))
    grad_upper = owned(grad_upper, 1)
    if inside:
        packed_grad, grad_merge, grad_up = ring_scatter(
            packed_part,
            heads_count,
            8,
            job("tn", [middle_all], [mixed_heads], 256) + job("tn", [d_query_pre], [(packed_all, jax.ShapeDtypeStruct(latent_all.shape, jnp.float32))], 256),
        )
    else:
        packed_grad = ring_scatter(packed_part, heads_count, 8)
        grad_merge = matmul_high(mixed_heads.T, middle_all)
        grad_up = matmul_high(latent_all.T, d_query_pre)
    packed_grad, grad_upper = lax.optimization_barrier((packed_grad, grad_upper))
    d_latent = packed_grad[:, :latent_dim]
    d_key_local = packed_grad[:, latent_dim : latent_dim + head_dim]
    d_value_local = packed_grad[:, latent_dim + head_dim :]
    d_pair = jnp.concatenate([rotate(d_key_local, local_position, -1.0), d_value_local], axis=1)
    d_latent_raw, grad_gain_query = norm_back(d_latent, latent_hat, inv_query, gain_query)
    raw = jnp.concatenate([d_latent_raw, d_pair], axis=1)
    raw_all = dp_gather(raw, dp_count, 11)
    raw_all, grad_merge, grad_up = lax.optimization_barrier((raw_all, grad_merge, grad_up))
    grad_up = owned(grad_up, 0)
    part_shared = matmul_high(hidden_turn.T, raw_all)
    d_hidden_turn = matmul_high(raw_all, jnp.concatenate([query_down, key_value], axis=1).T)
    shared_cut, d_hidden_one = scatter_and_turn(part_shared, d_hidden_turn, heads_count, dp_count, 9)
    d_normed_in, grad_gain_attn = norm_back(d_hidden_one, normed_one, inv_one, gain_attn)
    input_grad = d_middle + d_normed_in
    grad_gains = jnp.concatenate([grad_gain_attn, grad_gain_query, grad_gain_ffn])
    shared_cut, grad_merge, grad_up = lax.optimization_barrier((shared_cut, grad_merge, grad_up))
    grad_merge = owned(grad_merge, 1)
    shared, gains_total = gather_and_sum(
        shared_cut, grad_gains.reshape(-1, 128), heads_count, dp_count, 10
    )
    gains_total = gains_total.reshape(-1)
    def flat(gains):
        return gains.reshape(-1, 128)

    everyone = 1.0 / (heads_count * dp_count)
    early, early_sums = all_moments(
        (5, 6, 7),
        (1.0, 1.0, 1.0),
        ((0, 0, 0), (1, 0, 0), (0, 0, down_weight.shape[0])),
        (gate_weight.T, up_weight.T, down_weight),
        (gate_weight_first.T, up_weight_first.T, down_weight_first),
        (gate_weight_second.T, up_weight_second.T, down_weight_second),
        (grad_both, grad_upper),
    )
    late, late_sums = all_moments(
        (0, 1, 2, 3, 4),
        (everyone, 1.0 / heads_count, 1.0 / heads_count, 1.0, 1.0),
        ((0, 0, 0), (1, 0, 0), (1, latent_dim, 0), (2, 0, 0), (3, 0, 0)),
        (flat(norm_gains), query_down, key_value, query_up, head_merge),
        (flat(norm_gains_first), query_down_first, key_value_first, query_up_first, head_merge_first),
        (flat(norm_gains_second), query_down_second, key_value_second, query_up_second, head_merge_second),
        (flat(gains_total), shared, grad_up, grad_merge),
    )
    stepped = late + early
    table = sum_all(early_sums + late_sums, heads_count, dp_count, 13)
    new_values, norms = finish(
        table,
        (
            flat(norm_gains),
            query_down,
            key_value,
            query_up,
            head_merge,
            gate_weight.T,
            up_weight.T,
            down_weight,
        ),
        [entry[2] for entry in stepped],
    )
    results = []
    for slot in range(8):
        entry = (stepped[slot][0], stepped[slot][1], new_values[slot])
        if slot == 0:
            entry = tuple(x.reshape(-1) for x in entry)
        if slot in (5, 6):
            entry = tuple(x.T for x in entry)
        results.extend(entry)
    return (block_output, input_grad, *results, norms[:, :2])


def solution(mesh):
    placed = (
        P(("dp", "heads"), None),
        P(("dp", "heads"), None),
        P("dp", None),
        P(),
        P(),
        P(),
        P("dp", None),
        P("dp", None),
        P("dp", None),
        P("dp", None),
        P("dp", None),
        P("dp", None),
        P("dp", "heads"),
        P("dp", "heads"),
        P("dp", "heads"),
        P("heads", "dp"),
        P("heads", "dp"),
        P("heads", "dp"),
        P("dp", "heads"),
        P("dp", "heads"),
        P("dp", "heads"),
        P("dp", "heads"),
        P("dp", "heads"),
        P("dp", "heads"),
        P("heads", "dp"),
        P("heads", "dp"),
        P("heads", "dp"),
    )
    return jax.shard_map(
        on_device,
        mesh=mesh,
        in_specs=placed,
        out_specs=(
            P(("dp", "heads"), None),
            P(("dp", "heads"), None),
            P(),
            P(),
            P(),
            P("dp", None),
            P("dp", None),
            P("dp", None),
            P("dp", None),
            P("dp", None),
            P("dp", None),
            P("dp", "heads"),
            P("dp", "heads"),
            P("dp", "heads"),
            P("heads", "dp"),
            P("heads", "dp"),
            P("heads", "dp"),
            P("dp", "heads"),
            P("dp", "heads"),
            P("dp", "heads"),
            P("dp", "heads"),
            P("dp", "heads"),
            P("dp", "heads"),
            P("heads", "dp"),
            P("heads", "dp"),
            P("heads", "dp"),
            P(),
        ),
        check_vma=False,
    )
```
